32 devices in a mesh: dp: 16 (over z, y, x), tp: 2 (over core).
Axes of the slice: x: 2, y: 2, z: 4, core: 2. Of those that a mesh axis runs over, the one named last changes fastest.
Arguments:
- tokens: bfloat16 [32768, 768], P('dp', 'tp'), may hold values from -6 to 6
- lengths: int32 [16, 8], P('dp'), may hold values from 1 to 512, 2048 in all within a row
- query_weight: bfloat16 [768, 768], P(None, 'tp'), may hold values from -0.21875 to 0.21875
- w_key: bfloat16 [768, 768], P(None, 'tp'), may hold values from -0.21875 to 0.21875
- value_weight: bfloat16 [768, 768], P(None, 'tp'), may hold values from -0.21875 to 0.21875
- w_out: bfloat16 [768, 768], P('tp'), may hold values from -0.875 to 0.875
- w_up: bfloat16 [768, 3072], P(None, 'tp'), may hold values from -0.21875 to 0.21875
- w_down: bfloat16 [3072, 768], P('tp'), may hold values from -0.109375 to 0.109375
- gain_attn: float32 [768], replicated, may hold values from 0.5 to 1.5
- shift_attn: float32 [768], replicated, may hold values from -0.6 to 0.6
- gain_ffn: float32 [768], replicated, may hold values from 0.5 to 1.5
- shift_ffn: float32 [768], replicated, may hold values from -0.6 to 0.6
- factors: float32 [24576], replicated, may hold values from -1 to 1
- first_moment: float32 [24576], P(('dp', 'tp')), may hold values from -0.6 to 0.6
- second_moment: float32 [24576], P(('dp', 'tp')), may hold values from 0.0001 to 0.01
- cotangent: bfloat16 [32768, 768], P('dp', 'tp'), may hold values from -6 to 6
Outputs:
- encoded: bfloat16 [32768, 768], P('dp', 'tp')
- d_tokens: float32 [32768, 768], P('dp', 'tp')
- gradients: float32 [24576], P(('dp', 'tp'))
- first_new: float32 [24576], P(('dp', 'tp'))
- second_new: float32 [24576], P(('dp', 'tp'))
- factors_new: float32 [24576], replicated
The draws below stay inside these ranges and needn't reach their ends.
Inputs may be any that keep to these rules, and one draw needn't show every extreme that they name: The 8 lengths of each row add up to 2048; the largest of each row is 512.
All inputs are finite; a program needn't handle non-finite values.
Results may differ from the reference program's by a relative error of at most 0.018.
Values may be sent and summed in bfloat16 or wider, within the bound.
No kernel may reach another device: no remote copies, remote signals or barrier semaphores. Data moves between devices by JAX's collectives and lax.ppermute only.
A program may use at most 384 MiB of HBM per device.

```python
import math
import jax
import jax.numpy as jnp
import numpy as np
from jax import lax

D = 768
HEADS = 12
HEAD = 64
FF = 3072
ADAPTER_RANK = 8
SENTS = 8
TOK_DEV = 2048
LONGEST = 512
TOKENS = 32768
PARAMS = 24576
N_DP = 16


def draw_factors(key, part):
    key = jax.random.fold_in(key, 11)
    first_key, second_key = jax.random.split(key)
    size_half = 2 * D * ADAPTER_RANK
    down_part = jax.random.normal(first_key, (size_half,), jnp.float32) * D ** (-0.5)
    up_part = jax.random.normal(second_key, (size_half,), jnp.float32) * 0.1
    return jnp.clip(jnp.concatenate([down_part, up_part]), -1.0, 1.0)


def level_of(own_key, dims, cuts, smallest, top_value):
    def one(axis_at, shards_of):
        steps = jax.random.uniform(jax.random.fold_in(jax.random.fold_in(own_key, 6), axis_at), (shards_of,), jnp.float32, smallest / len(cuts), top_value / len(cuts))
        return jnp.repeat(jnp.exp(steps), dims[axis_at] // shards_of).reshape((-1,) + (1,) * (len(dims) - axis_at - 1))

    loudness = one(*cuts[0])
    for cut in cuts[1:]:
        loudness = loudness * one(*cut)
    return loudness


def split_up(amount, total, reach, skew):
    weights = [(1 << 20) // math.isqrt(rank ** skew) + 1 for rank in range(2, amount + 1)]
    spare, given = total - reach - (amount - 1), [1] * (amount - 1)
    while spare > 0:
        movable = [i for i in range(amount - 1) if given[i] < reach]
        pool, remaining = sum([weights[i] for i in movable]), spare
        for i in movable:
            addition = min(reach - given[i], max(1, remaining * weights[i] // pool), spare)
            given[i] = given[i] + addition
            spare = spare - addition
    return np.array([reach] + given)


def uneven(key, count, total, limit, slope):
    if count == 2:
        one = jax.random.randint(key, (), max(1, total - limit), min(limit, total - 1) + 1)
        return jnp.stack([one, total - one])
    sizes = jnp.asarray(split_up(count, total, limit, slope), jnp.int32)
    couples = (count - 1) // 2
    donor, receiver = sizes[1:1 + 2 * couples:2], sizes[2:2 + 2 * couples:2]
    margin = jnp.minimum(donor - 1, limit - receiver)
    shifted = jax.random.randint(jax.random.fold_in(key, 1), (couples,), 0, 1 << 20) % (margin + 1)
    sizes = sizes.at[1:1 + 2 * couples:2].set(donor - shifted).at[2:2 + 2 * couples:2].set(receiver + shifted)
    return sizes[jax.random.permutation(jax.random.fold_in(key, 2), count)]


def gaussian(rng, extent, width, limit, cuts=(), kind=jnp.bfloat16):
    gain = level_of(rng, extent, cuts, -0.22, 0.18) if cuts else 1.0
    array = jax.random.normal(rng, extent, jnp.float32) * width * gain
    return jnp.minimum(jnp.maximum(array, -limit), limit).astype(kind)


def setup_inputs(seed: int = 0) -> dict:
    arg_keys = jax.random.split(jax.random.key(seed), 17)
    tokens = gaussian(arg_keys[0], (TOKENS, D), 1.0, 6.0, ((0, 16), (1, 2)))
    lengths = jax.vmap(lambda own: uneven(own, SENTS, TOK_DEV, LONGEST, 2))(jax.random.split(arg_keys[1], N_DP)).reshape((N_DP, SENTS)).astype(jnp.int32)
    query_weight = gaussian(arg_keys[2], (D, D), D ** -0.5, 0.21875, ((1, 2),))
    w_key = gaussian(arg_keys[3], (D, D), D ** -0.5, 0.21875, ((1, 2),))
    value_weight = gaussian(arg_keys[4], (D, D), D ** -0.5, 0.21875, ((1, 2),))
    w_out = gaussian(arg_keys[5], (D, D), (D // 16) ** -0.5, 0.875, ((0, 2),))
    w_up = gaussian(arg_keys[6], (D, FF), D ** -0.5, 0.21875, ((1, 2),))
    w_down = gaussian(arg_keys[7], (FF, D), FF ** -0.5, 0.109375, ((0, 2),))
    gain_attn = jnp.clip(1.0 + 0.1 * jax.random.normal(arg_keys[8], (D,), jnp.float32), 0.5, 1.5)
    shift_attn = gaussian(arg_keys[9], (D,), 0.1, 0.6, (), jnp.float32)
    gain_ffn = jnp.clip(1.0 + 0.1 * jax.random.normal(arg_keys[10], (D,), jnp.float32), 0.5, 1.5)
    shift_ffn = gaussian(arg_keys[11], (D,), 0.1, 0.6, (), jnp.float32)
    factors = draw_factors(jax.random.fold_in(arg_keys[16], 71), 0)
    first_moment = gaussian(arg_keys[13], (PARAMS,), 0.1, 0.6, ((0, 32),), jnp.float32)
    second_moment = jnp.clip(jnp.exp(math.log(0.01) - 4.6051702 * jax.random.uniform(arg_keys[14], (PARAMS,), jnp.float32) ** level_of(arg_keys[14], (PARAMS,), ((0, 32),), -0.2, 0.2)), 0.0001, 0.01)
    cotangent = gaussian(arg_keys[15], (TOKENS, D), 1.0, 6.0, ((0, 16), (1, 2)))
    return {"tokens": tokens, "lengths": lengths, "query_weight": query_weight, "w_key": w_key, "value_weight": value_weight, "w_out": w_out, "w_up": w_up, "w_down": w_down, "gain_attn": gain_attn, "shift_attn": shift_attn, "gain_ffn": gain_ffn, "shift_ffn": shift_ffn, "factors": factors, "first_moment": first_moment, "second_moment": second_moment, "cotangent": cotangent}


EPS_NORM = 1e-05
EPS_ADAM = 1e-08
BETA_ONE = 0.9
BETA_TWO = 0.999
BIAS_ONE = 1.0 - 0.9 ** 10
BIAS_TWO = 1.0 - 0.999 ** 10
RATE_DOWN = 0.002
RATE_RATIO = 16.0
DECAY_RATE = 0.01
ADAPTER_SCALE = 2.0
MASKED_SCORE = -1e+30

@jax.custom_vjp
def reduced_rows(v):
    return lax.optimization_barrier(v.astype(jnp.bfloat16)).astype(jnp.float32)

@jax.custom_vjp
def reduced_backward(v):
    return v

def low_keep(v):
    return (reduced_rows(v), None)

def low_pass(kept, grad):
    return (grad,)

def back_keep(v):
    return (v, None)

def back_low(kept, grad):
    return (reduced_rows(grad),)
reduced_rows.defvjp(low_keep, low_pass)
reduced_backward.defvjp(back_keep, back_low)

def matrix_product(left_side, right_side):
    return jnp.dot(left_side, right_side, precision=lax.Precision.HIGHEST, preferred_element_type=jnp.float32)

def normalize(residual, gain_vec, shift_vec):
    row_mean = lax.optimization_barrier(jnp.mean(residual, axis=-1, keepdims=True))
    centered = residual - row_mean
    row_var = lax.optimization_barrier(jnp.mean(centered * centered, axis=-1, keepdims=True))
    return centered * lax.rsqrt(row_var + EPS_NORM) * gain_vec + shift_vec

def exact_gelu(values):
    return jax.nn.gelu(values, approximate=False)

def adam_update(gradient, moment_one, moment_two, weights, position, boundary):
    first_new = BETA_ONE * moment_one + (1.0 - BETA_ONE) * gradient
    second_new = BETA_TWO * moment_two + (1.0 - BETA_TWO) * gradient * gradient
    rates = jnp.where(position < boundary, RATE_DOWN, RATE_DOWN * RATE_RATIO)
    update = first_new / BIAS_ONE / (jnp.sqrt(second_new / BIAS_TWO) + EPS_ADAM)
    return (first_new, second_new, weights - rates * (update + DECAY_RATE * weights))

def split_factors(factors):
    size_down = D * ADAPTER_RANK
    down_query = factors[:size_down].reshape(D, ADAPTER_RANK)
    down_value = factors[size_down:2 * size_down].reshape(D, ADAPTER_RANK)
    query_up_weight = factors[2 * size_down:3 * size_down].reshape(ADAPTER_RANK, D)
    value_up_weight = factors[3 * size_down:].reshape(ADAPTER_RANK, D)
    return (down_query, down_value, query_up_weight, value_up_weight)

def block_forward(input_features, factors, frozen, segment):
    query_weight, w_key, value_weight, w_out, w_up, w_down, gain_attn, shift_attn, gain_ffn, shift_ffn = frozen
    down_query, down_value, query_up_weight, value_up_weight = split_factors(factors)
    tok_count = input_features.shape[0]
    query_middle = reduced_backward(reduced_rows(matrix_product(input_features, reduced_rows(down_query))))
    value_middle = reduced_backward(reduced_rows(matrix_product(input_features, reduced_rows(down_value))))
    query_combined = reduced_rows(reduced_backward(matrix_product(input_features, query_weight) + ADAPTER_SCALE * matrix_product(query_middle, reduced_rows(query_up_weight))))
    key_all = reduced_rows(reduced_backward(matrix_product(input_features, w_key)))
    value_combined = reduced_rows(reduced_backward(matrix_product(input_features, value_weight) + ADAPTER_SCALE * matrix_product(value_middle, reduced_rows(value_up_weight))))
    query_heads = query_combined.reshape(tok_count, HEADS, HEAD)
    key_heads = key_all.reshape(tok_count, HEADS, HEAD)
    value_heads = value_combined.reshape(tok_count, HEADS, HEAD)
    same_segment = segment[:, None] == segment[None, :]
    raw_scores = jnp.einsum('qhd,khd->hqk', query_heads, key_heads, precision=lax.Precision.HIGHEST) * (1.0 / math.sqrt(HEAD))
    raw_scores = reduced_backward(raw_scores)
    scores = jnp.where(same_segment[None], raw_scores, MASKED_SCORE)
    row_max = lax.optimization_barrier(jnp.max(scores, axis=-1, keepdims=True))
    weights_exp = jnp.exp(scores - row_max)
    prob_rows = reduced_rows(weights_exp / lax.optimization_barrier(jnp.sum(weights_exp, axis=-1, keepdims=True)))
    attended = jnp.einsum('hqk,khd->qhd', prob_rows, value_heads, precision=lax.Precision.HIGHEST).reshape(tok_count, D)
    attended = reduced_rows(reduced_backward(attended))
    attn_mixed = reduced_backward(matrix_product(attended, w_out))
    hidden = normalize(input_features + attn_mixed, gain_attn, shift_attn)
    upper_proj = reduced_backward(matrix_product(reduced_rows(hidden), w_up))
    ffn_out = reduced_backward(matrix_product(reduced_rows(exact_gelu(upper_proj)), w_down))
    return normalize(hidden + ffn_out, gain_ffn, shift_ffn)

def reference(tokens, lengths, query_weight, w_key, value_weight, w_out, w_up, w_down, gain_attn, shift_attn, gain_ffn, shift_ffn, factors, first_moment, second_moment, cotangent):
    frozen = tuple((weight.astype(jnp.float32) for weight in (query_weight, w_key, value_weight, w_out, w_up, w_down, gain_attn, shift_attn, gain_ffn, shift_ffn)))
    grouped = tokens.astype(jnp.float32).reshape(N_DP, TOK_DEV, D)
    cot_groups = cotangent.astype(jnp.float32).reshape(N_DP, TOK_DEV, D)
    factors_f = factors.astype(jnp.float32)

    def one_group(running, inputs):
        input_features, sent_lens, cot_rows = inputs
        sent_ends = jnp.cumsum(sent_lens).astype(jnp.int32)
        position = jnp.arange(TOK_DEV, dtype=jnp.int32)
        segment = lax.optimization_barrier(jnp.sum((position[:, None] >= sent_ends[None, :]).astype(jnp.int32), axis=1)).astype(jnp.int32)
        encoded_rows, pullback = jax.vjp(lambda feats, facs: block_forward(feats, facs, frozen, segment), input_features, factors_f)
        d_rows, d_factors = pullback(cot_rows)
        return (running + d_factors, (encoded_rows.astype(jnp.bfloat16), d_rows))
    summed, (encoded, d_groups) = lax.scan(one_group, jnp.zeros((PARAMS,), jnp.float32), (grouped, lengths, cot_groups))
    gradients = summed * (1.0 / math.sqrt(TOKENS))
    position = jnp.arange(PARAMS, dtype=jnp.int32)
    first_new, second_new, factors_new = adam_update(gradients, first_moment, second_moment, factors_f, position, 2 * D * ADAPTER_RANK)
    return (encoded.reshape(TOKENS, D), d_groups.reshape(TOKENS, D), gradients, first_new, second_new, factors_new)
```

```python
import functools
import math

import jax
import jax.numpy as jnp
from jax import lax
from jax.experimental import pallas as pl
from jax.experimental.pallas import tpu as pltpu
from jax.sharding import PartitionSpec as P

HEAD = 64
RANK = 8
EPS_NORM = 1e-05
EPS_ADAM = 1e-08
BETA_ONE = 0.9
BETA_TWO = 0.999
BIAS_ONE = 1.0 - 0.9**10
BIAS_TWO = 1.0 - 0.999**10
RATE_DOWN = 0.002
RATE_RATIO = 16.0
DECAY_RATE = 0.01
ADAPTER_SCALE = 2.0
MASKED = -1e30
LOG2E = 1.4426950408889634
LN2 = 0.6931471805599453

TILE = 128
ALIGN = 16
PAIR = 2 * HEAD
VMEM_LIMIT = 56 * 1024 * 1024
BF16 = jnp.bfloat16
F32 = jnp.float32

ANY = pl.BlockSpec(memory_space=pl.ANY)
SMEM = pl.BlockSpec(memory_space=pltpu.SMEM)
VMEM = pl.BlockSpec(memory_space=pltpu.VMEM)


def shape_of(dims, kind):
    return jax.ShapeDtypeStruct(dims, kind)


def params():
    return pltpu.CompilerParams(vmem_limit_bytes=VMEM_LIMIT)


def nn(left, right):
    return lax.dot_general(left, right, (((1,), (0,)), ((), ())), preferred_element_type=F32)


def nt(left, right):
    return lax.dot_general(left, right, (((1,), (1,)), ((), ())), preferred_element_type=F32)


def tn(left, right):
    return lax.dot_general(left, right, (((0,), (0,)), ((), ())), preferred_element_type=F32)


def start_all(copies):
    for copy in copies:
        copy.start()
    return copies


def wait_all(copies):
    for copy in copies:
        copy.wait()


def for_each_sentence(lengths_ref, sentences, longest, visit):
    def one(index, carry):
        first, tile = carry
        end = first + lengths_ref[index]
        start = pl.multiple_of((first // ALIGN) * ALIGN, ALIGN)
        steps = (end - start + (TILE - 1)) // TILE
        for count in range(1, (longest + ALIGN - 1 + TILE - 1) // TILE + 1):

            @pl.when(steps == count)
            def _():
                visit(count, start, first, end, tile)

        return end, tile + steps

    lax.fori_loop(0, sentences, one, (jnp.int32(0), jnp.int32(0)))


def key_rows_masked(values, start, first, end, fill):
    window, lanes = values.shape

    def masked(low, high):
        rows = low + lax.broadcasted_iota(jnp.int32, (high - low, lanes), 0)
        inside = rows < end - start
        if low == 0:
            inside = inside & (rows >= first - start)
        return jnp.where(inside, values[low:high], fill)

    if window == TILE:
        return masked(0, TILE)
    rows = lax.broadcasted_iota(jnp.int32, (ALIGN, lanes), 0)
    top = jnp.where(rows >= first - start, values[:ALIGN], fill)
    return jnp.concatenate(
        [top, values[ALIGN : window - TILE], masked(window - TILE, window)], axis=0
    )


def split_pair(rows):
    lane = lax.broadcasted_iota(jnp.int32, rows.shape, 1)
    zero = jnp.zeros_like(rows)
    return jnp.concatenate(
        [jnp.where(lane < HEAD, rows, zero), jnp.where(lane < HEAD, zero, rows)], axis=0
    )


def merge_pair(columns):
    row = lax.broadcasted_iota(jnp.int32, (PAIR, TILE), 0)
    return jnp.where(row < HEAD, columns[:, :TILE], columns[:, TILE:]).T


def prepare_kernel(wq_ref, wk_ref, wv_ref, down_ref, up_ref, wcat_ref):
    width = wq_ref.shape[1]
    down = down_ref[...]
    lane = lax.broadcasted_iota(jnp.int32, down.shape, 1)
    zero = jnp.zeros_like(down)
    down_q = jnp.where(lane < RANK, down, zero)
    down_v = jnp.where((lane >= RANK) & (lane < 2 * RANK), down, zero)
    up = up_ref[...]
    wcat_ref[:, :width] = (
        wq_ref[...].astype(F32) + ADAPTER_SCALE * nn(down_q, up)
    ).astype(BF16)
    wcat_ref[:, width : 2 * width] = wk_ref[...]
    wcat_ref[:, 2 * width : 3 * width] = (
        wv_ref[...].astype(F32) + ADAPTER_SCALE * nn(down_v, up)
    ).astype(BF16)
    wcat_ref[:, 3 * width :] = down


def prepare(wq, wk, wv, down, up):
    features, width = wq.shape
    return pl.pallas_call(
        prepare_kernel,
        out_shape=shape_of((features, 3 * width + 128), BF16),
        in_specs=[VMEM] * 5,
        out_specs=VMEM,
        compiler_params=params(),
        name="prepare",
    )(wq, wk, wv, down, up)


def forward_kernel(
    longest,
    tp_ref,
    lengths_ref,
    xown_ref,
    xoth_ref,
    wcat_ref,
    q_out,
    k_out,
    v_out,
    mid_out,
    keep_out,
    send_out,
    lse_ref,
    x_buf,
    q_buf,
    k_buf,
    v_buf,
    mid_buf,
    att_buf,
    vt_buf,
    in_sem,
    out_sem,
):
    rows, width = xown_ref.shape
    half = rows // 2
    pairs = width // PAIR
    me = tp_ref[0]
    mine = pl.multiple_of(me * width, 128)
    theirs = pl.multiple_of((1 - me) * width, 128)
    loads = start_all(
        [
            pltpu.make_async_copy(xown_ref, x_buf.at[:, pl.ds(mine, width)], in_sem.at[0]),
            pltpu.make_async_copy(xoth_ref, x_buf.at[:, pl.ds(theirs, width)], in_sem.at[1]),
        ]
    )
    for buf in (q_buf, k_buf, v_buf):
        buf[rows:, :] = jnp.zeros((buf.shape[0] - rows, width), BF16)
    lse_ref[...] = jnp.full(lse_ref.shape, -MASKED, F32)
    wait_all(loads)
    block = min(512, rows)

    @pl.loop(0, rows // block)
    def _(index):
        at = pl.ds(pl.multiple_of(index * block, block), block)
        features = x_buf[at, :]
        q_buf[at, :] = (
            nn(features, wcat_ref[:, :width]) * (LOG2E / math.sqrt(HEAD))
        ).astype(BF16)
        k_buf[at, :] = nn(features, wcat_ref[:, width : 2 * width]).astype(BF16)
        v_buf[at, :] = nn(features, wcat_ref[:, 2 * width : 3 * width]).astype(BF16)
        mid_buf[at, :] = nn(features, wcat_ref[:, 3 * width :]).astype(BF16)

    stores = start_all(
        [
            pltpu.make_async_copy(q_buf.at[pl.ds(0, rows)], q_out, out_sem.at[0]),
            pltpu.make_async_copy(k_buf.at[pl.ds(0, rows)], k_out, out_sem.at[1]),
            pltpu.make_async_copy(v_buf.at[pl.ds(0, rows)], v_out, out_sem.at[2]),
            pltpu.make_async_copy(mid_buf, mid_out, out_sem.at[3]),
        ]
    )

    def visit(count, start, first, end, tile):
        window = count * TILE
        keys_at = pl.ds(start, window)
        for pair in range(pairs):
            cols = slice(pair * PAIR, (pair + 1) * PAIR)
            vt_buf[pair, :, :window] = v_buf[keys_at, cols].T

        def one_tile(index, _):
            low = pl.multiple_of(start + index * TILE, ALIGN)
            at = pl.ds(low, TILE)
            row = low + lax.broadcasted_iota(jnp.int32, (TILE, PAIR), 0)
            row_valid = (row >= first) & (row < end)
            lane = lax.broadcasted_iota(jnp.int32, (1, 2 * TILE), 1)
            place = low + jnp.where(lane < TILE, lane, lane - TILE)
            lane_valid = (place >= first) & (place < end)
            for pair in range(pairs):
                cols = slice(pair * PAIR, (pair + 1) * PAIR)
                scores = nt(k_buf[keys_at, cols], split_pair(q_buf[at, cols]))
                scores = key_rows_masked(scores, start, first, end, MASKED)
                top = jnp.max(scores, axis=0, keepdims=True)
                weights = jnp.exp2(scores - top)
                total = jnp.sum(weights, axis=0, keepdims=True)
                columns = nn(vt_buf[pair, :, :window], weights.astype(BF16)) * (1.0 / total)
                merged = merge_pair(columns)
                old = att_buf[at, cols].astype(F32)
                att_buf[at, cols] = jnp.where(row_valid, merged, old).astype(BF16)
                lse_ref[pair, pl.ds(tile + index, 1), :] = jnp.where(
                    lane_valid, top + jnp.log2(total), -MASKED
                )
            return 0

        lax.fori_loop(0, count, one_tile, 0)

    for_each_sentence(lengths_ref, lengths_ref.shape[0], longest, visit)
    mine_rows = pl.multiple_of(me * half, half)
    their_rows = pl.multiple_of((1 - me) * half, half)
    stores += start_all(
        [
            pltpu.make_async_copy(att_buf.at[pl.ds(their_rows, half)], send_out, out_sem.at[4]),
            pltpu.make_async_copy(att_buf.at[pl.ds(mine_rows, half)], keep_out, out_sem.at[5]),
        ]
    )
    wait_all(stores)


def tiles_at_most(rows, sentences):
    return -(-(rows + sentences * (ALIGN - 1 + TILE - 1)) // TILE)


def forward(tp, lengths, x_own, x_oth, wcat, longest):
    rows, width = x_own.shape
    half = rows // 2
    pairs = width // PAIR
    tiles = -(-tiles_at_most(rows, lengths.shape[0]) // 8) * 8
    padded = rows + TILE
    widest = -(-(longest + ALIGN - 1) // TILE) * TILE
    return pl.pallas_call(
        functools.partial(forward_kernel, longest),
        out_shape=[
            shape_of((rows, width), BF16),
            shape_of((rows, width), BF16),
            shape_of((rows, width), BF16),
            shape_of((rows, 128), BF16),
            shape_of((half, width), BF16),
            shape_of((half, width), BF16),
            shape_of((pairs, tiles, 2 * TILE), F32),
        ],
        in_specs=[SMEM, SMEM, ANY, ANY, VMEM],
        out_specs=[ANY] * 6 + [VMEM],
        scratch_shapes=[
            pltpu.VMEM((rows, 2 * width), BF16),
            pltpu.VMEM((padded, width), BF16),
            pltpu.VMEM((padded, width), BF16),
            pltpu.VMEM((padded, width), BF16),
            pltpu.VMEM((rows, 128), BF16),
            pltpu.VMEM((padded, width), BF16),
            pltpu.VMEM((pairs, PAIR, widest), BF16),
            pltpu.SemaphoreType.DMA((2,)),
            pltpu.SemaphoreType.DMA((6,)),
        ],
        compiler_params=params(),
        name="forward",
    )(tp, lengths, x_own, x_oth, wcat)


def cdf_and_slope(upper):
    size = jnp.abs(upper)
    inner = 1.0 / (1.0 + (0.3275911 / math.sqrt(2.0)) * size)
    bell = jnp.exp2(upper * upper * (-0.5 * LOG2E))
    poly = 0.5 * 1.061405429
    for factor in (-1.453152027, 1.421413741, -0.284496736, 0.254829592):
        poly = poly * inner + 0.5 * factor
    tail = poly * inner * bell
    below = jnp.where(upper < 0.0, tail, 1.0 - tail)
    return below, below + upper * bell * (1.0 / math.sqrt(2.0 * math.pi))


def row_mean(values):
    return jnp.mean(values, axis=-1, keepdims=True)


def rows_kernel(
    tp_ref,
    keep_ref,
    recv_ref,
    xown_ref,
    xoth_ref,
    cotown_ref,
    cototh_ref,
    wout_own,
    wout_oth,
    wup_own,
    wup_oth,
    wdown_own,
    wdown_oth,
    gain1_ref,
    shift1_ref,
    gain2_ref,
    shift2_ref,
    enc_keep,
    enc_send,
    dres_keep,
    dres_send,
    datt_keep,
    datt_send,
    att_buf,
    x_buf,
    cot_buf,
    wout_buf,
    wup_buf,
    wdown_buf,
    slope_buf,
    enc_buf,
    dres_buf,
    datt_buf,
    in_sem,
    out_sem,
):
    half, width = keep_ref.shape
    units = wup_own.shape[1]
    me = tp_ref[0]
    mine = pl.multiple_of(me * width, 128)
    theirs = pl.multiple_of((1 - me) * width, 128)
    own_rows = pl.ds(pl.multiple_of(me * half, half), half)
    copy = pltpu.make_async_copy
    loads = start_all(
        [
            copy(keep_ref, att_buf.at[:, pl.ds(0, width)], in_sem.at[0]),
            copy(recv_ref, att_buf.at[:, pl.ds(width, width)], in_sem.at[1]),
            copy(wout_own, wout_buf.at[pl.ds(0, width)], in_sem.at[2]),
            copy(wout_oth, wout_buf.at[pl.ds(width, width)], in_sem.at[3]),
            copy(xown_ref.at[own_rows], x_buf.at[:, pl.ds(mine, width)], in_sem.at[4]),
            copy(xoth_ref.at[own_rows], x_buf.at[:, pl.ds(theirs, width)], in_sem.at[5]),
            copy(wup_own, wup_buf.at[:, pl.ds(0, units)], in_sem.at[6]),
            copy(wup_oth, wup_buf.at[:, pl.ds(units, units)], in_sem.at[7]),
            copy(wdown_own, wdown_buf.at[pl.ds(0, units)], in_sem.at[8]),
            copy(wdown_oth, wdown_buf.at[pl.ds(units, units)], in_sem.at[9]),
            copy(cotown_ref.at[own_rows], cot_buf.at[:, pl.ds(mine, width)], in_sem.at[10]),
            copy(cototh_ref, cot_buf.at[:, pl.ds(theirs, width)], in_sem.at[11]),
        ]
    )
    wait_all(loads)
    gain1, shift1 = gain1_ref[...], shift1_ref[...]
    gain2, shift2 = gain2_ref[...], shift2_ref[...]
    block = min(256, half)
    chunk = min(512, units)
    chunks = 2 * units // chunk

    @pl.loop(0, half // block)
    def _(index):
        at = pl.ds(pl.multiple_of(index * block, block), block)
        resid = x_buf[at, :].astype(F32) + nn(att_buf[at, :], wout_buf[...])
        centered = resid - row_mean(resid)
        scale1 = lax.rsqrt(row_mean(centered * centered) + EPS_NORM)
        normed1 = centered * scale1
        hidden = normed1 * gain1 + shift1
        hidden_low = hidden.astype(BF16)
        outer = hidden
        for part in range(chunks):
            cols = slice(part * chunk, (part + 1) * chunk)
            upper = nn(hidden_low, wup_buf[:, cols])
            below, slope = cdf_and_slope(upper)
            slope_buf[:, cols] = slope.astype(BF16)
            outer = outer + nn((upper * below).astype(BF16), wdown_buf[cols, :])
        centered = outer - row_mean(outer)
        scale2 = lax.rsqrt(row_mean(centered * centered) + EPS_NORM)
        normed2 = centered * scale2
        enc_buf[at, :] = (normed2 * gain2 + shift2).astype(BF16)
        pulled = cot_buf[at, :].astype(F32) * gain2
        d_outer = scale2 * (pulled - row_mean(pulled) - normed2 * row_mean(pulled * normed2))
        d_low = d_outer.astype(BF16)
        d_hidden = d_outer
        for part in range(chunks):
            cols = slice(part * chunk, (part + 1) * chunk)
            d_act = nt(d_low, wdown_buf[cols, :])
            d_upper = (d_act * slope_buf[:, cols].astype(F32)).astype(BF16)
            d_hidden = d_hidden + nt(d_upper, wup_buf[:, cols])
        pulled = d_hidden * gain1
        d_res = scale1 * (pulled - row_mean(pulled) - normed1 * row_mean(pulled * normed1))
        dres_buf[at, :] = d_res
        datt_buf[at, :] = nt(d_res.astype(BF16), wout_buf[...]).astype(BF16)

    stores = start_all(
        [
            copy(datt_buf.at[:, pl.ds(width, width)], datt_send, out_sem.at[0]),
            copy(datt_buf.at[:, pl.ds(0, width)], datt_keep, out_sem.at[1]),
            copy(enc_buf.at[:, pl.ds(theirs, width)], enc_send, out_sem.at[2]),
            copy(enc_buf.at[:, pl.ds(mine, width)], enc_keep, out_sem.at[3]),
            copy(dres_buf.at[:, pl.ds(theirs, width)], dres_send, out_sem.at[4]),
            copy(dres_buf.at[:, pl.ds(mine, width)], dres_keep, out_sem.at[5]),
        ]
    )
    wait_all(stores)


def rows_step(tp, keep, recv, x_own, x_oth, cot_own, cot_oth, weights, norms):
    half, width = keep.shape
    units = weights[2].shape[1]
    block = min(256, half)
    return pl.pallas_call(
        rows_kernel,
        out_shape=[
            shape_of((half, width), BF16),
            shape_of((half, width), BF16),
            shape_of((half, width), F32),
            shape_of((half, width), F32),
            shape_of((half, width), BF16),
            shape_of((half, width), BF16),
        ],
        in_specs=[SMEM] + [ANY] * 12 + [VMEM] * 4,
        out_specs=[ANY] * 6,
        scratch_shapes=[
            pltpu.VMEM((half, 2 * width), BF16),
            pltpu.VMEM((half, 2 * width), BF16),
            pltpu.VMEM((half, 2 * width), BF16),
            pltpu.VMEM((2 * width, 2 * width), BF16),
            pltpu.VMEM((2 * width, 2 * units), BF16),
            pltpu.VMEM((2 * units, 2 * width), BF16),
            pltpu.VMEM((block, 2 * units), BF16),
            pltpu.VMEM((half, 2 * width), BF16),
            pltpu.VMEM((half, 2 * width), F32),
            pltpu.VMEM((half, 2 * width), BF16),
            pltpu.SemaphoreType.DMA((12,)),
            pltpu.SemaphoreType.DMA((6,)),
        ],
        compiler_params=params(),
        name="rows_step",
    )(tp, keep, recv, x_own, x_oth, cot_own, cot_oth, *weights, *norms)


def backward_kernel(
    longest,
    tp_ref,
    lengths_ref,
    q_ref,
    k_ref,
    v_ref,
    dkeep_ref,
    drecv_ref,
    xown_ref,
    xoth_ref,
    mid_ref,
    lse_ref,
    upq_ref,
    upv_ref,
    d_out,
    grad_ref,
    q_buf,
    k_buf,
    v_buf,
    do_buf,
    x_buf,
    mid_buf,
    dk_acc,
    dv_acc,
    d_buf,
    kt_buf,
    in_sem,
    out_sem,
):
    rows, width = q_ref.shape
    half = rows // 2
    pairs = width // PAIR
    me = tp_ref[0]
    mine = pl.multiple_of(me * width, 128)
    theirs = pl.multiple_of((1 - me) * width, 128)
    mine_rows = pl.ds(pl.multiple_of(me * half, half), half)
    their_rows = pl.ds(pl.multiple_of((1 - me) * half, half), half)
    copy = pltpu.make_async_copy
    body_rows = pl.ds(0, rows)
    loads = start_all(
        [
            copy(q_ref, q_buf.at[body_rows], in_sem.at[0]),
            copy(k_ref, k_buf.at[body_rows], in_sem.at[1]),
            copy(v_ref, v_buf.at[body_rows], in_sem.at[2]),
            copy(dkeep_ref, do_buf.at[mine_rows], in_sem.at[3]),
            copy(drecv_ref, do_buf.at[their_rows], in_sem.at[4]),
        ]
    )
    late = start_all(
        [
            copy(xown_ref, x_buf.at[:, pl.ds(mine, width)], in_sem.at[5]),
            copy(xoth_ref, x_buf.at[:, pl.ds(theirs, width)], in_sem.at[6]),
            copy(mid_ref, mid_buf, in_sem.at[7]),
        ]
    )
    extra = q_buf.shape[0] - rows
    for buf in (q_buf, k_buf, v_buf, do_buf):
        buf[rows:, :] = jnp.zeros((extra, width), BF16)
    zero_block = TILE

    @pl.loop(0, q_buf.shape[0] // zero_block)
    def _(index):
        at = pl.ds(pl.multiple_of(index * zero_block, zero_block), zero_block)
        dk_acc[at, :] = jnp.zeros((zero_block, width), F32)
        dv_acc[at, :] = jnp.zeros((zero_block, width), F32)

    wait_all(loads)

    def visit(count, start, first, end, tile):
        window = count * TILE
        keys_at = pl.ds(start, window)
        for pair in range(pairs):
            cols = slice(pair * PAIR, (pair + 1) * PAIR)
            kt_buf[pair, :, :window] = k_buf[keys_at, cols].T

        def one_tile(index, _):
            low = pl.multiple_of(start + index * TILE, ALIGN)
            at = pl.ds(low, TILE)
            row = low + lax.broadcasted_iota(jnp.int32, (TILE, PAIR), 0)
            row_valid = (row >= first) & (row < end)
            for pair in range(pairs):
                cols = slice(pair * PAIR, (pair + 1) * PAIR)
                queries = split_pair(q_buf[at, cols])
                d_rows = split_pair(do_buf[at, cols])
                scores = nt(k_buf[keys_at, cols], queries)
                d_probs = nt(v_buf[keys_at, cols], d_rows)
                probs = jnp.exp2(scores - lse_ref[pair, pl.ds(tile + index, 1), :])
                probs = key_rows_masked(probs, start, first, end, 0.0)
                product = probs * d_probs
                delta = jnp.sum(product, axis=0, keepdims=True)
                d_scores = (product - probs * delta).astype(BF16)
                dv_acc[keys_at, cols] += nn(probs.astype(BF16), d_rows)
                dk_acc[keys_at, cols] += nn(d_scores, queries)
                merged = merge_pair(nn(kt_buf[pair, :, :window], d_scores))
                merged = merged * (1.0 / math.sqrt(HEAD))
                old = d_buf[at, cols].astype(F32)
                d_buf[at, cols] = jnp.where(row_valid, merged, old).astype(BF16)
            return 0

        lax.fori_loop(0, count, one_tile, 0)

    for_each_sentence(lengths_ref, lengths_ref.shape[0], longest, visit)

    block = min(512, rows)

    @pl.loop(0, rows // block)
    def _(index):
        at = pl.ds(pl.multiple_of(index * block, block), block)
        d_buf[at, width : 2 * width] = (dk_acc[at, :] * LN2).astype(BF16)
        d_buf[at, 2 * width :] = dv_acc[at, :].astype(BF16)

    store = start_all([copy(d_buf.at[body_rows], d_out, out_sem.at[0])])
    wait_all(late)
    d_query = d_buf[:rows, :width]
    d_value = d_buf[:rows, 2 * width :]
    mid = mid_buf[...]
    stretch = lax.broadcasted_iota(jnp.int32, (16, 128), 0)
    picked = stretch == lax.broadcasted_iota(jnp.int32, (16, 128), 1) // RANK
    features = 2 * width
    flat = features * RANK // 128
    for which, (grads, up_ref) in enumerate(((d_query, upq_ref), (d_value, upv_ref))):
        d_mid = nt(grads, up_ref[...]).astype(BF16)
        down = tn(d_mid, x_buf[...]).T
        down = jnp.where(picked[None], down.reshape(flat, 16, 128), 0.0)
        grad_ref[pl.ds(which * flat, flat), :] = jnp.sum(down, axis=1)
        up = ADAPTER_SCALE * tn(mid, grads)
        up = up[which * RANK : (which + 1) * RANK]
        steps = features // 128
        base = (2 + which) * flat
        for step in range(width // 128):
            part = up[:, step * 128 : (step + 1) * 128]
            for r in range(RANK):
                grad_ref[pl.ds(base + r * steps + me * (width // 128) + step, 1), :] = part[
                    r : r + 1
                ]
                grad_ref[
                    pl.ds(base + r * steps + (1 - me) * (width // 128) + step, 1), :
                ] = jnp.zeros((1, 128), F32)
    wait_all(store)


def backward(tp, lengths, q, k, v, d_keep, d_recv, x_own, x_oth, mid, lse, up_q, up_v, longest):
    rows, width = q.shape
    pairs = width // PAIR
    padded = rows + TILE
    widest = -(-(longest + ALIGN - 1) // TILE) * TILE
    return pl.pallas_call(
        functools.partial(backward_kernel, longest),
        out_shape=[
            shape_of((rows, 3 * width), BF16),
            shape_of((8 * width * RANK // 128, 128), F32),
        ],
        in_specs=[SMEM, SMEM] + [ANY] * 8 + [VMEM] * 3,
        out_specs=[ANY, VMEM],
        scratch_shapes=[
            pltpu.VMEM((padded, width), BF16),
            pltpu.VMEM((padded, width), BF16),
            pltpu.VMEM((padded, width), BF16),
            pltpu.VMEM((padded, width), BF16),
            pltpu.VMEM((rows, 2 * width), BF16),
            pltpu.VMEM((rows, 128), BF16),
            pltpu.VMEM((padded, width), F32),
            pltpu.VMEM((padded, width), F32),
            pltpu.VMEM((padded, 3 * width), BF16),
            pltpu.VMEM((pairs, PAIR, widest), BF16),
            pltpu.SemaphoreType.DMA((8,)),
            pltpu.SemaphoreType.DMA((1,)),
        ],
        compiler_params=params(),
        name="backward",
    )(tp, lengths, q, k, v, d_keep, d_recv, x_own, x_oth, mid, lse, up_q, up_v)


def token_send_kernel(tp_ref, d_ref, wcat_ref, dres_ref, out_ref):
    half, width = dres_ref.shape
    me = tp_ref[0]
    block = min(512, half)
    weight_at = pl.ds(pl.multiple_of((1 - me) * width, 128), width)

    @pl.loop(0, half // block)
    def _(index):
        part = pl.ds(pl.multiple_of(index * block, block), block)
        own = pl.ds(pl.multiple_of(me * half + index * block, block), block)
        other = pl.ds(pl.multiple_of((1 - me) * half + index * block, block), block)
        weights = wcat_ref[weight_at, : 3 * width]
        out_ref[own, :] = (dres_ref[part, :] + nt(d_ref[own, :], weights)).astype(BF16)
        out_ref[other, :] = nt(d_ref[other, :], weights).astype(BF16)


def token_keep_kernel(tp_ref, d_ref, wcat_ref, dres_ref, recv_ref, out_ref):
    half, width = dres_ref.shape
    me = tp_ref[0]
    block = min(512, half)
    weight_at = pl.ds(pl.multiple_of(me * width, 128), width)

    @pl.loop(0, half // block)
    def _(index):
        part = pl.ds(pl.multiple_of(index * block, block), block)
        own = pl.ds(pl.multiple_of(me * half + index * block, block), block)
        other = pl.ds(pl.multiple_of((1 - me) * half + index * block, block), block)
        weights = wcat_ref[weight_at, : 3 * width]
        out_ref[own, :] = (
            dres_ref[part, :] + nt(d_ref[own, :], weights) + recv_ref[own, :].astype(F32)
        )
        out_ref[other, :] = nt(d_ref[other, :], weights) + recv_ref[other, :].astype(F32)


def token_step(tp, d, wcat, dres, recv=None):
    rows = d.shape[0]
    width = dres.shape[1]
    last = recv is not None
    return pl.pallas_call(
        token_keep_kernel if last else token_send_kernel,
        out_shape=shape_of((rows, width), F32 if last else BF16),
        in_specs=[SMEM] + [VMEM] * (4 if last else 3),
        out_specs=VMEM,
        compiler_params=params(),
        name="token_keep" if last else "token_send",
    )(*((tp, d, wcat, dres) + ((recv,) if last else ())))


def adam_update(gradient, moment_one, moment_two, weights, rates):
    first_new = BETA_ONE * moment_one + (1.0 - BETA_ONE) * gradient
    second_new = BETA_TWO * moment_two + (1.0 - BETA_TWO) * gradient * gradient
    update = first_new / BIAS_ONE / (jnp.sqrt(second_new / BIAS_TWO) + EPS_ADAM)
    return first_new, second_new, weights - rates * (update + DECAY_RATE * weights)


def summed_over_all(values, dp_size):
    values = values + swap(values)
    step = 1
    while step < dp_size:
        order = [(i, i ^ step) for i in range(dp_size)]
        values = values + lax.ppermute(values, "dp", order)
        step *= 2
    return values


def swap(values):
    return lax.ppermute(values, "tp", [(0, 1), (1, 0)])


def body(
    tokens,
    lengths,
    query_weight,
    w_key,
    value_weight,
    w_out,
    w_up,
    w_down,
    gain_attn,
    shift_attn,
    gain_ffn,
    shift_ffn,
    factors,
    first_moment,
    second_moment,
    cotangent,
):
    rows, width = tokens.shape
    features = 2 * width
    half = rows // 2
    longest = min(512, rows)
    me = lax.axis_index("tp")
    tp = me.astype(jnp.int32).reshape(1)
    dp_size = lax.axis_size("dp")
    col_start = me * width
    other_rows = (1 - me) * half
    size_down = features * RANK
    own_lengths = lengths.reshape(-1)

    x_oth = swap(tokens)
    down = jnp.concatenate(
        [
            factors[:size_down].reshape(features, RANK),
            factors[size_down : 2 * size_down].reshape(features, RANK),
        ],
        axis=1,
    ).astype(BF16)
    down = jnp.pad(down, ((0, 0), (0, 128 - 2 * RANK)))
    up = lax.dynamic_slice_in_dim(
        factors[2 * size_down :].reshape(2 * RANK, features), col_start, width, 1
    ).astype(BF16)
    up_q = jnp.tile(ADAPTER_SCALE * up[:RANK], (128 // RANK, 1))
    up_v = jnp.tile(ADAPTER_SCALE * up[RANK:], (128 // RANK, 1))
    up_rows = jnp.pad(up, ((0, 128 - 2 * RANK), (0, 0)))
    wcat = prepare(query_weight, w_key, value_weight, down, up_rows)

    held = lax.optimization_barrier((x_oth, w_out, w_up, w_down, cotangent))
    x_oth = held[0]
    out_oth, up_oth, down_oth = swap(held[1]), swap(held[2]), swap(held[3])
    cot_oth = swap(lax.dynamic_slice_in_dim(held[4], other_rows, half, 0))
    moments = jnp.stack([first_moment, second_moment])
    all_moments = lax.all_gather(moments, ("dp", "tp"), axis=1, tiled=True)

    q, k, v, mid, att_keep, att_send, lse = forward(
        tp, own_lengths, tokens, x_oth, wcat, longest
    )
    att_recv = swap(att_send)
    norms = [part.reshape(1, features) for part in (gain_attn, shift_attn, gain_ffn, shift_ffn)]
    enc_keep, enc_send, dres_keep, dres_send, datt_keep, datt_send = rows_step(
        tp,
        att_keep,
        att_recv,
        tokens,
        x_oth,
        cotangent,
        cot_oth,
        (w_out, out_oth, w_up, up_oth, w_down, down_oth),
        norms,
    )
    datt_recv = swap(datt_send)
    enc_recv = swap(enc_send)
    encoded = jnp.where(
        me == 0,
        jnp.concatenate([enc_keep, enc_recv], axis=0),
        jnp.concatenate([enc_recv, enc_keep], axis=0),
    )
    d_all, grad_term = backward(
        tp,
        own_lengths,
        q,
        k,
        v,
        datt_keep,
        datt_recv,
        tokens,
        x_oth,
        mid,
        lse,
        up_q,
        up_v,
        longest,
    )
    total = summed_over_all(grad_term, dp_size)
    tok_recv = swap(token_step(tp, d_all, wcat, dres_send))
    d_tokens = token_step(tp, d_all, wcat, dres_keep, tok_recv)

    gradient = total.reshape(-1) * (1.0 / math.sqrt(rows * dp_size))
    place = jnp.arange(gradient.shape[0], dtype=jnp.int32)
    rates = jnp.where(place < 2 * size_down, RATE_DOWN, RATE_DOWN * RATE_RATIO)
    _, _, factors_new = adam_update(
        gradient, all_moments[0], all_moments[1], factors, rates
    )
    share = first_moment.shape[0]
    share_start = lax.axis_index(("dp", "tp")) * share
    grad_share = lax.dynamic_slice_in_dim(gradient, share_start, share)
    first_new, second_new, _ = adam_update(grad_share, first_moment, second_moment, 0.0, 0.0)
    return encoded, d_tokens, grad_share, first_new, second_new, factors_new


def solution(mesh):
    placed = (
        P("dp", "tp"),
        P("dp", None),
        P(None, "tp"),
        P(None, "tp"),
        P(None, "tp"),
        P("tp", None),
        P(None, "tp"),
        P("tp", None),
        P(),
        P(),
        P(),
        P(),
        P(),
        P(("dp", "tp")),
        P(("dp", "tp")),
        P("dp", "tp"),
    )
    return jax.shard_map(
        body,
        mesh=mesh,
        in_specs=placed,
        out_specs=(
            P("dp", "tp"),
            P("dp", "tp"),
            P(("dp", "tp")),
            P(("dp", "tp")),
            P(("dp", "tp")),
            P(),
        ),
        check_vma=False,
    )
```

```python
import functools
import math

import jax
import jax.numpy as jnp
from jax import lax
from jax.experimental import pallas as pl
from jax.experimental.pallas import tpu as pltpu
from jax.sharding import PartitionSpec as P

HEAD = 64
RANK = 8
EPS_NORM = 1e-05
EPS_ADAM = 1e-08
BETA_ONE = 0.9
BETA_TWO = 0.999
BIAS_ONE = 1.0 - 0.9**10
BIAS_TWO = 1.0 - 0.999**10
RATE_DOWN = 0.002
RATE_RATIO = 16.0
DECAY_RATE = 0.01
ADAPTER_SCALE = 2.0
MASKED = -1e30
LOG2E = 1.4426950408889634
LN2 = 0.6931471805599453

TILE = 128
ALIGN = 16
PAIR = 2 * HEAD
GATHER_ROWS = 128
VMEM_LIMIT = 56 * 1024 * 1024
BF16 = jnp.bfloat16
F32 = jnp.float32

ANY = pl.BlockSpec(memory_space=pl.ANY)
SMEM = pl.BlockSpec(memory_space=pltpu.SMEM)
VMEM = pl.BlockSpec(memory_space=pltpu.VMEM)


def shape_of(dims, kind):
    return jax.ShapeDtypeStruct(dims, kind)


def params():
    return pltpu.CompilerParams(vmem_limit_bytes=VMEM_LIMIT)


def nn(left, right):
    return lax.dot_general(left, right, (((1,), (0,)), ((), ())), preferred_element_type=F32)


def nt(left, right):
    return lax.dot_general(left, right, (((1,), (1,)), ((), ())), preferred_element_type=F32)


def tn(left, right):
    return lax.dot_general(left, right, (((0,), (0,)), ((), ())), preferred_element_type=F32)


def start_all(copies):
    for copy in copies:
        copy.start()
    return copies


def wait_all(copies):
    for copy in copies:
        copy.wait()


def for_each_sentence(lengths_ref, longest, rows, chunk, await_chunk, visit):
    def one(index, carry):
        first, tile, loaded = carry
        end = first + lengths_ref[index]
        start = pl.multiple_of((first // ALIGN) * ALIGN, ALIGN)
        steps = (end - start + (TILE - 1)) // TILE
        needed = jnp.minimum((start + steps * TILE + chunk - 1) // chunk, rows // chunk)
        loaded = await_chunks(loaded, needed)
        for count in range(1, (longest + ALIGN - 1 + TILE - 1) // TILE + 1):

            @pl.when(steps == count)
            def _():
                visit(count, start, first, end, tile)

        return end, tile + steps, loaded

    def await_chunks(loaded, needed):
        def one_chunk(index, _):
            await_chunk(index)
            return 0

        lax.fori_loop(loaded, needed, one_chunk, 0)
        return jnp.maximum(loaded, needed)

    zero = jnp.int32(0)
    carry = lax.fori_loop(0, lengths_ref.shape[0], one, (zero, zero, zero))
    await_chunks(carry[2], jnp.int32(rows // chunk))


def window_parts(window, start, first, end):
    def mask(low, high, lanes):
        rows = low + lax.broadcasted_iota(jnp.int32, (high - low, lanes), 0)
        return (rows >= first - start) & (rows < end - start)

    if window == TILE:
        return [(0, TILE, mask)]
    return [
        (0, ALIGN, mask),
        (ALIGN, window - TILE, None),
        (window - TILE, window, mask),
    ]


def key_rows_masked(values, start, first, end, fill):
    window, lanes = values.shape
    return jnp.concatenate(
        [
            values[low:high]
            if mask is None
            else jnp.where(mask(low, high, lanes), values[low:high], fill)
            for low, high, mask in window_parts(window, start, first, end)
        ],
        axis=0,
    )


def store_window(ref, cols, values, start, first, end):
    window, lanes = values.shape
    for low, high, mask in window_parts(window, start, first, end):
        at = pl.ds(pl.multiple_of(start + low, ALIGN), high - low)
        part = values[low:high]
        if mask is not None:
            part = jnp.where(mask(low, high, lanes), part, ref[at, cols].astype(F32))
        ref[at, cols] = part.astype(BF16)


def pair_columns(pair, base=0):
    return slice(base + pair * PAIR, base + (pair + 1) * PAIR)


DEPTH = 1


def run_staged(pairs, count, score, weigh, finish):
    units = [(pair, part) for pair in range(pairs) for part in range(count)]
    scored = {}
    for step in range(len(units) + DEPTH):
        if step < len(units):
            scored[step] = score(*units[step])
        if step >= DEPTH:
            pair, part = units[step - DEPTH]
            weigh(pair, part, scored.pop(step - DEPTH))
            if part == count - 1:
                finish(pair)


def split_pair(rows):
    lane = lax.broadcasted_iota(jnp.int32, rows.shape, 1)
    zero = jnp.zeros_like(rows)
    return jnp.concatenate(
        [jnp.where(lane < HEAD, rows, zero), jnp.where(lane < HEAD, zero, rows)], axis=0
    )


def merge_pair(columns):
    row = lax.broadcasted_iota(jnp.int32, (PAIR, TILE), 0)
    return jnp.where(row < HEAD, columns[:, :TILE], columns[:, TILE:]).T


def spread_mask():
    row = lax.broadcasted_iota(jnp.int32, (128 // RANK, 128), 0)
    return row == lax.broadcasted_iota(jnp.int32, (128 // RANK, 128), 1) // RANK


def prepare_kernel(tp_ref, factors_ref, wq_ref, wk_ref, wv_ref, wcat_ref, upq_ref, upv_ref):
    features, width = wq_ref.shape
    flat = features * RANK // 128
    steps = features // 128
    own = tp_ref[0] * (width // 128)
    group = 128 // RANK
    picked = spread_mask()
    lane = lax.broadcasted_iota(jnp.int32, (128, 128), 1)
    row = lax.broadcasted_iota(jnp.int32, (128, 128), 0)
    compact = jnp.zeros((features, 128), F32)
    for which, (w_ref, up_ref) in enumerate(((wq_ref, upq_ref), (wv_ref, upv_ref))):
        held = factors_ref[which * flat : (which + 1) * flat, :].reshape(flat, 1, 128)
        down = jnp.where(picked[None], jnp.broadcast_to(held, (flat, group, 128)), 0.0)
        down = down.reshape(features, 128).astype(BF16)
        base = (2 + which) * flat
        for step in range(width // 128):
            part = factors_ref[pl.ds(base + own + step, RANK, stride=steps), :]
            up_ref[:, step * 128 : (step + 1) * 128] = jnp.concatenate([part] * group).astype(
                BF16
            )
        scale = LOG2E / math.sqrt(HEAD) if which == 0 else 1.0
        combined = w_ref[...].astype(F32) + ADAPTER_SCALE * nn(down, up_ref[...])
        at = which * 2 * width
        wcat_ref[:, at : at + width] = (combined * scale).astype(BF16)
        choose = jnp.where(lane == which * RANK + row % RANK, 1.0, 0.0).astype(BF16)
        compact = compact + nn(down, choose)
    wcat_ref[:, width : 2 * width] = wk_ref[...]
    wcat_ref[:, 3 * width :] = compact.astype(BF16)


def prepare(tp, factors, wq, wk, wv):
    features, width = wq.shape
    return pl.pallas_call(
        prepare_kernel,
        out_shape=[
            shape_of((features, 3 * width + 128), BF16),
            shape_of((128, width), BF16),
            shape_of((128, width), BF16),
        ],
        in_specs=[SMEM] + [VMEM] * 4,
        out_specs=[VMEM] * 3,
        compiler_params=params(),
        cost_estimate=pl.CostEstimate(
            flops=4 * 128 * features * width, bytes_accessed=9 * features * width, transcendentals=0
        ),
        name="prepare",
    )(tp, factors, wq, wk, wv)


def forward_kernel(
    longest,
    tp_ref,
    lengths_ref,
    xown_ref,
    xoth_ref,
    wcat_ref,
    qkv_out,
    mid_out,
    keep_out,
    send_out,
    lse_ref,
    x_buf,
    qkv_buf,
    mid_buf,
    att_buf,
    vt_buf,
    p_buf,
    in_sem,
    out_sem,
):
    rows, width = xown_ref.shape
    half = rows // 2
    pairs = width // PAIR
    me = tp_ref[0]
    mine = pl.ds(pl.multiple_of(me * width, 128), width)
    theirs = pl.ds(pl.multiple_of((1 - me) * width, 128), width)
    copy = pltpu.make_async_copy
    block = min(512, rows)
    blocks = rows // block

    def loads(index):
        at = pl.ds(pl.multiple_of(index * block, block), block)
        return [
            copy(xown_ref.at[at], x_buf.at[at, mine], in_sem.at[0, index]),
            copy(xoth_ref.at[at], x_buf.at[at, theirs], in_sem.at[1, index]),
        ]

    def stores(index):
        at = pl.ds(pl.multiple_of(index * block, block), block)
        return [
            copy(qkv_buf.at[at], qkv_out.at[at], out_sem.at[0, index]),
            copy(mid_buf.at[at], mid_out.at[at], out_sem.at[1, index]),
        ]

    for index in range(blocks):
        start_all(loads(index))
    qkv_buf[rows:, :] = jnp.zeros((qkv_buf.shape[0] - rows, 3 * width), BF16)
    lse_ref[...] = jnp.full(lse_ref.shape, -MASKED, F32)

    @pl.loop(0, blocks)
    def _(index):
        at = pl.ds(pl.multiple_of(index * block, block), block)
        wait_all(loads(index))
        features = x_buf[at, :]
        for low in range(0, 3 * width, 256):
            high = min(low + 256, wcat_ref.shape[1])
            part = nn(features, wcat_ref[:, low:high]).astype(BF16)
            inner = min(high, 3 * width) - low
            qkv_buf[at, low : low + inner] = part[:, :inner]
            if inner < high - low:
                mid_buf[at, :] = part[:, inner:]
        start_all(stores(index))

    def visit(count, start, first, end, tile):
        window = count * TILE
        keys_at = pl.ds(start, window)

        def score(pair, part):
            if part == 0:
                vt_buf[pair, :, :window] = qkv_buf[keys_at, pair_columns(pair, 2 * width)].T
            low = pl.multiple_of(start + part * TILE, ALIGN)
            queries = split_pair(qkv_buf[pl.ds(low, TILE), pair_columns(pair)])
            return nt(qkv_buf[keys_at, pair_columns(pair, width)], queries)

        inverse = {}

        def weigh(pair, part, scores):
            low = start + part * TILE
            scores = key_rows_masked(scores, start, first, end, MASKED)
            top = jnp.max(scores, axis=0, keepdims=True)
            weights = jnp.exp2(scores - top)
            total = jnp.sum(weights, axis=0, keepdims=True)
            p_buf[pair, :window, part * 2 * TILE : (part + 1) * 2 * TILE] = weights.astype(BF16)
            inverse[pair, part] = 1.0 / total
            lane = lax.broadcasted_iota(jnp.int32, (1, 2 * TILE), 1)
            spot = low + jnp.where(lane < TILE, lane, lane - TILE)
            lse_ref[pair, pl.ds(tile + part, 1), :] = jnp.where(
                (spot >= first) & (spot < end), top + jnp.log2(total), -MASKED
            )

        def finish(pair):
            columns = nn(vt_buf[pair, :, :window], p_buf[pair, :window, : count * 2 * TILE])
            merged = [
                merge_pair(columns[:, part * 2 * TILE : (part + 1) * 2 * TILE] * inverse[pair, part])
                for part in range(count)
            ]
            store_window(
                att_buf, pair_columns(pair), jnp.concatenate(merged, axis=0), start, first, end
            )

        run_staged(pairs, count, score, weigh, finish)

    for_each_sentence(lengths_ref, longest, rows, rows, lambda index: None, visit)
    mine_rows = pl.ds(pl.multiple_of(me * half, half), half)
    their_rows = pl.ds(pl.multiple_of((1 - me) * half, half), half)
    last = start_all(
        [
            copy(att_buf.at[their_rows], send_out, out_sem.at[0, blocks]),
            copy(att_buf.at[mine_rows], keep_out, out_sem.at[1, blocks]),
        ]
    )
    for index in range(blocks):
        wait_all(stores(index))
    wait_all(last)


def tiles_at_most(rows, sentences):
    return -(-(rows + sentences * (ALIGN - 1 + TILE - 1)) // TILE)


def widest_window(longest):
    return -(-(longest + ALIGN - 1) // TILE) * TILE


def forward(tp, lengths, x_own, x_oth, wcat, longest):
    rows, width = x_own.shape
    half = rows // 2
    pairs = width // PAIR
    tiles = -(-tiles_at_most(rows, lengths.shape[0]) // 8) * 8
    padded = rows + TILE
    widest = widest_window(longest)
    blocks = rows // min(512, rows)
    return pl.pallas_call(
        functools.partial(forward_kernel, longest),
        out_shape=[
            shape_of((rows, 3 * width), BF16),
            shape_of((rows, 128), BF16),
            shape_of((half, width), BF16),
            shape_of((half, width), BF16),
            shape_of((pairs, tiles, 2 * TILE), F32),
        ],
        in_specs=[SMEM, SMEM, ANY, ANY, VMEM],
        out_specs=[ANY] * 4 + [VMEM],
        scratch_shapes=[
            pltpu.VMEM((rows, 2 * width), BF16),
            pltpu.VMEM((padded, 3 * width), BF16),
            pltpu.VMEM((rows, 128), BF16),
            pltpu.VMEM((padded, width), BF16),
            pltpu.VMEM((pairs, PAIR, widest), BF16),
            pltpu.VMEM((pairs, widest, 2 * widest), BF16),
            pltpu.SemaphoreType.DMA((2, blocks)),
            pltpu.SemaphoreType.DMA((2, blocks + 1)),
        ],
        compiler_params=params(),
        cost_estimate=pl.CostEstimate(
            flops=20 * rows * width * width, bytes_accessed=14 * rows * width, transcendentals=0
        ),
        name="forward",
    )(tp, lengths, x_own, x_oth, wcat)


def cdf_and_slope(upper):
    size = jnp.abs(upper)
    inner = 1.0 / (1.0 + (0.3275911 / math.sqrt(2.0)) * size)
    bell = jnp.exp2(upper * upper * (-0.5 * LOG2E))
    poly = 0.5 * 1.061405429
    for factor in (-1.453152027, 1.421413741, -0.284496736, 0.254829592):
        poly = poly * inner + 0.5 * factor
    tail = poly * inner * bell
    below = jnp.where(upper < 0.0, tail, 1.0 - tail)
    return below, below + upper * bell * (1.0 / math.sqrt(2.0 * math.pi))


def row_mean(values):
    return jnp.mean(values, axis=-1, keepdims=True)


def norm_pull(scale, normed, pulled):
    return scale * (pulled - row_mean(pulled) - normed * row_mean(pulled * normed))


def rows_kernel(
    tp_ref,
    keep_ref,
    recv_ref,
    xown_ref,
    xoth_ref,
    cotown_ref,
    cototh_ref,
    wout_own,
    wout_oth,
    wup_own,
    wup_oth,
    wdown_own,
    wdown_oth,
    gain1_ref,
    shift1_ref,
    gain2_ref,
    shift2_ref,
    enc_keep,
    enc_send,
    dres_keep,
    dres_send,
    datt_keep,
    datt_send,
    att_buf,
    x_buf,
    cot_buf,
    wout_buf,
    wup_buf,
    wdown_buf,
    normed_buf,
    low_buf,
    act_buf,
    slope_buf,
    outer_buf,
    enc_buf,
    datt_buf,
    in_sem,
    out_sem,
):
    half, width = keep_ref.shape
    units = wup_own.shape[1]
    me = tp_ref[0]
    mine = pl.ds(pl.multiple_of(me * width, 128), width)
    theirs = pl.ds(pl.multiple_of((1 - me) * width, 128), width)
    own_rows = pl.ds(pl.multiple_of(me * half, half), half)
    copy = pltpu.make_async_copy
    first = start_all(
        [
            copy(wout_own, wout_buf.at[pl.ds(0, width)], in_sem.at[2]),
            copy(wout_oth, wout_buf.at[pl.ds(width, width)], in_sem.at[3]),
            copy(keep_ref, att_buf.at[:, pl.ds(0, width)], in_sem.at[0]),
            copy(recv_ref, att_buf.at[:, pl.ds(width, width)], in_sem.at[1]),
            copy(xown_ref.at[own_rows], x_buf.at[:, mine], in_sem.at[4]),
            copy(xoth_ref.at[own_rows], x_buf.at[:, theirs], in_sem.at[5]),
        ]
    )
    up_loads = start_all(
        [
            copy(wup_own, wup_buf.at[:, pl.ds(0, units)], in_sem.at[6]),
            copy(wup_oth, wup_buf.at[:, pl.ds(units, units)], in_sem.at[7]),
        ]
    )
    down_loads = start_all(
        [
            copy(wdown_own, wdown_buf.at[pl.ds(0, units)], in_sem.at[8]),
            copy(wdown_oth, wdown_buf.at[pl.ds(units, units)], in_sem.at[9]),
        ]
    )
    cot_loads = start_all(
        [
            copy(cotown_ref.at[own_rows], cot_buf.at[:, mine], in_sem.at[10]),
            copy(cototh_ref, cot_buf.at[:, theirs], in_sem.at[11]),
        ]
    )
    gain1, shift1 = gain1_ref[...], shift1_ref[...]
    gain2, shift2 = gain2_ref[...], shift2_ref[...]
    block = min(512, half)
    blocks = half // block
    chunk = min(512, units)
    chunks = 2 * units // chunk
    scales = {}
    stores = []

    def rows_of(index):
        return slice(index * block, (index + 1) * block)

    def cols_of(part):
        return slice(part * chunk, (part + 1) * chunk)

    def mix(index):
        at = rows_of(index)
        outer_buf[at, :] = x_buf[at, :].astype(F32) + nn(att_buf[at, :], wout_buf[...])

    def first_norm(index):
        at = rows_of(index)
        resid = outer_buf[at, :]
        centered = resid - row_mean(resid)
        scale = lax.rsqrt(row_mean(centered * centered) + EPS_NORM)
        normed = centered * scale
        scales[index] = scale
        normed_buf[at, :] = normed
        low_buf[at, :] = (normed * gain1 + shift1).astype(BF16)

    def widen(index, part):
        at, cols = rows_of(index), cols_of(part)
        upper = nn(low_buf[at, :], wup_buf[:, cols])
        below, slope = cdf_and_slope(upper)
        act_buf[at, cols] = (upper * below).astype(BF16)
        slope_buf[at, cols] = slope.astype(BF16)

    def narrow(index):
        at = rows_of(index)
        outer_buf[at, :] = (
            normed_buf[at, :] * gain1 + shift1 + nn(act_buf[at, :], wdown_buf[...])
        )

    def second_norm(index):
        at = rows_of(index)
        outer = outer_buf[at, :]
        centered = outer - row_mean(outer)
        scale = lax.rsqrt(row_mean(centered * centered) + EPS_NORM)
        normed = centered * scale
        enc_buf[at, :] = (normed * gain2 + shift2).astype(BF16)
        d_outer = norm_pull(scale, normed, cot_buf[at, :].astype(F32) * gain2)
        outer_buf[at, :] = d_outer
        low_buf[at, :] = d_outer.astype(BF16)

    def widen_back(index, part):
        at, cols = rows_of(index), cols_of(part)
        d_act = nt(low_buf[at, :], wdown_buf[cols, :])
        act_buf[at, cols] = (d_act * slope_buf[at, cols].astype(F32)).astype(BF16)

    def narrow_back(index):
        at = rows_of(index)
        outer_buf[at, :] = outer_buf[at, :] + nt(act_buf[at, :], wup_buf[...])

    def first_norm_back(index):
        at = rows_of(index)
        d_res = norm_pull(scales[index], normed_buf[at, :], outer_buf[at, :] * gain1)
        outer_buf[at, :] = d_res
        low_buf[at, :] = d_res.astype(BF16)

    def unmix(index):
        at = rows_of(index)
        datt_buf[at, :] = nt(low_buf[at, :], wout_buf[...]).astype(BF16)
        stores.extend(
            start_all(
                [
                    copy(datt_buf.at[at, pl.ds(width, width)], datt_send.at[at], out_sem.at[0, index]),
                    copy(datt_buf.at[at, pl.ds(0, width)], datt_keep.at[at], out_sem.at[1, index]),
                ]
            )
        )

    def send_out(index):
        at = rows_of(index)
        stores.extend(
            start_all(
                [
                    copy(enc_buf.at[at, theirs], enc_send.at[at], out_sem.at[2, index]),
                    copy(enc_buf.at[at, mine], enc_keep.at[at], out_sem.at[3, index]),
                    copy(outer_buf.at[at, theirs], dres_send.at[at], out_sem.at[4, index]),
                    copy(outer_buf.at[at, mine], dres_keep.at[at], out_sem.at[5, index]),
                ]
            )
        )

    def staggered(work, beside):
        for part in range(chunks):
            work(part)
            if part == 0 and beside is not None:
                beside()

    wait_all(first)
    for index in range(blocks):
        mix(index)
        if index == 0:
            first_norm(0)
    wait_all(up_loads)
    for index in range(blocks):
        if index == 1:
            wait_all(down_loads)
            narrow(0)
        later = functools.partial(first_norm, index + 1) if index + 1 < blocks else None
        if index > 0:
            if index == 1:
                wait_all(cot_loads)
            earlier = functools.partial(second_norm, index - 1)
            both = [step for step in (later, earlier) if step is not None]
        else:
            both = [later] if later is not None else []
        staggered(functools.partial(widen, index), lambda both=both: [step() for step in both])
        if index > 0:
            narrow(index)
    if blocks == 1:
        wait_all(down_loads)
        wait_all(cot_loads)
        narrow(0)
        second_norm(0)
    for index in range(blocks):
        if index == 0:
            beside = functools.partial(second_norm, blocks - 1) if blocks > 1 else None
        else:
            beside = functools.partial(first_norm_back, index - 1)
        staggered(functools.partial(widen_back, index), beside)
        narrow_back(index)
        if index > 0:
            unmix(index - 1)
            send_out(index - 1)
    first_norm_back(blocks - 1)
    unmix(blocks - 1)
    send_out(blocks - 1)
    wait_all(stores)


def rows_step(tp, keep, recv, x_own, x_oth, cot_own, cot_oth, weights, norms):
    half, width = keep.shape
    units = weights[2].shape[1]
    blocks = half // min(512, half)
    return pl.pallas_call(
        rows_kernel,
        out_shape=[
            shape_of((half, width), BF16),
            shape_of((half, width), BF16),
            shape_of((half, width), F32),
            shape_of((half, width), F32),
            shape_of((half, width), BF16),
            shape_of((half, width), BF16),
        ],
        in_specs=[SMEM] + [ANY] * 12 + [VMEM] * 4,
        out_specs=[ANY] * 6,
        scratch_shapes=[
            pltpu.VMEM((half, 2 * width), BF16),
            pltpu.VMEM((half, 2 * width), BF16),
            pltpu.VMEM((half, 2 * width), BF16),
            pltpu.VMEM((2 * width, 2 * width), BF16),
            pltpu.VMEM((2 * width, 2 * units), BF16),
            pltpu.VMEM((2 * units, 2 * width), BF16),
            pltpu.VMEM((half, 2 * width), F32),
            pltpu.VMEM((half, 2 * width), BF16),
            pltpu.VMEM((half, 2 * units), BF16),
            pltpu.VMEM((half, 2 * units), BF16),
            pltpu.VMEM((half, 2 * width), F32),
            pltpu.VMEM((half, 2 * width), BF16),
            pltpu.VMEM((half, 2 * width), BF16),
            pltpu.SemaphoreType.DMA((12,)),
            pltpu.SemaphoreType.DMA((6, blocks)),
        ],
        compiler_params=params(),
        cost_estimate=pl.CostEstimate(
            flops=2 * half * (4 * width * (2 * width + 4 * units)),
            bytes_accessed=24 * half * width,
            transcendentals=0,
        ),
        name="rows_step",
    )(tp, keep, recv, x_own, x_oth, cot_own, cot_oth, *weights, *norms)


def backward_kernel(
    longest,
    tp_ref,
    lengths_ref,
    qkv_ref,
    dkeep_ref,
    drecv_ref,
    xown_ref,
    xoth_ref,
    mid_ref,
    lse_ref,
    upq_ref,
    upv_ref,
    d_out,
    grad_ref,
    qkv_buf,
    do_buf,
    x_buf,
    mid_buf,
    d_buf,
    kt_buf,
    q_split,
    do_split,
    p_buf,
    ds_buf,
    in_sem,
    late_sem,
    out_sem,
):
    half, width = dkeep_ref.shape
    rows = 2 * half
    pairs = width // PAIR
    me = tp_ref[0]
    mine = pl.ds(pl.multiple_of(me * width, 128), width)
    theirs = pl.ds(pl.multiple_of((1 - me) * width, 128), width)
    copy = pltpu.make_async_copy
    block = min(512, half)
    blocks = rows // block

    def block_rows(index):
        return pl.ds(pl.multiple_of(index * block, block), block)

    def d_load(ref, part, index):
        return copy(ref.at[block_rows(part)], do_buf.at[block_rows(index)], in_sem.at[1, index])

    def qkv_load(index):
        at = block_rows(index)
        return copy(qkv_ref.at[at], qkv_buf.at[at], in_sem.at[0, index])

    for index in range(blocks):
        qkv_load(index).start()
        if index < blocks // 2:
            d_load(dkeep_ref, index, me * (blocks // 2) + index).start()
            d_load(drecv_ref, index, (1 - me) * (blocks // 2) + index).start()
    late = start_all(
        [
            copy(xown_ref, x_buf.at[:, mine], late_sem.at[0]),
            copy(xoth_ref, x_buf.at[:, theirs], late_sem.at[1]),
            copy(mid_ref, mid_buf, late_sem.at[2]),
        ]
    )
    for buf in (qkv_buf, do_buf):
        buf[rows:, :] = jnp.zeros((buf.shape[0] - rows, buf.shape[1]), BF16)

    def await_chunk(index):
        qkv_load(index).wait()
        d_load(dkeep_ref, 0, index).wait()

    def visit(count, start, first, end, tile):
        window = count * TILE
        keys_at = pl.ds(start, window)

        def lanes(part):
            return slice(part * 2 * TILE, (part + 1) * 2 * TILE)

        def score(pair, part):
            keys = qkv_buf[keys_at, pair_columns(pair, width)]
            if part == 0:
                kt_buf[pair, :, :window] = keys.T
            at = pl.ds(pl.multiple_of(start + part * TILE, ALIGN), TILE)
            queries = split_pair(qkv_buf[at, pair_columns(pair)])
            d_rows = split_pair(do_buf[at, pair_columns(pair)])
            q_split[pair, lanes(part), :] = queries
            do_split[pair, lanes(part), :] = d_rows
            return (
                nt(keys, queries),
                nt(qkv_buf[keys_at, pair_columns(pair, 2 * width)], d_rows),
            )

        def weigh(pair, part, scored):
            scores, d_probs = scored
            probs = jnp.exp2(scores - lse_ref[pair, pl.ds(tile + part, 1), :])
            probs = key_rows_masked(probs, start, first, end, 0.0)
            product = probs * d_probs
            delta = jnp.sum(product, axis=0, keepdims=True)
            p_buf[pair, :window, lanes(part)] = probs.astype(BF16)
            ds_buf[pair, :window, lanes(part)] = (product - probs * delta).astype(BF16)

        def finish(pair):
            every = slice(0, count * 2 * TILE)
            d_scores = ds_buf[pair, :window, every]
            d_values = nn(p_buf[pair, :window, every], do_split[pair, every, :])
            d_keys = nn(d_scores, q_split[pair, every, :]) * LN2
            columns = nn(kt_buf[pair, :, :window], d_scores) * LN2
            d_queries = jnp.concatenate(
                [merge_pair(columns[:, lanes(part)]) for part in range(count)], axis=0
            )
            for base, values in enumerate((d_queries, d_keys, d_values)):
                store_window(d_buf, pair_columns(pair, base * width), values, start, first, end)

        run_staged(pairs, count, score, weigh, finish)

    for_each_sentence(lengths_ref, longest, rows, block, await_chunk, visit)
    store = start_all([copy(d_buf.at[pl.ds(0, rows)], d_out, out_sem.at[0])])
    wait_all(late)
    d_query = d_buf[:rows, :width]
    d_value = d_buf[:rows, 2 * width :]
    mid = mid_buf[...]
    picked = spread_mask()
    features = 2 * width
    flat = features * RANK // 128
    steps = features // 128
    natural = ADAPTER_SCALE / (math.sqrt(HEAD) * LN2)
    for which, (grads, up_ref, scale) in enumerate(
        ((d_query, upq_ref, natural), (d_value, upv_ref, ADAPTER_SCALE))
    ):
        d_mid = (nt(up_ref[...], grads) * scale).astype(BF16)
        down = nn(d_mid, x_buf[...]).T
        down = jnp.where(picked[None], down.reshape(flat, 128 // RANK, 128), 0.0)
        grad_ref[pl.ds(which * flat, flat), :] = jnp.sum(down, axis=1)
        up = tn(mid, grads)[which * RANK : (which + 1) * RANK] * scale
        base = (2 + which) * flat
        own = me * (width // 128)
        other = (1 - me) * (width // 128)
        for step in range(width // 128):
            part = up[:, step * 128 : (step + 1) * 128]
            grad_ref[pl.ds(base + own + step, RANK, stride=steps), :] = part
            grad_ref[pl.ds(base + other + step, RANK, stride=steps), :] = jnp.zeros_like(part)
    wait_all(store)


def backward(tp, lengths, qkv, d_keep, d_recv, x_own, x_oth, mid, lse, up_q, up_v, longest):
    half, width = d_keep.shape
    rows = 2 * half
    pairs = width // PAIR
    padded = rows + TILE
    widest = widest_window(longest)
    blocks = rows // min(512, half)
    return pl.pallas_call(
        functools.partial(backward_kernel, longest),
        out_shape=[
            shape_of((rows, 3 * width), BF16),
            shape_of((8 * width * RANK // 128, 128), F32),
        ],
        in_specs=[SMEM, SMEM] + [ANY] * 6 + [VMEM] * 3,
        out_specs=[ANY, VMEM],
        scratch_shapes=[
            pltpu.VMEM((padded, 3 * width), BF16),
            pltpu.VMEM((padded, width), BF16),
            pltpu.VMEM((rows, 2 * width), BF16),
            pltpu.VMEM((rows, 128), BF16),
            pltpu.VMEM((padded, 3 * width), BF16),
            pltpu.VMEM((pairs, PAIR, widest), BF16),
            pltpu.VMEM((pairs, 2 * widest, PAIR), BF16),
            pltpu.VMEM((pairs, 2 * widest, PAIR), BF16),
            pltpu.VMEM((pairs, widest, 2 * widest), BF16),
            pltpu.VMEM((pairs, widest, 2 * widest), BF16),
            pltpu.SemaphoreType.DMA((2, blocks)),
            pltpu.SemaphoreType.DMA((3,)),
            pltpu.SemaphoreType.DMA((1,)),
        ],
        compiler_params=params(),
        cost_estimate=pl.CostEstimate(
            flops=30 * rows * width * width, bytes_accessed=20 * rows * width, transcendentals=0
        ),
        name="backward",
    )(tp, lengths, qkv, d_keep, d_recv, x_own, x_oth, mid, lse, up_q, up_v)


def token_kernel(last, tp_ref, d_ref, wcat_ref, dres_ref, *refs):
    out_ref = refs[-1]
    width = out_ref.shape[1]
    blocks = pl.num_programs(0)
    own = pl.program_id(0) // (blocks // 2) == tp_ref[0]
    added = jnp.where(own, dres_ref[...], 0.0)
    if last:
        added = added + refs[0][...].astype(F32)
    out_ref[...] = (nt(d_ref[...], wcat_ref[:, : 3 * width]) + added).astype(out_ref.dtype)


def token_step(tp, d, wcat, dres, recv=None):
    rows = d.shape[0]
    half, width = dres.shape
    last = recv is not None
    block = min(512, half)
    halves = half // block

    def weights_at(index, tp_ref):
        return (tp_ref[0] if last else 1 - tp_ref[0], 0)

    def resid_at(index, tp_ref):
        return (jnp.clip(index - tp_ref[0] * halves, 0, halves - 1), 0)

    def rows_at(index, tp_ref):
        return (index, 0)

    return pl.pallas_call(
        functools.partial(token_kernel, last),
        grid_spec=pltpu.PrefetchScalarGridSpec(
            num_scalar_prefetch=1,
            grid=(2 * halves,),
            in_specs=[
                pl.BlockSpec((block, 3 * width), rows_at),
                pl.BlockSpec((width, wcat.shape[1]), weights_at),
                pl.BlockSpec((block, width), resid_at),
            ]
            + ([pl.BlockSpec((block, width), rows_at)] if last else []),
            out_specs=pl.BlockSpec((block, width), rows_at),
        ),
        out_shape=shape_of((rows, width), F32 if last else BF16),
        compiler_params=params(),
        cost_estimate=pl.CostEstimate(
            flops=6 * rows * width * width, bytes_accessed=12 * rows * width, transcendentals=0
        ),
        name="token_keep" if last else "token_send",
    )(*((tp, d, wcat, dres) + ((recv,) if last else ())))


def adam_update(gradient, moment_one, moment_two, weights, rates):
    first_new = BETA_ONE * moment_one + (1.0 - BETA_ONE) * gradient
    second_new = BETA_TWO * moment_two + (1.0 - BETA_TWO) * gradient * gradient
    update = first_new / BIAS_ONE / (jnp.sqrt(second_new / BIAS_TWO) + EPS_ADAM)
    return first_new, second_new, weights - rates * (update + DECAY_RATE * weights)


def summed_over_all(values, dp_size):
    values = values + swap(values)
    step = 1
    while step < dp_size:
        order = [(i, i ^ step) for i in range(dp_size)]
        values = values + lax.ppermute(values, "dp", order)
        step *= 2
    return values


def swap(values):
    return lax.ppermute(values, "tp", [(0, 1), (1, 0)])


def body(
    tokens,
    lengths,
    query_weight,
    w_key,
    value_weight,
    w_out,
    w_up,
    w_down,
    gain_attn,
    shift_attn,
    gain_ffn,
    shift_ffn,
    factors,
    first_moment,
    second_moment,
    cotangent,
):
    rows, width = tokens.shape
    features = 2 * width
    half = rows // 2
    longest = min(512, rows)
    me = lax.axis_index("tp")
    tp = me.astype(jnp.int32).reshape(1)
    dp_size = lax.axis_size("dp")
    other_rows = (1 - me) * half
    size_down = features * RANK
    own_lengths = lengths.reshape(-1)

    x_oth = swap(tokens)
    wcat, up_q, up_v = prepare(tp, factors.reshape(-1, 128), query_weight, w_key, value_weight)

    held = lax.optimization_barrier((x_oth, w_out, w_up, w_down, cotangent))
    x_oth = held[0]
    out_oth, up_oth, down_oth = swap(held[1]), swap(held[2]), swap(held[3])
    cot_oth = swap(lax.dynamic_slice_in_dim(held[4], other_rows, half, 0))
    share = first_moment.shape[0]
    moments = jnp.concatenate([first_moment, second_moment])
    moments = jnp.pad(moments, (0, GATHER_ROWS * 128 - 2 * share)).reshape(-1, 128)
    gathered = lax.all_gather(moments, ("dp", "tp"), axis=0, tiled=False)
    gathered = gathered.reshape(gathered.shape[0], -1)
    all_moments = gathered[:, : 2 * share].reshape(-1, 2, share)

    qkv, mid, att_keep, att_send, lse = forward(
        tp, own_lengths, tokens, x_oth, wcat, longest
    )
    att_recv = swap(att_send)
    norms = [part.reshape(1, features) for part in (gain_attn, shift_attn, gain_ffn, shift_ffn)]
    enc_keep, enc_send, dres_keep, dres_send, datt_keep, datt_send = rows_step(
        tp,
        att_keep,
        att_recv,
        tokens,
        x_oth,
        cotangent,
        cot_oth,
        (w_out, out_oth, w_up, up_oth, w_down, down_oth),
        norms,
    )
    datt_recv = swap(datt_send)
    enc_recv = swap(enc_send)
    encoded = jnp.where(
        me == 0,
        jnp.concatenate([enc_keep, enc_recv], axis=0),
        jnp.concatenate([enc_recv, enc_keep], axis=0),
    )
    d_all, grad_term = backward(
        tp,
        own_lengths,
        qkv,
        datt_keep,
        datt_recv,
        tokens,
        x_oth,
        mid,
        lse,
        up_q,
        up_v,
        longest,
    )
    total = summed_over_all(grad_term, dp_size)
    tok_recv = swap(token_step(tp, d_all, wcat, dres_send))
    d_tokens = token_step(tp, d_all, wcat, dres_keep, tok_recv)

    gradient = total.reshape(-1) * (1.0 / math.sqrt(rows * dp_size))
    place = jnp.arange(gradient.shape[0], dtype=jnp.int32)
    rates = jnp.where(place < 2 * size_down, RATE_DOWN, RATE_DOWN * RATE_RATIO)
    _, _, factors_new = adam_update(
        gradient,
        all_moments[:, 0].reshape(-1),
        all_moments[:, 1].reshape(-1),
        factors,
        rates,
    )
    share_start = lax.axis_index(("dp", "tp")) * share
    grad_share = lax.dynamic_slice_in_dim(gradient, share_start, share)
    first_new, second_new, _ = adam_update(grad_share, first_moment, second_moment, 0.0, 0.0)
    return encoded, d_tokens, grad_share, first_new, second_new, factors_new


def solution(mesh):
    placed = (
        P("dp", "tp"),
        P("dp", None),
        P(None, "tp"),
        P(None, "tp"),
        P(None, "tp"),
        P("tp", None),
        P(None, "tp"),
        P("tp", None),
        P(),
        P(),
        P(),
        P(),
        P(),
        P(("dp", "tp")),
        P(("dp", "tp")),
        P("dp", "tp"),
    )
    return jax.shard_map(
        body,
        mesh=mesh,
        in_specs=placed,
        out_specs=(
            P("dp", "tp"),
            P("dp", "tp"),
            P(("dp", "tp")),
            P(("dp", "tp")),
            P(("dp", "tp")),
            P(),
        ),
        check_vma=False,
    )
```

```python
import functools
import math

import jax
import jax.numpy as jnp
from jax import lax
from jax.experimental import pallas as pl
from jax.experimental.pallas import tpu as pltpu
from jax.sharding import PartitionSpec as P

HEAD = 64
RANK = 8
EPS_NORM = 1e-05
EPS_ADAM = 1e-08
BETA_ONE = 0.9
BETA_TWO = 0.999
BIAS_ONE = 1.0 - 0.9**10
BIAS_TWO = 1.0 - 0.999**10
RATE_DOWN = 0.002
RATE_RATIO = 16.0
DECAY_RATE = 0.01
ADAPTER_SCALE = 2.0
MASKED = -1e30
LOG2E = 1.4426950408889634
LN2 = 0.6931471805599453

TILE = 128
ALIGN = 16
PAIR = 2 * HEAD
BF16 = jnp.bfloat16
F32 = jnp.float32

ANY = pl.BlockSpec(memory_space=pl.ANY)
SMEM = pl.BlockSpec(memory_space=pltpu.SMEM)
VMEM = pl.BlockSpec(memory_space=pltpu.VMEM)


def shape_of(dims, kind):
    return jax.ShapeDtypeStruct(dims, kind)


def params(mib):
    return pltpu.CompilerParams(vmem_limit_bytes=mib * 1024 * 1024)


def nn(left, right):
    return lax.dot_general(left, right, (((1,), (0,)), ((), ())), preferred_element_type=F32)


def nt(left, right):
    return lax.dot_general(left, right, (((1,), (1,)), ((), ())), preferred_element_type=F32)


def tn(left, right):
    return lax.dot_general(left, right, (((0,), (0,)), ((), ())), preferred_element_type=F32)


def start_all(copies):
    for copy in copies:
        copy.start()
    return copies


def wait_all(copies):
    for copy in copies:
        copy.wait()


def for_each_sentence(lengths_ref, longest, rows, chunk, await_chunk, visit):
    def one(index, carry):
        first, tile, loaded = carry
        end = first + lengths_ref[index]
        start = pl.multiple_of((first // ALIGN) * ALIGN, ALIGN)
        steps = (end - start + (TILE - 1)) // TILE
        needed = jnp.minimum((start + steps * TILE + chunk - 1) // chunk, rows // chunk)
        loaded = await_chunks(loaded, needed)
        for count in range(1, (longest + ALIGN - 1 + TILE - 1) // TILE + 1):

            @pl.when(steps == count)
            def _():
                visit(count, start, first, end, tile)

        return end, tile + steps, loaded

    def await_chunks(loaded, needed):
        def one_chunk(index, _):
            await_chunk(index)
            return 0

        lax.fori_loop(loaded, needed, one_chunk, 0)
        return jnp.maximum(loaded, needed)

    zero = jnp.int32(0)
    carry = lax.fori_loop(0, lengths_ref.shape[0], one, (zero, zero, zero))
    await_chunks(carry[2], jnp.int32(rows // chunk))


def window_parts(window, start, first, end):
    def mask(low, high, lanes):
        rows = low + lax.broadcasted_iota(jnp.int32, (high - low, lanes), 0)
        return (rows >= first - start) & (rows < end - start)

    if window == TILE:
        return [(0, TILE, mask)]
    return [
        (0, ALIGN, mask),
        (ALIGN, window - TILE, None),
        (window - TILE, window, mask),
    ]


def key_rows_masked(values, start, first, end, fill):
    window, lanes = values.shape
    return jnp.concatenate(
        [
            values[low:high]
            if mask is None
            else jnp.where(mask(low, high, lanes), values[low:high], fill)
            for low, high, mask in window_parts(window, start, first, end)
        ],
        axis=0,
    )


def store_window(ref, cols, values, start, first, end):
    window, lanes = values.shape
    for low, high, mask in window_parts(window, start, first, end):
        at = pl.ds(pl.multiple_of(start + low, ALIGN), high - low)
        part = values[low:high]
        if mask is not None:
            part = jnp.where(mask(low, high, lanes), part, ref[at, cols].astype(F32))
        ref[at, cols] = part.astype(BF16)


def pair_columns(pair, base=0):
    return pl.ds(pl.multiple_of(base + pair * PAIR, PAIR), PAIR)


DEPTH = 1
TOGETHER = 4


def run_staged(pairs, count, score, weigh, finish):
    def work(units):
        scored = {}
        for step in range(len(units) + DEPTH):
            if step < len(units):
                scored[step] = score(*units[step])
            if step >= DEPTH:
                pair, part = units[step - DEPTH]
                weigh(pair, part, scored.pop(step - DEPTH))
                if part == count - 1:
                    finish(pair)

    if count <= TOGETHER:
        work([(pair, part) for pair in range(pairs) for part in range(count)])
    else:

        @pl.loop(0, pairs)
        def _(pair):
            work([(pair, part) for part in range(count)])


def split_pair(rows):
    lane = lax.broadcasted_iota(jnp.int32, rows.shape, 1)
    zero = jnp.zeros_like(rows)
    return jnp.concatenate(
        [jnp.where(lane < HEAD, rows, zero), jnp.where(lane < HEAD, zero, rows)], axis=0
    )


def merge_pair(columns):
    row = lax.broadcasted_iota(jnp.int32, (PAIR, TILE), 0)
    return jnp.where(row < HEAD, columns[:, :TILE], columns[:, TILE:]).T


def spread_mask():
    row = lax.broadcasted_iota(jnp.int32, (128 // RANK, 128), 0)
    return row == lax.broadcasted_iota(jnp.int32, (128 // RANK, 128), 1) // RANK


def prepare_kernel(tp_ref, factors_ref, wq_ref, wk_ref, wv_ref, wcat_ref, upq_ref, upv_ref):
    features, width = wq_ref.shape
    flat = features * RANK // 128
    steps = features // 128
    own = tp_ref[0] * (width // 128)
    group = 128 // RANK
    picked = spread_mask()
    lane = lax.broadcasted_iota(jnp.int32, (128, 128), 1)
    row = lax.broadcasted_iota(jnp.int32, (128, 128), 0)
    compact = jnp.zeros((features, 128), F32)
    for which, (w_ref, up_ref) in enumerate(((wq_ref, upq_ref), (wv_ref, upv_ref))):
        held = factors_ref[which * flat : (which + 1) * flat, :].reshape(flat, 1, 128)
        down = jnp.where(picked[None], jnp.broadcast_to(held, (flat, group, 128)), 0.0)
        down = down.reshape(features, 128).astype(BF16)
        base = (2 + which) * flat
        for step in range(width // 128):
            part = factors_ref[pl.ds(base + own + step, RANK, stride=steps), :]
            up_ref[:, step * 128 : (step + 1) * 128] = jnp.concatenate([part] * group).astype(
                BF16
            )
        scale = LOG2E / math.sqrt(HEAD) if which == 0 else 1.0
        combined = w_ref[...].astype(F32) + ADAPTER_SCALE * nn(down, up_ref[...])
        at = which * 2 * width
        wcat_ref[:, at : at + width] = (combined * scale).astype(BF16)
        choose = jnp.where(lane == which * RANK + row % RANK, 1.0, 0.0).astype(BF16)
        compact = compact + nn(down, choose)
    wcat_ref[:, width : 2 * width] = wk_ref[...]
    wcat_ref[:, 3 * width :] = compact.astype(BF16)


def prepare(tp, factors, wq, wk, wv):
    features, width = wq.shape
    return pl.pallas_call(
        prepare_kernel,
        out_shape=[
            shape_of((features, 3 * width + 128), BF16),
            shape_of((128, width), BF16),
            shape_of((128, width), BF16),
        ],
        in_specs=[SMEM] + [VMEM] * 4,
        out_specs=[VMEM] * 3,
        compiler_params=params(56),
        cost_estimate=pl.CostEstimate(
            flops=4 * 128 * features * width, bytes_accessed=9 * features * width, transcendentals=0
        ),
        name="prepare",
    )(tp, factors, wq, wk, wv)


def forward_kernel(
    longest,
    tp_ref,
    lengths_ref,
    xown_ref,
    xoth_ref,
    wcat_ref,
    qkv_out,
    mid_out,
    keep_out,
    send_out,
    lse_ref,
    x_buf,
    qkv_buf,
    mid_buf,
    att_buf,
    vt_buf,
    p_buf,
    in_sem,
    out_sem,
):
    rows, width = xown_ref.shape
    half = rows // 2
    pairs = width // PAIR
    me = tp_ref[0]
    mine = pl.ds(pl.multiple_of(me * width, 128), width)
    theirs = pl.ds(pl.multiple_of((1 - me) * width, 128), width)
    copy = pltpu.make_async_copy
    block = min(512, rows)
    blocks = rows // block

    def loads(index):
        at = pl.ds(pl.multiple_of(index * block, block), block)
        return [
            copy(xown_ref.at[at], x_buf.at[at, mine], in_sem.at[0, index]),
            copy(xoth_ref.at[at], x_buf.at[at, theirs], in_sem.at[1, index]),
        ]

    def stores(index):
        at = pl.ds(pl.multiple_of(index * block, block), block)
        return [
            copy(qkv_buf.at[at], qkv_out.at[at], out_sem.at[0, index]),
            copy(mid_buf.at[at], mid_out.at[at], out_sem.at[1, index]),
        ]

    for index in range(blocks):
        start_all(loads(index))
    qkv_buf[rows:, :] = jnp.zeros((qkv_buf.shape[0] - rows, 3 * width), BF16)
    lse_ref[...] = jnp.full(lse_ref.shape, -MASKED, F32)

    @pl.loop(0, blocks)
    def _(index):
        at = pl.ds(pl.multiple_of(index * block, block), block)
        wait_all(loads(index))
        features = x_buf[at, :]
        for low in range(0, 3 * width, 256):
            high = min(low + 256, wcat_ref.shape[1])
            part = nn(features, wcat_ref[:, low:high]).astype(BF16)
            inner = min(high, 3 * width) - low
            qkv_buf[at, low : low + inner] = part[:, :inner]
            if inner < high - low:
                mid_buf[at, :] = part[:, inner:]
        start_all(stores(index))

    def visit(count, start, first, end, tile):
        window = count * TILE
        keys_at = pl.ds(start, window)

        def score(pair, part):
            if part == 0:
                vt_buf[pair, :, :window] = qkv_buf[keys_at, pair_columns(pair, 2 * width)].T
            low = pl.multiple_of(start + part * TILE, ALIGN)
            queries = split_pair(qkv_buf[pl.ds(low, TILE), pair_columns(pair)])
            return nt(qkv_buf[keys_at, pair_columns(pair, width)], queries)

        inverse = {}

        def weigh(pair, part, scores):
            low = start + part * TILE
            scores = key_rows_masked(scores, start, first, end, MASKED)
            top = jnp.max(scores, axis=0, keepdims=True)
            weights = jnp.exp2(scores - top)
            total = jnp.sum(weights, axis=0, keepdims=True)
            p_buf[pair, :window, part * 2 * TILE : (part + 1) * 2 * TILE] = weights.astype(BF16)
            inverse[part if count > TOGETHER else (pair, part)] = 1.0 / total
            lane = lax.broadcasted_iota(jnp.int32, (1, 2 * TILE), 1)
            spot = low + jnp.where(lane < TILE, lane, lane - TILE)
            lse_ref[pair, pl.ds(tile + part, 1), :] = jnp.where(
                (spot >= first) & (spot < end), top + jnp.log2(total), -MASKED
            )

        def finish(pair):
            columns = nn(vt_buf[pair, :, :window], p_buf[pair, :window, : count * 2 * TILE])
            merged = [
                merge_pair(
                    columns[:, part * 2 * TILE : (part + 1) * 2 * TILE]
                    * inverse[part if count > TOGETHER else (pair, part)]
                )
                for part in range(count)
            ]
            store_window(
                att_buf, pair_columns(pair), jnp.concatenate(merged, axis=0), start, first, end
            )

        run_staged(pairs, count, score, weigh, finish)

    for_each_sentence(lengths_ref, longest, rows, rows, lambda index: None, visit)
    mine_rows = pl.ds(pl.multiple_of(me * half, half), half)
    their_rows = pl.ds(pl.multiple_of((1 - me) * half, half), half)
    last = start_all(
        [
            copy(att_buf.at[their_rows], send_out, out_sem.at[0, blocks]),
            copy(att_buf.at[mine_rows], keep_out, out_sem.at[1, blocks]),
        ]
    )
    for index in range(blocks):
        wait_all(stores(index))
    wait_all(last)


def tiles_at_most(rows, sentences):
    return -(-(rows + sentences * (ALIGN - 1 + TILE - 1)) // TILE)


def widest_window(longest):
    return -(-(longest + ALIGN - 1) // TILE) * TILE


def forward(tp, lengths, x_own, x_oth, wcat, longest):
    rows, width = x_own.shape
    half = rows // 2
    pairs = width // PAIR
    tiles = -(-tiles_at_most(rows, lengths.shape[0]) // 8) * 8
    padded = rows + TILE
    widest = widest_window(longest)
    blocks = rows // min(512, rows)
    return pl.pallas_call(
        functools.partial(forward_kernel, longest),
        out_shape=[
            shape_of((rows, 3 * width), BF16),
            shape_of((rows, 128), BF16),
            shape_of((half, width), BF16),
            shape_of((half, width), BF16),
            shape_of((pairs, tiles, 2 * TILE), F32),
        ],
        in_specs=[SMEM, SMEM, ANY, ANY, VMEM],
        out_specs=[ANY] * 4 + [VMEM],
        scratch_shapes=[
            pltpu.VMEM((rows, 2 * width), BF16),
            pltpu.VMEM((padded, 3 * width), BF16),
            pltpu.VMEM((rows, 128), BF16),
            pltpu.VMEM((padded, width), BF16),
            pltpu.VMEM((pairs, PAIR, widest), BF16),
            pltpu.VMEM((pairs, widest, 2 * widest), BF16),
            pltpu.SemaphoreType.DMA((2, blocks)),
            pltpu.SemaphoreType.DMA((2, blocks + 1)),
        ],
        compiler_params=params(56),
        cost_estimate=pl.CostEstimate(
            flops=20 * rows * width * width, bytes_accessed=14 * rows * width, transcendentals=0
        ),
        name="forward",
    )(tp, lengths, x_own, x_oth, wcat)


def cdf_and_slope(upper):
    below = 0.5 + 0.5 * lax.erf(upper * math.sqrt(0.5))
    bell = jnp.exp2(upper * upper * (-0.5 * LOG2E))
    return below, below + upper * bell * (1.0 / math.sqrt(2.0 * math.pi))


def row_mean(values):
    return jnp.mean(values, axis=-1, keepdims=True)


def norm_pull(scale, normed, pulled):
    return scale * (pulled - row_mean(pulled) - normed * row_mean(pulled * normed))


BAND = 64


def rows_kernel(
    tp_ref,
    keep_ref,
    recv_ref,
    xown_ref,
    xoth_ref,
    cotown_ref,
    cototh_ref,
    wout_own,
    wout_oth,
    wup_own,
    wup_oth,
    wdown_own,
    wdown_oth,
    gain1_ref,
    shift1_ref,
    gain2_ref,
    shift2_ref,
    enc_keep,
    enc_send,
    dres_out,
    datt_keep,
    datt_send,
    att_buf,
    x_buf,
    cot_buf,
    wout_buf,
    wup_buf,
    wdown_buf,
    normed_buf,
    scale_buf,
    low_buf,
    act_buf,
    slope_buf,
    fresh_buf,
    held_buf,
    fresh_low_buf,
    held_low_buf,
    outer_buf,
    dres_buf,
    enc_buf,
    datt_buf,
    in_sem,
    out_sem,
):
    half, width = keep_ref.shape
    units = wup_own.shape[1]
    me = tp_ref[0]
    mine = pl.ds(pl.multiple_of(me * width, 128), width)
    theirs = pl.ds(pl.multiple_of((1 - me) * width, 128), width)
    own_rows = pl.ds(pl.multiple_of(me * half, half), half)
    copy = pltpu.make_async_copy
    first = start_all(
        [
            copy(wout_own, wout_buf.at[pl.ds(0, width)], in_sem.at[2]),
            copy(wout_oth, wout_buf.at[pl.ds(width, width)], in_sem.at[3]),
            copy(keep_ref, att_buf.at[:, pl.ds(0, width)], in_sem.at[0]),
            copy(recv_ref, att_buf.at[:, pl.ds(width, width)], in_sem.at[1]),
            copy(xown_ref.at[own_rows], x_buf.at[:, mine], in_sem.at[4]),
            copy(xoth_ref.at[own_rows], x_buf.at[:, theirs], in_sem.at[5]),
        ]
    )
    up_loads = start_all(
        [
            copy(wup_own, wup_buf.at[:, pl.ds(0, units)], in_sem.at[6]),
            copy(wup_oth, wup_buf.at[:, pl.ds(units, units)], in_sem.at[7]),
        ]
    )
    down_loads = start_all(
        [
            copy(wdown_own, wdown_buf.at[pl.ds(0, units)], in_sem.at[8]),
            copy(wdown_oth, wdown_buf.at[pl.ds(units, units)], in_sem.at[9]),
        ]
    )
    cot_loads = start_all(
        [
            copy(cotown_ref.at[own_rows], cot_buf.at[:, mine], in_sem.at[10]),
            copy(cototh_ref, cot_buf.at[:, theirs], in_sem.at[11]),
        ]
    )
    gain1, shift1, gain2, shift2 = (
        ref[...].reshape(1, 2 * width) for ref in (gain1_ref, shift1_ref, gain2_ref, shift2_ref)
    )
    block = min(256, half)
    blocks = half // block
    chunk = min(768, units)
    chunks = 2 * units // chunk
    features = 2 * width
    strips = [slice(low, low + 256) for low in range(0, features, 256)]
    bands = [slice(low, low + BAND) for low in range(0, block, BAND)]

    def rows_of(index):
        return pl.ds(pl.multiple_of(index * block, block), block)

    def band_of(index, band):
        return pl.ds(pl.multiple_of(index * block + band.start, BAND), BAND)

    def cols_of(part):
        return pl.ds(pl.multiple_of(part * chunk, chunk), chunk)

    def mix(index, strip):
        at = rows_of(index)
        fresh_buf[:, strip] = x_buf[at, strip].astype(F32) + nn(att_buf[at, :], wout_buf[:, strip])

    def first_norm(index, band):
        at = band_of(index, band)
        resid = held_buf[band, :]
        centered = resid - row_mean(resid)
        scale = lax.rsqrt(row_mean(centered * centered) + EPS_NORM)
        normed = centered * scale
        scale_buf[at, :] = scale
        normed_buf[at, :] = normed
        low_buf[at, :] = (normed * gain1 + shift1).astype(BF16)

    def widen(part):
        cols = cols_of(part)
        upper = nn(low_buf[...], wup_buf[:, cols])
        below, slope = cdf_and_slope(upper)
        act_buf[:, cols] = (upper * below).astype(BF16)
        slope_buf[:, cols] = slope.astype(BF16)

    def narrow(index, strip):
        at = rows_of(index)
        hidden = normed_buf[at, strip] * gain1[:, strip] + shift1[:, strip]
        fresh_buf[:, strip] = hidden + nn(act_buf[at, :], wdown_buf[:, strip])

    def second_norm(index, band):
        at = band_of(index, band)
        outer = held_buf[band, :]
        centered = outer - row_mean(outer)
        scale = lax.rsqrt(row_mean(centered * centered) + EPS_NORM)
        normed = centered * scale
        enc_buf[at, :] = (normed * gain2 + shift2).astype(BF16)
        d_outer = norm_pull(scale, normed, cot_buf[at, :].astype(F32) * gain2)
        outer_buf[at, :] = d_outer
        low_buf[at, :] = d_outer.astype(BF16)

    def widen_back(part):
        cols = cols_of(part)
        d_act = nt(low_buf[...], wdown_buf[cols, :])
        act_buf[:, cols] = (d_act * slope_buf[:, cols].astype(F32)).astype(BF16)

    def narrow_back(index, strip):
        at = rows_of(index)
        fresh_buf[:, strip] = outer_buf[at, strip] + nt(act_buf[at, :], wup_buf[strip, :])

    def first_norm_back(index, band):
        at = band_of(index, band)
        d_res = norm_pull(scale_buf[at, :], normed_buf[at, :], held_buf[band, :] * gain1)
        dres_buf[at, :] = d_res
        fresh_low_buf[band, :] = d_res.astype(BF16)

    def unmix(index, strip):
        at = rows_of(index)
        datt_buf[at, strip] = nt(held_low_buf[...], wout_buf[strip, :]).astype(BF16)

    def hand_on():
        held_buf[...] = fresh_buf[...]

    def hand_on_low():
        held_low_buf[...] = fresh_low_buf[...]

    def step(at, low, high, product, norm, last=None):
        clamped = [
            jnp.maximum(at - place, 0) if not isinstance(at, int) else max(at - place, 0)
            for place in range(3)
        ]
        if low <= 1 < high:
            hand_on()
        if last is not None and low <= 2 < high:
            hand_on_low()
        for turn in range(max(len(strips), len(bands))):
            if low <= 0 < high and turn < len(strips):
                product(clamped[0], strips[turn])
            if last is not None and low <= 2 < high and turn < len(strips):
                last(clamped[2], strips[turn])
            if low <= 1 < high and turn < len(bands):
                norm(clamped[1], bands[turn])

    def staggered(product, norm, last=None):
        @pl.loop(0, blocks)
        def _(at):
            step(at, 0, 3, product, norm, last)

        step(blocks, 1, 3, product, norm, last)
        if last is not None:
            step(blocks + 1, 2, 3, product, norm, last)

    def stores(index):
        at = rows_of(index)
        return [
            copy(datt_buf.at[at, pl.ds(width, width)], datt_send.at[at], out_sem.at[0, index]),
            copy(datt_buf.at[at, pl.ds(0, width)], datt_keep.at[at], out_sem.at[1, index]),
            copy(dres_buf.at[at], dres_out.at[at], out_sem.at[2, index]),
        ]

    wait_all(first)
    staggered(mix, first_norm)
    wait_all(up_loads)
    pl.loop(0, chunks)(widen)
    wait_all(down_loads)
    wait_all(cot_loads)
    staggered(narrow, second_norm)
    enc_stores = start_all(
        [
            copy(enc_buf.at[:, theirs], enc_send, out_sem.at[3, 0]),
            copy(enc_buf.at[:, mine], enc_keep, out_sem.at[4, 0]),
        ]
    )
    pl.loop(0, chunks)(widen_back)
    staggered(narrow_back, first_norm_back, unmix)
    for index in range(blocks):
        start_all(stores(index))
    for index in range(blocks):
        wait_all(stores(index))
    wait_all(enc_stores)


def rows_step(tp, keep, recv, x_own, x_oth, cot_own, cot_oth, weights, norms):
    half, width = keep.shape
    units = weights[2].shape[1]
    block = min(256, half)
    return pl.pallas_call(
        rows_kernel,
        out_shape=[
            shape_of((half, width), BF16),
            shape_of((half, width), BF16),
            shape_of((half, 2 * width), F32),
            shape_of((half, width), BF16),
            shape_of((half, width), BF16),
        ],
        in_specs=[SMEM, ANY, VMEM] + [ANY] * 10 + [VMEM] * 4,
        out_specs=[ANY] * 5,
        scratch_shapes=[
            pltpu.VMEM((half, 2 * width), BF16),
            pltpu.VMEM((half, 2 * width), BF16),
            pltpu.VMEM((half, 2 * width), BF16),
            pltpu.VMEM((2 * width, 2 * width), BF16),
            pltpu.VMEM((2 * width, 2 * units), BF16),
            pltpu.VMEM((2 * units, 2 * width), BF16),
            pltpu.VMEM((half, 2 * width), F32),
            pltpu.VMEM((half, 1), F32),
            pltpu.VMEM((half, 2 * width), BF16),
            pltpu.VMEM((half, 2 * units), BF16),
            pltpu.VMEM((half, 2 * units), BF16),
            pltpu.VMEM((block, 2 * width), F32),
            pltpu.VMEM((block, 2 * width), F32),
            pltpu.VMEM((block, 2 * width), BF16),
            pltpu.VMEM((block, 2 * width), BF16),
            pltpu.VMEM((half, 2 * width), F32),
            pltpu.VMEM((half, 2 * width), F32),
            pltpu.VMEM((half, 2 * width), BF16),
            pltpu.VMEM((half, 2 * width), BF16),
            pltpu.SemaphoreType.DMA((12,)),
            pltpu.SemaphoreType.DMA((5, half // block)),
        ],
        compiler_params=params(56),
        cost_estimate=pl.CostEstimate(
            flops=2 * half * (4 * width * (2 * width + 4 * units)),
            bytes_accessed=24 * half * width,
            transcendentals=0,
        ),
        name="rows_step",
    )(tp, keep, recv, x_own, x_oth, cot_own, cot_oth, *weights, *norms)


def backward_kernel(
    longest,
    tp_ref,
    lengths_ref,
    qkv_ref,
    dkeep_ref,
    drecv_ref,
    xown_ref,
    xoth_ref,
    mid_ref,
    lse_ref,
    upq_ref,
    upv_ref,
    d_out,
    keep_ref,
    send_ref,
    qkv_buf,
    do_buf,
    x_buf,
    mid_buf,
    d_buf,
    kt_buf,
    q_split,
    do_split,
    p_buf,
    ds_buf,
    grad_ref,
    in_sem,
    late_sem,
    out_sem,
):
    half, width = dkeep_ref.shape
    rows = 2 * half
    pairs = width // PAIR
    me = tp_ref[0]
    mine = pl.ds(pl.multiple_of(me * width, 128), width)
    theirs = pl.ds(pl.multiple_of((1 - me) * width, 128), width)
    copy = pltpu.make_async_copy
    block = min(512, half)
    blocks = rows // block

    def block_rows(index):
        return pl.ds(pl.multiple_of(index * block, block), block)

    def d_load(ref, part, index):
        return copy(ref.at[block_rows(part)], do_buf.at[block_rows(index)], in_sem.at[1, index])

    def qkv_load(index):
        at = block_rows(index)
        return copy(qkv_ref.at[at], qkv_buf.at[at], in_sem.at[0, index])

    for index in range(blocks):
        qkv_load(index).start()
        if index < blocks // 2:
            d_load(dkeep_ref, index, me * (blocks // 2) + index).start()
            d_load(drecv_ref, index, (1 - me) * (blocks // 2) + index).start()
    late = start_all(
        [
            copy(xown_ref, x_buf.at[:, mine], late_sem.at[0]),
            copy(xoth_ref, x_buf.at[:, theirs], late_sem.at[1]),
            copy(mid_ref, mid_buf, late_sem.at[2]),
        ]
    )
    for buf in (qkv_buf, do_buf):
        buf[rows:, :] = jnp.zeros((buf.shape[0] - rows, buf.shape[1]), BF16)

    def await_chunk(index):
        qkv_load(index).wait()
        d_load(dkeep_ref, 0, index).wait()

    def visit(count, start, first, end, tile):
        window = count * TILE
        keys_at = pl.ds(start, window)

        def lanes(part):
            return slice(part * 2 * TILE, (part + 1) * 2 * TILE)

        def score(pair, part):
            keys = qkv_buf[keys_at, pair_columns(pair, width)]
            if part == 0:
                kt_buf[pair, :, :window] = keys.T
            at = pl.ds(pl.multiple_of(start + part * TILE, ALIGN), TILE)
            queries = split_pair(qkv_buf[at, pair_columns(pair)])
            d_rows = split_pair(do_buf[at, pair_columns(pair)])
            q_split[pair, lanes(part), :] = queries
            do_split[pair, lanes(part), :] = d_rows
            return (
                nt(keys, queries),
                nt(qkv_buf[keys_at, pair_columns(pair, 2 * width)], d_rows),
            )

        def weigh(pair, part, scored):
            scores, d_probs = scored
            probs = jnp.exp2(scores - lse_ref[pair, pl.ds(tile + part, 1), :])
            probs = key_rows_masked(probs, start, first, end, 0.0)
            product = probs * d_probs
            delta = jnp.sum(product, axis=0, keepdims=True)
            p_buf[pair, :window, lanes(part)] = probs.astype(BF16)
            ds_buf[pair, :window, lanes(part)] = (product - probs * delta).astype(BF16)

        def finish(pair):
            every = slice(0, count * 2 * TILE)
            d_scores = ds_buf[pair, :window, every]
            d_values = nn(p_buf[pair, :window, every], do_split[pair, every, :])
            d_keys = nn(d_scores, q_split[pair, every, :]) * LN2
            columns = nn(kt_buf[pair, :, :window], d_scores) * LN2
            d_queries = jnp.concatenate(
                [merge_pair(columns[:, lanes(part)]) for part in range(count)], axis=0
            )
            for base, values in enumerate((d_queries, d_keys, d_values)):
                store_window(d_buf, pair_columns(pair, base * width), values, start, first, end)

        run_staged(pairs, count, score, weigh, finish)

    for_each_sentence(lengths_ref, longest, rows, block, await_chunk, visit)
    store = start_all([copy(d_buf.at[pl.ds(0, rows)], d_out, out_sem.at[0])])
    wait_all(late)
    d_query = d_buf[:rows, :width]
    d_value = d_buf[:rows, 2 * width :]
    mid = mid_buf[...]
    picked = spread_mask()
    features = 2 * width
    flat = features * RANK // 128
    steps = features // 128
    natural = ADAPTER_SCALE / (math.sqrt(HEAD) * LN2)
    for which, (grads, up_ref, scale) in enumerate(
        ((d_query, upq_ref, natural), (d_value, upv_ref, ADAPTER_SCALE))
    ):
        d_mid = (nt(up_ref[...], grads) * scale).astype(BF16)
        down = nn(d_mid, x_buf[...]).T
        down = jnp.where(picked[None], down.reshape(flat, 128 // RANK, 128), 0.0)
        grad_ref[pl.ds(which * flat, flat), :] = jnp.sum(down, axis=1)
        up = tn(mid, grads)[which * RANK : (which + 1) * RANK] * scale
        base = (2 + which) * flat
        own = me * (width // 128)
        other = (1 - me) * (width // 128)
        for step in range(width // 128):
            part = up[:, step * 128 : (step + 1) * 128]
            grad_ref[pl.ds(base + own + step, RANK, stride=steps), :] = part
            grad_ref[pl.ds(base + other + step, RANK, stride=steps), :] = jnp.zeros_like(part)
    share = keep_ref.shape[0]
    keep_ref[...] = grad_ref[pl.ds(pl.multiple_of(me * share, 8), share), :]
    send_ref[...] = grad_ref[pl.ds(pl.multiple_of((1 - me) * share, 8), share), :]
    wait_all(store)


def backward(tp, lengths, qkv, d_keep, d_recv, x_own, x_oth, mid, lse, up_q, up_v, longest):
    half, width = d_keep.shape
    rows = 2 * half
    pairs = width // PAIR
    padded = rows + TILE
    widest = widest_window(longest)
    blocks = rows // min(512, half)
    return pl.pallas_call(
        functools.partial(backward_kernel, longest),
        out_shape=[
            shape_of((rows, 3 * width), BF16),
            shape_of((4 * width * RANK // 128, 128), F32),
            shape_of((4 * width * RANK // 128, 128), F32),
        ],
        in_specs=[SMEM, SMEM, ANY, ANY, VMEM] + [ANY] * 3 + [VMEM] * 3,
        out_specs=[ANY, VMEM, VMEM],
        scratch_shapes=[
            pltpu.VMEM((padded, 3 * width), BF16),
            pltpu.VMEM((padded, width), BF16),
            pltpu.VMEM((rows, 2 * width), BF16),
            pltpu.VMEM((rows, 128), BF16),
            pltpu.VMEM((padded, 3 * width), BF16),
            pltpu.VMEM((pairs, PAIR, widest), BF16),
            pltpu.VMEM((pairs, 2 * widest, PAIR), BF16),
            pltpu.VMEM((pairs, 2 * widest, PAIR), BF16),
            pltpu.VMEM((pairs, widest, 2 * widest), BF16),
            pltpu.VMEM((pairs, widest, 2 * widest), BF16),
            pltpu.VMEM((8 * width * RANK // 128, 128), F32),
            pltpu.SemaphoreType.DMA((2, blocks)),
            pltpu.SemaphoreType.DMA((3,)),
            pltpu.SemaphoreType.DMA((1,)),
        ],
        compiler_params=params(56),
        cost_estimate=pl.CostEstimate(
            flops=30 * rows * width * width, bytes_accessed=20 * rows * width, transcendentals=0
        ),
        name="backward",
    )(tp, lengths, qkv, d_keep, d_recv, x_own, x_oth, mid, lse, up_q, up_v)


def token_kernel(tp_ref, d_ref, wcat_ref, dres_ref, keep_ref, send_ref):
    width = keep_ref.shape[1]
    blocks = pl.num_programs(0)
    me = tp_ref[0]
    own = pl.program_id(0) // (blocks // 2) == me
    total = nt(d_ref[...], wcat_ref[:, : 3 * width]) + jnp.where(own, dres_ref[...], 0.0)
    low, high = total[:, :width], total[:, width:]
    keep_ref[...] = jnp.where(me == 0, low, high)
    send_ref[...] = jnp.where(me == 0, high, low).astype(BF16)


def token_step(tp, d, wcat, dres):
    rows = d.shape[0]
    half, features = dres.shape
    width = features // 2
    block = min(512, half)
    halves = half // block

    def resid_at(index, tp_ref):
        return (jnp.clip(index - tp_ref[0] * halves, 0, halves - 1), 0)

    def rows_at(index, tp_ref):
        return (index, 0)

    return pl.pallas_call(
        token_kernel,
        grid_spec=pltpu.PrefetchScalarGridSpec(
            num_scalar_prefetch=1,
            grid=(2 * halves,),
            in_specs=[
                pl.BlockSpec((block, 3 * width), rows_at),
                pl.BlockSpec(wcat.shape, lambda index, tp_ref: (0, 0)),
                pl.BlockSpec((block, features), resid_at),
            ],
            out_specs=[pl.BlockSpec((block, width), rows_at)] * 2,
        ),
        out_shape=[shape_of((rows, width), F32), shape_of((rows, width), BF16)],
        compiler_params=params(56),
        cost_estimate=pl.CostEstimate(
            flops=12 * rows * width * width, bytes_accessed=14 * rows * width, transcendentals=0
        ),
        name="token_step",
    )(tp, d, wcat, dres)


def adam_update(gradient, moment_one, moment_two, weights, rates):
    first_new = BETA_ONE * moment_one + (1.0 - BETA_ONE) * gradient
    second_new = BETA_TWO * moment_two + (1.0 - BETA_TWO) * gradient * gradient
    update = first_new / BIAS_ONE / (jnp.sqrt(second_new / BIAS_TWO) + EPS_ADAM)
    return first_new, second_new, weights - rates * (update + DECAY_RATE * weights)


def exchange_groups(size):
    step = 1
    while step < size:
        if step * 2 < size:
            yield step, [step, 2 * step, 3 * step]
            step *= 4
        else:
            yield step, [step]
            step *= 2


def partners(values, size, offsets):
    return [
        lax.ppermute(values, "dp", [(i, i ^ offset) for i in range(size)]) for offset in offsets
    ]


def joined(total, moments, others, index):
    rows = total.shape[0]
    sums = [other[:rows] for other in others]
    parts = [moments] + [other[rows:] for other in others]
    if len(sums) == 3:
        total = (total + sums[0]) + (sums[1] + sums[2])
    else:
        total = total + sums[0]
    count = len(parts)
    ordered = [
        functools.reduce(
            lambda held, offset: jnp.where(index == offset, parts[spot ^ offset], held),
            range(1, count),
            parts[spot],
        )
        for spot in range(count)
    ]
    return total, jnp.concatenate(ordered, axis=0)


def in_order(mine, other, me):
    return jnp.where(
        me == 0, jnp.concatenate([mine, other], axis=0), jnp.concatenate([other, mine], axis=0)
    )


def tied(*values):
    return lax.optimization_barrier(values)


def swap(values):
    return lax.ppermute(values, "tp", [(0, 1), (1, 0)])


def body(
    tokens,
    lengths,
    query_weight,
    w_key,
    value_weight,
    w_out,
    w_up,
    w_down,
    gain_attn,
    shift_attn,
    gain_ffn,
    shift_ffn,
    factors,
    first_moment,
    second_moment,
    cotangent,
):
    rows, width = tokens.shape
    features = 2 * width
    half = rows // 2
    longest = min(512, rows)
    me = lax.axis_index("tp")
    tp = me.astype(jnp.int32).reshape(1)
    dp_size = lax.axis_size("dp")
    other_rows = (1 - me) * half
    size_down = features * RANK
    own_lengths = lengths.reshape(-1)

    share = first_moment.shape[0]
    share_rows = -(-2 * share // 128)

    x_oth = swap(tokens)
    cot_oth = swap(lax.dynamic_slice_in_dim(cotangent, other_rows, half, 0))
    out_oth = swap(w_out)
    wcat, up_q, up_v = prepare(tp, factors.reshape(-1, 128), query_weight, w_key, value_weight)
    x_oth, cot_oth, out_oth, wcat, w_up_late, w_down_late = tied(
        x_oth, cot_oth, out_oth, wcat, w_up, w_down
    )
    up_oth, down_oth = swap(w_up_late), swap(w_down_late)

    qkv, mid, att_keep, att_send, lse = forward(
        tp, own_lengths, tokens, x_oth, wcat, longest
    )
    att_recv = swap(att_send)
    moments = jnp.concatenate([first_moment, second_moment])
    moments = jnp.pad(moments, (0, share_rows * 128 - 2 * share)).reshape(share_rows, 128)
    att_recv, moments = tied(att_recv, moments)
    enc_keep, enc_send, dres, datt_keep, datt_send = rows_step(
        tp,
        att_keep,
        att_recv,
        tokens,
        x_oth,
        cotangent,
        cot_oth,
        (w_out, out_oth, w_up, up_oth, w_down, down_oth),
        (gain_attn, shift_attn, gain_ffn, shift_ffn),
    )
    datt_recv = swap(datt_send)
    enc_recv = swap(enc_send)
    d_all, grad_keep, grad_send = backward(
        tp,
        own_lengths,
        qkv,
        datt_keep,
        datt_recv,
        tokens,
        x_oth,
        mid,
        lse,
        up_q,
        up_v,
        longest,
    )
    total = grad_keep + swap(grad_send)
    tok_keep, tok_send = token_step(tp, d_all, wcat, dres)
    place = lax.axis_index("dp")
    for step, offsets in exchange_groups(dp_size):
        others = partners(jnp.concatenate([total, moments], axis=0), dp_size, offsets)
        if step > 1:
            if step == 4:
                others, encoded, d_tokens = tied(others, encoded, d_tokens)
        else:
            others, tok_send = tied(others, tok_send)
            tok_recv = swap(tok_send)
            encoded = in_order(enc_keep, enc_recv, me)
            d_tokens = tok_keep + tok_recv.astype(F32)
        total, moments = joined(total, moments, others, (place // step) % (len(offsets) + 1))
    mine = jnp.concatenate([total, moments], axis=0)
    other = swap(mine)
    half_rows = total.shape[0]
    total = in_order(mine[:half_rows], other[:half_rows], me)
    moments = jnp.where(
        me == 0, jnp.stack([mine, other]), jnp.stack([other, mine])
    )[:, half_rows:].reshape(2, dp_size, -1)[:, :, : 2 * share]
    moments = jnp.swapaxes(moments, 0, 1).reshape(2 * dp_size, 2, share)

    gradient = total.reshape(-1) * (1.0 / math.sqrt(rows * dp_size))
    place = jnp.arange(gradient.shape[0], dtype=jnp.int32)
    rates = jnp.where(place < 2 * size_down, RATE_DOWN, RATE_DOWN * RATE_RATIO)
    _, _, factors_new = adam_update(
        gradient, moments[:, 0].reshape(-1), moments[:, 1].reshape(-1), factors, rates
    )
    share_start = lax.axis_index(("dp", "tp")) * share
    grad_share = lax.dynamic_slice_in_dim(gradient, share_start, share)
    first_new, second_new, _ = adam_update(grad_share, first_moment, second_moment, 0.0, 0.0)
    return encoded, d_tokens, grad_share, first_new, second_new, factors_new


def solution(mesh):
    placed = (
        P("dp", "tp"),
        P("dp", None),
        P(None, "tp"),
        P(None, "tp"),
        P(None, "tp"),
        P("tp", None),
        P(None, "tp"),
        P("tp", None),
        P(),
        P(),
        P(),
        P(),
        P(),
        P(("dp", "tp")),
        P(("dp", "tp")),
        P("dp", "tp"),
    )
    return jax.shard_map(
        body,
        mesh=mesh,
        in_specs=placed,
        out_specs=(
            P("dp", "tp"),
            P("dp", "tp"),
            P(("dp", "tp")),
            P(("dp", "tp")),
            P(("dp", "tp")),
            P(),
        ),
        check_vma=False,
    )
```

```python
import functools
import math

import jax
import jax.numpy as jnp
from jax import lax
from jax.experimental import pallas as pl
from jax.experimental.pallas import tpu as pltpu
from jax.sharding import PartitionSpec as P

HEAD = 64
RANK = 8
EPS_NORM = 1e-05
EPS_ADAM = 1e-08
BETA_ONE = 0.9
BETA_TWO = 0.999
BIAS_ONE = 1.0 - 0.9**10
BIAS_TWO = 1.0 - 0.999**10
RATE_DOWN = 0.002
RATE_RATIO = 16.0
DECAY_RATE = 0.01
ADAPTER_SCALE = 2.0
MASKED = -1e30
LOG2E = 1.4426950408889634
LN2 = 0.6931471805599453

TILE = 128
ALIGN = 16
PAIR = 2 * HEAD
BF16 = jnp.bfloat16
F32 = jnp.float32

ANY = pl.BlockSpec(memory_space=pl.ANY)
SMEM = pl.BlockSpec(memory_space=pltpu.SMEM)
VMEM = pl.BlockSpec(memory_space=pltpu.VMEM)


def shape_of(dims, kind):
    return jax.ShapeDtypeStruct(dims, kind)


def params(mib):
    return pltpu.CompilerParams(vmem_limit_bytes=mib * 1024 * 1024)


def nn(left, right):
    return lax.dot_general(left, right, (((1,), (0,)), ((), ())), preferred_element_type=F32)


def nt(left, right):
    return lax.dot_general(left, right, (((1,), (1,)), ((), ())), preferred_element_type=F32)


def tn(left, right):
    return lax.dot_general(left, right, (((0,), (0,)), ((), ())), preferred_element_type=F32)


def start_all(copies):
    for copy in copies:
        copy.start()
    return copies


def wait_all(copies):
    for copy in copies:
        copy.wait()


def for_each_sentence(lengths_ref, longest, rows, chunk, await_chunk, visit):
    def one(index, carry):
        first, tile, loaded = carry
        end = first + lengths_ref[index]
        start = pl.multiple_of((first // ALIGN) * ALIGN, ALIGN)
        steps = (end - start + (TILE - 1)) // TILE
        needed = jnp.minimum((start + steps * TILE + chunk - 1) // chunk, rows // chunk)
        loaded = await_chunks(loaded, needed)
        for count in range(1, (longest + ALIGN - 1 + TILE - 1) // TILE + 1):

            @pl.when(steps == count)
            def _():
                visit(count, start, first, end, tile)

        return end, tile + steps, loaded

    def await_chunks(loaded, needed):
        def one_chunk(index, _):
            await_chunk(index)
            return 0

        lax.fori_loop(loaded, needed, one_chunk, 0)
        return jnp.maximum(loaded, needed)

    zero = jnp.int32(0)
    carry = lax.fori_loop(0, lengths_ref.shape[0], one, (zero, zero, zero))
    await_chunks(carry[2], jnp.int32(rows // chunk))


def window_parts(window, start, first, end):
    def mask(low, high, lanes):
        rows = low + lax.broadcasted_iota(jnp.int32, (high - low, lanes), 0)
        return (rows >= first - start) & (rows < end - start)

    if window == TILE:
        return [(0, TILE, mask)]
    return [
        (0, ALIGN, mask),
        (ALIGN, window - TILE, None),
        (window - TILE, window, mask),
    ]


def key_rows_masked(values, start, first, end, fill):
    window, lanes = values.shape
    return jnp.concatenate(
        [
            values[low:high]
            if mask is None
            else jnp.where(mask(low, high, lanes), values[low:high], fill)
            for low, high, mask in window_parts(window, start, first, end)
        ],
        axis=0,
    )


def store_window(ref, cols, values, start, first, end):
    window, lanes = values.shape
    for low, high, mask in window_parts(window, start, first, end):
        at = pl.ds(pl.multiple_of(start + low, ALIGN), high - low)
        part = values[low:high]
        if mask is not None:
            part = jnp.where(mask(low, high, lanes), part, ref[at, cols].astype(F32))
        ref[at, cols] = part.astype(BF16)


def pair_columns(pair, base=0):
    return pl.ds(pl.multiple_of(base + pair * PAIR, PAIR), PAIR)


DEPTH = 1
TOGETHER = 4


def run_staged(pairs, count, score, weigh, finish):
    def work(units):
        scored = {}
        for step in range(len(units) + DEPTH):
            if step < len(units):
                scored[step] = score(*units[step])
            if step >= DEPTH:
                pair, part = units[step - DEPTH]
                weigh(pair, part, scored.pop(step - DEPTH))
                if part == count - 1:
                    finish(pair)

    if count <= TOGETHER:
        work([(pair, part) for pair in range(pairs) for part in range(count)])
    else:

        @pl.loop(0, pairs)
        def _(pair):
            work([(pair, part) for part in range(count)])


def split_pair(rows):
    lane = lax.broadcasted_iota(jnp.int32, rows.shape, 1)
    zero = jnp.zeros_like(rows)
    return jnp.concatenate(
        [jnp.where(lane < HEAD, rows, zero), jnp.where(lane < HEAD, zero, rows)], axis=0
    )


def merge_pair(columns):
    row = lax.broadcasted_iota(jnp.int32, (PAIR, TILE), 0)
    return jnp.where(row < HEAD, columns[:, :TILE], columns[:, TILE:]).T


def spread_mask():
    row = lax.broadcasted_iota(jnp.int32, (128 // RANK, 128), 0)
    return row == lax.broadcasted_iota(jnp.int32, (128 // RANK, 128), 1) // RANK


def prepare_kernel(tp_ref, factors_ref, wq_ref, wk_ref, wv_ref, wcat_ref, upq_ref, upv_ref):
    features, width = wq_ref.shape
    flat = features * RANK // 128
    steps = features // 128
    own = tp_ref[0] * (width // 128)
    group = 128 // RANK
    picked = spread_mask()
    lane = lax.broadcasted_iota(jnp.int32, (128, 128), 1)
    row = lax.broadcasted_iota(jnp.int32, (128, 128), 0)
    compact = jnp.zeros((features, 128), F32)
    for which, (w_ref, up_ref) in enumerate(((wq_ref, upq_ref), (wv_ref, upv_ref))):
        held = factors_ref[which * flat : (which + 1) * flat, :].reshape(flat, 1, 128)
        down = jnp.where(picked[None], jnp.broadcast_to(held, (flat, group, 128)), 0.0)
        down = down.reshape(features, 128).astype(BF16)
        base = (2 + which) * flat
        for step in range(width // 128):
            part = factors_ref[pl.ds(base + own + step, RANK, stride=steps), :]
            up_ref[:, step * 128 : (step + 1) * 128] = jnp.concatenate([part] * group).astype(
                BF16
            )
        scale = LOG2E / math.sqrt(HEAD) if which == 0 else 1.0
        combined = w_ref[...].astype(F32) + ADAPTER_SCALE * nn(down, up_ref[...])
        at = which * 2 * width
        wcat_ref[:, at : at + width] = (combined * scale).astype(BF16)
        choose = jnp.where(lane == which * RANK + row % RANK, 1.0, 0.0).astype(BF16)
        compact = compact + nn(down, choose)
    wcat_ref[:, width : 2 * width] = wk_ref[...]
    wcat_ref[:, 3 * width :] = compact.astype(BF16)


def prepare(tp, factors, wq, wk, wv):
    features, width = wq.shape
    return pl.pallas_call(
        prepare_kernel,
        out_shape=[
            shape_of((features, 3 * width + 128), BF16),
            shape_of((128, width), BF16),
            shape_of((128, width), BF16),
        ],
        in_specs=[SMEM] + [VMEM] * 4,
        out_specs=[VMEM] * 3,
        compiler_params=params(56),
        cost_estimate=pl.CostEstimate(
            flops=4 * 128 * features * width, bytes_accessed=9 * features * width, transcendentals=0
        ),
        name="prepare",
    )(tp, factors, wq, wk, wv)


def forward_kernel(
    longest,
    tp_ref,
    lengths_ref,
    xown_ref,
    xoth_ref,
    wcat_ref,
    qkv_out,
    mid_out,
    keep_out,
    send_out,
    lse_ref,
    x_buf,
    qkv_buf,
    mid_buf,
    att_buf,
    vt_buf,
    p_buf,
    in_sem,
    out_sem,
):
    rows, width = xown_ref.shape
    half = rows // 2
    pairs = width // PAIR
    me = tp_ref[0]
    mine = pl.ds(pl.multiple_of(me * width, 128), width)
    theirs = pl.ds(pl.multiple_of((1 - me) * width, 128), width)
    copy = pltpu.make_async_copy
    block = min(512, rows)
    blocks = rows // block

    def loads(index):
        at = pl.ds(pl.multiple_of(index * block, block), block)
        return [
            copy(xown_ref.at[at], x_buf.at[at, mine], in_sem.at[0, index]),
            copy(xoth_ref.at[at], x_buf.at[at, theirs], in_sem.at[1, index]),
        ]

    def stores(index):
        at = pl.ds(pl.multiple_of(index * block, block), block)
        return [
            copy(qkv_buf.at[at], qkv_out.at[at], out_sem.at[0, index]),
            copy(mid_buf.at[at], mid_out.at[at], out_sem.at[1, index]),
        ]

    for index in range(blocks):
        start_all(loads(index))
    qkv_buf[rows:, :] = jnp.zeros((qkv_buf.shape[0] - rows, 3 * width), BF16)
    lse_ref[...] = jnp.full(lse_ref.shape, -MASKED, F32)

    @pl.loop(0, blocks)
    def _(index):
        at = pl.ds(pl.multiple_of(index * block, block), block)
        wait_all(loads(index))
        features = x_buf[at, :]
        for low in range(0, 3 * width, 256):
            high = min(low + 256, wcat_ref.shape[1])
            part = nn(features, wcat_ref[:, low:high]).astype(BF16)
            inner = min(high, 3 * width) - low
            qkv_buf[at, low : low + inner] = part[:, :inner]
            if inner < high - low:
                mid_buf[at, :] = part[:, inner:]
        start_all(stores(index))

    def visit(count, start, first, end, tile):
        window = count * TILE
        keys_at = pl.ds(start, window)

        def score(pair, part):
            if part == 0:
                vt_buf[pair, :, :window] = qkv_buf[keys_at, pair_columns(pair, 2 * width)].T
            low = pl.multiple_of(start + part * TILE, ALIGN)
            queries = split_pair(qkv_buf[pl.ds(low, TILE), pair_columns(pair)])
            return nt(qkv_buf[keys_at, pair_columns(pair, width)], queries)

        inverse = {}

        def weigh(pair, part, scores):
            low = start + part * TILE
            scores = key_rows_masked(scores, start, first, end, MASKED)
            top = jnp.max(scores, axis=0, keepdims=True)
            weights = jnp.exp2(scores - top)
            total = jnp.sum(weights, axis=0, keepdims=True)
            p_buf[pair, :window, part * 2 * TILE : (part + 1) * 2 * TILE] = weights.astype(BF16)
            inverse[part if count > TOGETHER else (pair, part)] = 1.0 / total
            lane = lax.broadcasted_iota(jnp.int32, (1, 2 * TILE), 1)
            spot = low + jnp.where(lane < TILE, lane, lane - TILE)
            lse_ref[pair, pl.ds(tile + part, 1), :] = jnp.where(
                (spot >= first) & (spot < end), top + jnp.log2(total), -MASKED
            )

        def finish(pair):
            columns = nn(vt_buf[pair, :, :window], p_buf[pair, :window, : count * 2 * TILE])
            merged = [
                merge_pair(
                    columns[:, part * 2 * TILE : (part + 1) * 2 * TILE]
                    * inverse[part if count > TOGETHER else (pair, part)]
                )
                for part in range(count)
            ]
            store_window(
                att_buf, pair_columns(pair), jnp.concatenate(merged, axis=0), start, first, end
            )

        run_staged(pairs, count, score, weigh, finish)

    for_each_sentence(lengths_ref, longest, rows, rows, lambda index: None, visit)
    mine_rows = pl.ds(pl.multiple_of(me * half, half), half)
    their_rows = pl.ds(pl.multiple_of((1 - me) * half, half), half)
    last = start_all(
        [
            copy(att_buf.at[their_rows], send_out, out_sem.at[0, blocks]),
            copy(att_buf.at[mine_rows], keep_out, out_sem.at[1, blocks]),
        ]
    )
    for index in range(blocks):
        wait_all(stores(index))
    wait_all(last)


def tiles_at_most(rows, sentences):
    return -(-(rows + sentences * (ALIGN - 1 + TILE - 1)) // TILE)


def widest_window(longest):
    return -(-(longest + ALIGN - 1) // TILE) * TILE


def forward(tp, lengths, x_own, x_oth, wcat, longest):
    rows, width = x_own.shape
    half = rows // 2
    pairs = width // PAIR
    tiles = -(-tiles_at_most(rows, lengths.shape[0]) // 8) * 8
    padded = rows + TILE
    widest = widest_window(longest)
    blocks = rows // min(512, rows)
    return pl.pallas_call(
        functools.partial(forward_kernel, longest),
        out_shape=[
            shape_of((rows, 3 * width), BF16),
            shape_of((rows, 128), BF16),
            shape_of((half, width), BF16),
            pltpu.VMEM((half, width), BF16),
            shape_of((pairs, tiles, 2 * TILE), F32),
        ],
        in_specs=[SMEM, SMEM, ANY, VMEM, VMEM],
        out_specs=[ANY] * 3 + [VMEM] * 2,
        scratch_shapes=[
            pltpu.VMEM((rows, 2 * width), BF16),
            pltpu.VMEM((padded, 3 * width), BF16),
            pltpu.VMEM((rows, 128), BF16),
            pltpu.VMEM((padded, width), BF16),
            pltpu.VMEM((pairs, PAIR, widest), BF16),
            pltpu.VMEM((pairs, widest, 2 * widest), BF16),
            pltpu.SemaphoreType.DMA((2, blocks)),
            pltpu.SemaphoreType.DMA((2, blocks + 1)),
        ],
        compiler_params=params(56),
        cost_estimate=pl.CostEstimate(
            flops=20 * rows * width * width, bytes_accessed=14 * rows * width, transcendentals=0
        ),
        name="forward",
    )(tp, lengths, x_own, x_oth, wcat)


def cdf_and_slope(upper):
    below = 0.5 + 0.5 * lax.erf(upper * math.sqrt(0.5))
    bell = jnp.exp2(upper * upper * (-0.5 * LOG2E))
    return below, below + upper * bell * (1.0 / math.sqrt(2.0 * math.pi))


def row_mean(values):
    return jnp.mean(values, axis=-1, keepdims=True)


def norm_pull(scale, normed, pulled):
    return scale * (pulled - row_mean(pulled) - normed * row_mean(pulled * normed))


BAND = 64


def rows_kernel(
    tp_ref,
    keep_ref,
    recv_ref,
    xown_ref,
    xoth_ref,
    cotown_ref,
    cototh_ref,
    wout_own,
    wout_oth,
    wup_own,
    wup_oth,
    wdown_own,
    wdown_oth,
    gain1_ref,
    shift1_ref,
    gain2_ref,
    shift2_ref,
    enc_out,
    enc_send,
    dres_out,
    datt_keep,
    datt_send,
    att_buf,
    x_buf,
    cot_buf,
    wout_buf,
    wup_buf,
    wdown_buf,
    normed_buf,
    scale_buf,
    low_buf,
    act_buf,
    slope_buf,
    fresh_buf,
    held_buf,
    fresh_low_buf,
    held_low_buf,
    outer_buf,
    dres_buf,
    enc_buf,
    datt_buf,
    in_sem,
    out_sem,
):
    half, width = keep_ref.shape
    units = wup_own.shape[1]
    me = tp_ref[0]
    mine = pl.ds(pl.multiple_of(me * width, 128), width)
    theirs = pl.ds(pl.multiple_of((1 - me) * width, 128), width)
    own_rows = pl.ds(pl.multiple_of(me * half, half), half)
    copy = pltpu.make_async_copy
    first = start_all(
        [
            copy(wout_own, wout_buf.at[pl.ds(0, width)], in_sem.at[2]),
            copy(wout_oth, wout_buf.at[pl.ds(width, width)], in_sem.at[3]),
            copy(keep_ref, att_buf.at[:, pl.ds(0, width)], in_sem.at[0]),
            copy(recv_ref, att_buf.at[:, pl.ds(width, width)], in_sem.at[1]),
            copy(xown_ref.at[own_rows], x_buf.at[:, mine], in_sem.at[4]),
            copy(xoth_ref.at[own_rows], x_buf.at[:, theirs], in_sem.at[5]),
        ]
    )
    up_loads = start_all(
        [
            copy(wup_own, wup_buf.at[:, pl.ds(0, units)], in_sem.at[6]),
            copy(wup_oth, wup_buf.at[:, pl.ds(units, units)], in_sem.at[7]),
        ]
    )
    down_loads = start_all(
        [
            copy(wdown_own, wdown_buf.at[pl.ds(0, units)], in_sem.at[8]),
            copy(wdown_oth, wdown_buf.at[pl.ds(units, units)], in_sem.at[9]),
        ]
    )
    cot_loads = start_all(
        [
            copy(cotown_ref.at[own_rows], cot_buf.at[:, mine], in_sem.at[10]),
            copy(cototh_ref, cot_buf.at[:, theirs], in_sem.at[11]),
        ]
    )
    gain1, shift1, gain2, shift2 = (
        ref[...].reshape(1, 2 * width) for ref in (gain1_ref, shift1_ref, gain2_ref, shift2_ref)
    )
    block = min(256, half)
    blocks = half // block
    chunk = min(768, units)
    chunks = 2 * units // chunk
    features = 2 * width
    strips = [slice(low, low + 256) for low in range(0, features, 256)]
    bands = [slice(low, low + BAND) for low in range(0, block, BAND)]

    def rows_of(index):
        return pl.ds(pl.multiple_of(index * block, block), block)

    def band_of(index, band):
        return pl.ds(pl.multiple_of(index * block + band.start, BAND), BAND)

    def cols_of(part):
        return pl.ds(pl.multiple_of(part * chunk, chunk), chunk)

    def mix(index, strip):
        at = rows_of(index)
        fresh_buf[:, strip] = x_buf[at, strip].astype(F32) + nn(att_buf[at, :], wout_buf[:, strip])

    def first_norm(index, band):
        at = band_of(index, band)
        resid = held_buf[band, :]
        centered = resid - row_mean(resid)
        scale = lax.rsqrt(row_mean(centered * centered) + EPS_NORM)
        normed = centered * scale
        scale_buf[at, :] = scale
        normed_buf[at, :] = normed
        low_buf[at, :] = (normed * gain1 + shift1).astype(BF16)

    def widen(part):
        cols = cols_of(part)
        upper = nn(low_buf[...], wup_buf[:, cols])
        below, slope = cdf_and_slope(upper)
        act_buf[:, cols] = (upper * below).astype(BF16)
        slope_buf[:, cols] = slope.astype(BF16)

    def narrow(index, strip):
        at = rows_of(index)
        hidden = normed_buf[at, strip] * gain1[:, strip] + shift1[:, strip]
        fresh_buf[:, strip] = hidden + nn(act_buf[at, :], wdown_buf[:, strip])

    def second_norm(index, band):
        at = band_of(index, band)
        outer = held_buf[band, :]
        centered = outer - row_mean(outer)
        scale = lax.rsqrt(row_mean(centered * centered) + EPS_NORM)
        normed = centered * scale
        enc_buf[at, :] = (normed * gain2 + shift2).astype(BF16)
        d_outer = norm_pull(scale, normed, cot_buf[at, :].astype(F32) * gain2)
        outer_buf[at, :] = d_outer
        low_buf[at, :] = d_outer.astype(BF16)

    def widen_back(part):
        cols = cols_of(part)
        d_act = nt(low_buf[...], wdown_buf[cols, :])
        act_buf[:, cols] = (d_act * slope_buf[:, cols].astype(F32)).astype(BF16)

    def narrow_back(index, strip):
        at = rows_of(index)
        fresh_buf[:, strip] = outer_buf[at, strip] + nt(act_buf[at, :], wup_buf[strip, :])

    def first_norm_back(index, band):
        at = band_of(index, band)
        d_res = norm_pull(scale_buf[at, :], normed_buf[at, :], held_buf[band, :] * gain1)
        dres_buf[at, :] = d_res
        fresh_low_buf[band, :] = d_res.astype(BF16)

    def unmix(index, strip):
        at = rows_of(index)
        datt_buf[at, strip] = nt(held_low_buf[...], wout_buf[strip, :]).astype(BF16)

    def hand_on():
        held_buf[...] = fresh_buf[...]

    def hand_on_low():
        held_low_buf[...] = fresh_low_buf[...]

    def step(at, low, high, product, norm, last=None):
        clamped = [
            jnp.maximum(at - place, 0) if not isinstance(at, int) else max(at - place, 0)
            for place in range(3)
        ]
        if low <= 1 < high:
            hand_on()
        if last is not None and low <= 2 < high:
            hand_on_low()
        for turn in range(max(len(strips), len(bands))):
            if low <= 0 < high and turn < len(strips):
                product(clamped[0], strips[turn])
            if last is not None and low <= 2 < high and turn < len(strips):
                last(clamped[2], strips[turn])
            if low <= 1 < high and turn < len(bands):
                norm(clamped[1], bands[turn])

    def staggered(product, norm, last=None):
        @pl.loop(0, blocks)
        def _(at):
            step(at, 0, 3, product, norm, last)

        step(blocks, 1, 3, product, norm, last)
        if last is not None:
            step(blocks + 1, 2, 3, product, norm, last)

    def stores(index):
        at = rows_of(index)
        return [
            copy(datt_buf.at[at, pl.ds(width, width)], datt_send.at[at], out_sem.at[0, index]),
            copy(datt_buf.at[at, pl.ds(0, width)], datt_keep.at[at], out_sem.at[1, index]),
            copy(dres_buf.at[at], dres_out.at[at], out_sem.at[2, index]),
        ]

    wait_all(first)
    staggered(mix, first_norm)
    wait_all(up_loads)
    pl.loop(0, chunks)(widen)
    wait_all(down_loads)
    wait_all(cot_loads)
    staggered(narrow, second_norm)
    enc_stores = start_all(
        [
            copy(enc_buf.at[:, theirs], enc_send, out_sem.at[3, 0]),
            copy(enc_buf.at[:, mine], enc_out.at[own_rows], out_sem.at[4, 0]),
        ]
    )
    pl.loop(0, chunks)(widen_back)
    staggered(narrow_back, first_norm_back, unmix)
    for index in range(blocks):
        start_all(stores(index))
    for index in range(blocks):
        wait_all(stores(index))
    wait_all(enc_stores)


def rows_step(tp, keep, recv, x_own, x_oth, cot_own, cot_oth, weights, norms):
    half, width = keep.shape
    units = weights[2].shape[1]
    block = min(256, half)
    return pl.pallas_call(
        rows_kernel,
        out_shape=[
            shape_of((2 * half, width), BF16),
            shape_of((half, width), BF16),
            shape_of((half, 2 * width), F32),
            shape_of((half, width), BF16),
            pltpu.VMEM((half, width), BF16),
        ],
        in_specs=[SMEM, ANY, VMEM, ANY, VMEM, ANY, VMEM, ANY, VMEM] + [ANY] * 4 + [VMEM] * 4,
        out_specs=[ANY] * 4 + [VMEM],
        scratch_shapes=[
            pltpu.VMEM((half, 2 * width), BF16),
            pltpu.VMEM((half, 2 * width), BF16),
            pltpu.VMEM((half, 2 * width), BF16),
            pltpu.VMEM((2 * width, 2 * width), BF16),
            pltpu.VMEM((2 * width, 2 * units), BF16),
            pltpu.VMEM((2 * units, 2 * width), BF16),
            pltpu.VMEM((half, 2 * width), F32),
            pltpu.VMEM((half, 1), F32),
            pltpu.VMEM((half, 2 * width), BF16),
            pltpu.VMEM((half, 2 * units), BF16),
            pltpu.VMEM((half, 2 * units), BF16),
            pltpu.VMEM((block, 2 * width), F32),
            pltpu.VMEM((block, 2 * width), F32),
            pltpu.VMEM((block, 2 * width), BF16),
            pltpu.VMEM((block, 2 * width), BF16),
            pltpu.VMEM((half, 2 * width), F32),
            pltpu.VMEM((half, 2 * width), F32),
            pltpu.VMEM((half, 2 * width), BF16),
            pltpu.VMEM((half, 2 * width), BF16),
            pltpu.SemaphoreType.DMA((12,)),
            pltpu.SemaphoreType.DMA((5, half // block)),
        ],
        compiler_params=params(56),
        cost_estimate=pl.CostEstimate(
            flops=2 * half * (4 * width * (2 * width + 4 * units)),
            bytes_accessed=24 * half * width,
            transcendentals=0,
        ),
        name="rows_step",
    )(tp, keep, recv, x_own, x_oth, cot_own, cot_oth, *weights, *norms)


def backward_kernel(
    longest,
    tp_ref,
    lengths_ref,
    qkv_ref,
    dkeep_ref,
    drecv_ref,
    xown_ref,
    xoth_ref,
    mid_ref,
    lse_ref,
    upq_ref,
    upv_ref,
    wcat_ref,
    dres_ref,
    tok_keep_out,
    tok_send_out,
    keep_ref,
    send_ref,
    qkv_buf,
    do_buf,
    x_buf,
    mid_buf,
    d_buf,
    kt_buf,
    q_split,
    do_split,
    p_buf,
    ds_buf,
    grad_ref,
    wcat_buf,
    dres_buf,
    tok_keep_buf,
    tok_send_buf,
    in_sem,
    late_sem,
    out_sem,
):
    half, width = dkeep_ref.shape
    rows = 2 * half
    pairs = width // PAIR
    me = tp_ref[0]
    mine = pl.ds(pl.multiple_of(me * width, 128), width)
    theirs = pl.ds(pl.multiple_of((1 - me) * width, 128), width)
    copy = pltpu.make_async_copy
    block = min(512, half)
    blocks = rows // block

    def block_rows(index):
        return pl.ds(pl.multiple_of(index * block, block), block)

    def d_load(ref, part, index):
        return copy(ref.at[block_rows(part)], do_buf.at[block_rows(index)], in_sem.at[1, index])

    def qkv_load(index):
        at = block_rows(index)
        return copy(qkv_ref.at[at], qkv_buf.at[at], in_sem.at[0, index])

    for index in range(blocks):
        qkv_load(index).start()
        if index < blocks // 2:
            d_load(dkeep_ref, index, me * (blocks // 2) + index).start()
            d_load(drecv_ref, index, (1 - me) * (blocks // 2) + index).start()
    late = start_all(
        [
            copy(xown_ref, x_buf.at[:, mine], late_sem.at[0]),
            copy(xoth_ref, x_buf.at[:, theirs], late_sem.at[1]),
            copy(mid_ref, mid_buf, late_sem.at[2]),
            copy(wcat_ref, wcat_buf, late_sem.at[3]),
            copy(dres_ref, dres_buf, late_sem.at[4]),
        ]
    )
    for buf in (qkv_buf, do_buf):
        buf[rows:, :] = jnp.zeros((buf.shape[0] - rows, buf.shape[1]), BF16)

    def await_chunk(index):
        qkv_load(index).wait()
        d_load(dkeep_ref, 0, index).wait()

    def visit(count, start, first, end, tile):
        window = count * TILE
        keys_at = pl.ds(start, window)

        def lanes(part):
            return slice(part * 2 * TILE, (part + 1) * 2 * TILE)

        def score(pair, part):
            keys = qkv_buf[keys_at, pair_columns(pair, width)]
            if part == 0:
                kt_buf[pair, :, :window] = keys.T
            at = pl.ds(pl.multiple_of(start + part * TILE, ALIGN), TILE)
            queries = split_pair(qkv_buf[at, pair_columns(pair)])
            d_rows = split_pair(do_buf[at, pair_columns(pair)])
            q_split[pair, lanes(part), :] = queries
            do_split[pair, lanes(part), :] = d_rows
            return (
                nt(keys, queries),
                nt(qkv_buf[keys_at, pair_columns(pair, 2 * width)], d_rows),
            )

        def weigh(pair, part, scored):
            scores, d_probs = scored
            probs = jnp.exp2(scores - lse_ref[pair, pl.ds(tile + part, 1), :])
            probs = key_rows_masked(probs, start, first, end, 0.0)
            product = probs * d_probs
            delta = jnp.sum(product, axis=0, keepdims=True)
            p_buf[pair, :window, lanes(part)] = probs.astype(BF16)
            ds_buf[pair, :window, lanes(part)] = (product - probs * delta).astype(BF16)

        def finish(pair):
            every = slice(0, count * 2 * TILE)
            d_scores = ds_buf[pair, :window, every]
            d_values = nn(p_buf[pair, :window, every], do_split[pair, every, :])
            d_keys = nn(d_scores, q_split[pair, every, :]) * LN2
            columns = nn(kt_buf[pair, :, :window], d_scores) * LN2
            d_queries = jnp.concatenate(
                [merge_pair(columns[:, lanes(part)]) for part in range(count)], axis=0
            )
            for base, values in enumerate((d_queries, d_keys, d_values)):
                store_window(d_buf, pair_columns(pair, base * width), values, start, first, end)

        run_staged(pairs, count, score, weigh, finish)

    for_each_sentence(lengths_ref, longest, rows, block, await_chunk, visit)
    wait_all(late)

    def token_stores(index):
        at = block_rows(index)
        return [
            copy(tok_send_buf.at[at], tok_send_out.at[at], out_sem.at[0, index]),
            copy(tok_keep_buf.at[at], tok_keep_out.at[at], out_sem.at[1, index]),
        ]

    @pl.loop(0, blocks)
    def _(index):
        at = block_rows(index)
        total = nt(d_buf[at, :], wcat_buf[:, : 3 * width])
        low, high = total[:, :width], total[:, width:]
        tok_keep_buf[at, :] = jnp.where(me == 0, low, high)
        tok_send_buf[at, :] = jnp.where(me == 0, high, low).astype(BF16)

        @pl.when(index // (blocks // 2) == me)
        def _():
            resid = dres_buf[block_rows(lax.rem(index, blocks // 2)), :]
            low, high = resid[:, :width], resid[:, width:]
            tok_keep_buf[at, :] += jnp.where(me == 0, low, high)
            sent = tok_send_buf[at, :].astype(F32) + jnp.where(me == 0, high, low)
            tok_send_buf[at, :] = sent.astype(BF16)

        start_all(token_stores(index))

    d_query = d_buf[:rows, :width]
    d_value = d_buf[:rows, 2 * width :]
    mid = mid_buf[...]
    picked = spread_mask()
    features = 2 * width
    flat = features * RANK // 128
    steps = features // 128
    natural = ADAPTER_SCALE / (math.sqrt(HEAD) * LN2)
    for which, (grads, up_ref, scale) in enumerate(
        ((d_query, upq_ref, natural), (d_value, upv_ref, ADAPTER_SCALE))
    ):
        d_mid = (nt(up_ref[...], grads) * scale).astype(BF16)
        down = nn(d_mid, x_buf[...]).T
        down = jnp.where(picked[None], down.reshape(flat, 128 // RANK, 128), 0.0)
        grad_ref[pl.ds(which * flat, flat), :] = jnp.sum(down, axis=1)
        up = tn(mid, grads)[which * RANK : (which + 1) * RANK] * scale
        base = (2 + which) * flat
        own = me * (width // 128)
        other = (1 - me) * (width // 128)
        for step in range(width // 128):
            part = up[:, step * 128 : (step + 1) * 128]
            grad_ref[pl.ds(base + own + step, RANK, stride=steps), :] = part
            grad_ref[pl.ds(base + other + step, RANK, stride=steps), :] = jnp.zeros_like(part)
    share = keep_ref.shape[0]
    keep_ref[...] = grad_ref[pl.ds(pl.multiple_of(me * share, 8), share), :]
    send_ref[...] = grad_ref[pl.ds(pl.multiple_of((1 - me) * share, 8), share), :]
    for index in range(blocks):
        wait_all(token_stores(index))


def backward(
    tp, lengths, qkv, d_keep, d_recv, x_own, x_oth, mid, lse, up_q, up_v, wcat, dres, longest
):
    half, width = d_keep.shape
    rows = 2 * half
    pairs = width // PAIR
    padded = rows + TILE
    widest = widest_window(longest)
    blocks = rows // min(512, half)
    return pl.pallas_call(
        functools.partial(backward_kernel, longest),
        out_shape=[
            shape_of((rows, width), F32),
            shape_of((rows, width), BF16),
            pltpu.VMEM((4 * width * RANK // 128, 128), F32),
            pltpu.VMEM((4 * width * RANK // 128, 128), F32),
        ],
        in_specs=[SMEM, SMEM, ANY, ANY, VMEM, ANY, VMEM, ANY] + [VMEM] * 3 + [ANY] * 2,
        out_specs=[ANY, ANY, VMEM, VMEM],
        scratch_shapes=[
            pltpu.VMEM((padded, 3 * width), BF16),
            pltpu.VMEM((padded, width), BF16),
            pltpu.VMEM((rows, 2 * width), BF16),
            pltpu.VMEM((rows, 128), BF16),
            pltpu.VMEM((padded, 3 * width), BF16),
            pltpu.VMEM((pairs, PAIR, widest), BF16),
            pltpu.VMEM((pairs, 2 * widest, PAIR), BF16),
            pltpu.VMEM((pairs, 2 * widest, PAIR), BF16),
            pltpu.VMEM((pairs, widest, 2 * widest), BF16),
            pltpu.VMEM((pairs, widest, 2 * widest), BF16),
            pltpu.VMEM((8 * width * RANK // 128, 128), F32),
            pltpu.VMEM(wcat.shape, BF16),
            pltpu.VMEM((half, 2 * width), F32),
            pltpu.VMEM((rows, width), F32),
            pltpu.VMEM((rows, width), BF16),
            pltpu.SemaphoreType.DMA((2, blocks)),
            pltpu.SemaphoreType.DMA((5,)),
            pltpu.SemaphoreType.DMA((2, blocks)),
        ],
        compiler_params=params(56),
        cost_estimate=pl.CostEstimate(
            flops=30 * rows * width * width, bytes_accessed=20 * rows * width, transcendentals=0
        ),
        name="backward",
    )(tp, lengths, qkv, d_keep, d_recv, x_own, x_oth, mid, lse, up_q, up_v, wcat, dres)


def adam_update(gradient, moment_one, moment_two, weights, rates):
    first_new = BETA_ONE * moment_one + (1.0 - BETA_ONE) * gradient
    second_new = BETA_TWO * moment_two + (1.0 - BETA_TWO) * gradient * gradient
    update = first_new / BIAS_ONE / (jnp.sqrt(second_new / BIAS_TWO) + EPS_ADAM)
    return first_new, second_new, weights - rates * (update + DECAY_RATE * weights)


def exchange_groups(size):
    step = 1
    while step < size:
        if step * 2 < size:
            yield step, [step, 2 * step, 3 * step]
            step *= 4
        else:
            yield step, [step]
            step *= 2


def partners(values, size, offsets):
    return [
        lax.ppermute(values, "dp", [(i, i ^ offset) for i in range(size)]) for offset in offsets
    ]


def joined(total, moments, others, index):
    rows = total.shape[0]
    sums = [other[:rows] for other in others]
    parts = [moments] + [other[rows:] for other in others]
    if len(sums) == 3:
        total = (total + sums[0]) + (sums[1] + sums[2])
    else:
        total = total + sums[0]
    count = len(parts)
    ordered = [
        functools.reduce(
            lambda held, offset: jnp.where(index == offset, parts[spot ^ offset], held),
            range(1, count),
            parts[spot],
        )
        for spot in range(count)
    ]
    return total, jnp.concatenate(ordered, axis=0)


def in_order(mine, other, me):
    return jnp.where(
        me == 0, jnp.concatenate([mine, other], axis=0), jnp.concatenate([other, mine], axis=0)
    )


def in_vmem(values):
    return pltpu.with_memory_space_constraint(values, pltpu.VMEM)


def tied(*values):
    return lax.optimization_barrier(values)


def swap(values):
    return lax.ppermute(values, "tp", [(0, 1), (1, 0)])


def body(
    tokens,
    lengths,
    query_weight,
    w_key,
    value_weight,
    w_out,
    w_up,
    w_down,
    gain_attn,
    shift_attn,
    gain_ffn,
    shift_ffn,
    factors,
    first_moment,
    second_moment,
    cotangent,
):
    rows, width = tokens.shape
    features = 2 * width
    half = rows // 2
    longest = min(512, rows)
    me = lax.axis_index("tp")
    tp = me.astype(jnp.int32).reshape(1)
    dp_size = lax.axis_size("dp")
    other_rows = (1 - me) * half
    size_down = features * RANK
    own_lengths = lengths.reshape(-1)

    share = first_moment.shape[0]
    share_rows = -(-2 * share // 128)

    x_oth = swap(tokens)
    cot_oth = swap(lax.dynamic_slice_in_dim(cotangent, other_rows, half, 0))
    out_oth = swap(w_out)
    wcat, up_q, up_v = prepare(tp, factors.reshape(-1, 128), query_weight, w_key, value_weight)
    x_oth, cot_oth, out_oth, wcat, w_up_late, w_down_late = tied(
        x_oth, cot_oth, out_oth, wcat, w_up, w_down
    )
    up_oth, down_oth = swap(w_up_late), swap(w_down_late)
    cot_oth, out_oth, x_oth = in_vmem(cot_oth), in_vmem(out_oth), in_vmem(x_oth)

    qkv, mid, att_keep, att_send, lse = forward(
        tp, own_lengths, tokens, x_oth, wcat, longest
    )
    att_recv = in_vmem(swap(att_send))
    moments = jnp.concatenate([first_moment, second_moment])
    moments = jnp.pad(moments, (0, share_rows * 128 - 2 * share)).reshape(share_rows, 128)
    encoded, enc_send, dres, datt_keep, datt_send = rows_step(
        tp,
        att_keep,
        att_recv,
        tokens,
        x_oth,
        cotangent,
        cot_oth,
        (w_out, out_oth, w_up, up_oth, w_down, down_oth),
        (gain_attn, shift_attn, gain_ffn, shift_ffn),
    )
    datt_recv = in_vmem(swap(datt_send))
    enc_recv = swap(enc_send)
    tok_keep, tok_send, grad_keep, grad_send = backward(
        tp,
        own_lengths,
        qkv,
        datt_keep,
        datt_recv,
        tokens,
        x_oth,
        mid,
        lse,
        up_q,
        up_v,
        wcat,
        dres,
        longest,
    )
    grad_send, enc_recv = tied(grad_send, enc_recv)
    total = grad_keep + swap(grad_send)
    total, tok_send = tied(total, tok_send)
    tok_recv = swap(tok_send)
    encoded = lax.dynamic_update_slice(encoded, enc_recv, (other_rows, 0))
    d_tokens = tok_keep + tok_recv.astype(F32)
    place = lax.axis_index("dp")
    for turn, (step, offsets) in enumerate(exchange_groups(dp_size)):
        others = partners(jnp.concatenate([total, moments], axis=0), dp_size, offsets)
        if turn == 0:
            others, encoded = tied(others, encoded)
        elif turn == 1:
            others, d_tokens = tied(others, d_tokens)
        total, moments = joined(total, moments, others, (place // step) % (len(offsets) + 1))
    mine = jnp.concatenate([total, moments], axis=0)
    other = swap(mine)
    half_rows = total.shape[0]
    total = in_order(mine[:half_rows], other[:half_rows], me)
    moments = jnp.where(
        me == 0, jnp.stack([mine, other]), jnp.stack([other, mine])
    )[:, half_rows:].reshape(2, dp_size, -1)[:, :, : 2 * share]
    moments = jnp.swapaxes(moments, 0, 1).reshape(2 * dp_size, 2, share)

    gradient = total.reshape(-1) * (1.0 / math.sqrt(rows * dp_size))
    place = jnp.arange(gradient.shape[0], dtype=jnp.int32)
    rates = jnp.where(place < 2 * size_down, RATE_DOWN, RATE_DOWN * RATE_RATIO)
    _, _, factors_new = adam_update(
        gradient, moments[:, 0].reshape(-1), moments[:, 1].reshape(-1), factors, rates
    )
    share_start = lax.axis_index(("dp", "tp")) * share
    grad_share = lax.dynamic_slice_in_dim(gradient, share_start, share)
    first_new, second_new, _ = adam_update(grad_share, first_moment, second_moment, 0.0, 0.0)
    return encoded, d_tokens, grad_share, first_new, second_new, factors_new


def solution(mesh):
    placed = (
        P("dp", "tp"),
        P("dp", None),
        P(None, "tp"),
        P(None, "tp"),
        P(None, "tp"),
        P("tp", None),
        P(None, "tp"),
        P("tp", None),
        P(),
        P(),
        P(),
        P(),
        P(),
        P(("dp", "tp")),
        P(("dp", "tp")),
        P("dp", "tp"),
    )
    return jax.shard_map(
        body,
        mesh=mesh,
        in_specs=placed,
        out_specs=(
            P("dp", "tp"),
            P("dp", "tp"),
            P(("dp", "tp")),
            P(("dp", "tp")),
            P(("dp", "tp")),
            P(),
        ),
        check_vma=False,
    )
```

```python
import functools
import math

import jax
import jax.numpy as jnp
from jax import lax
from jax.experimental import pallas as pl
from jax.experimental.pallas import tpu as pltpu
from jax.sharding import PartitionSpec as P

HEAD = 64
RANK = 8
EPS_NORM = 1e-05
EPS_ADAM = 1e-08
BETA_ONE = 0.9
BETA_TWO = 0.999
BIAS_ONE = 1.0 - 0.9**10
BIAS_TWO = 1.0 - 0.999**10
RATE_DOWN = 0.002
RATE_RATIO = 16.0
DECAY_RATE = 0.01
ADAPTER_SCALE = 2.0
MASKED = -1e30
LOG2E = 1.4426950408889634
LN2 = 0.6931471805599453

TILE = 128
ALIGN = 16
PAIR = 2 * HEAD
BF16 = jnp.bfloat16
F32 = jnp.float32

ANY = pl.BlockSpec(memory_space=pl.ANY)
SMEM = pl.BlockSpec(memory_space=pltpu.SMEM)
VMEM = pl.BlockSpec(memory_space=pltpu.VMEM)


def shape_of(dims, kind):
    return jax.ShapeDtypeStruct(dims, kind)


def params(mib):
    return pltpu.CompilerParams(vmem_limit_bytes=mib * 1024 * 1024)


def nn(left, right):
    return lax.dot_general(left, right, (((1,), (0,)), ((), ())), preferred_element_type=F32)


def nt(left, right):
    return lax.dot_general(left, right, (((1,), (1,)), ((), ())), preferred_element_type=F32)


def tn(left, right):
    return lax.dot_general(left, right, (((0,), (0,)), ((), ())), preferred_element_type=F32)


def start_all(copies):
    for copy in copies:
        copy.start()
    return copies


def wait_all(copies):
    for copy in copies:
        copy.wait()


def for_each_sentence(lengths_ref, longest, rows, chunk, await_chunk, visit):
    def one(index, carry):
        first, tile, loaded = carry
        end = first + lengths_ref[index]
        start = pl.multiple_of((first // ALIGN) * ALIGN, ALIGN)
        steps = (end - start + (TILE - 1)) // TILE
        needed = jnp.minimum((start + steps * TILE + chunk - 1) // chunk, rows // chunk)
        loaded = await_chunks(loaded, needed)
        for count in range(1, (longest + ALIGN - 1 + TILE - 1) // TILE + 1):

            @pl.when(steps == count)
            def _():
                visit(count, start, first, end, tile)

        return end, tile + steps, loaded

    def await_chunks(loaded, needed):
        def one_chunk(index, _):
            await_chunk(index)
            return 0

        lax.fori_loop(loaded, needed, one_chunk, 0)
        return jnp.maximum(loaded, needed)

    zero = jnp.int32(0)
    carry = lax.fori_loop(0, lengths_ref.shape[0], one, (zero, zero, zero))
    await_chunks(carry[2], jnp.int32(rows // chunk))


def window_parts(window, start, first, end):
    def mask(low, high, lanes):
        rows = low + lax.broadcasted_iota(jnp.int32, (high - low, lanes), 0)
        return (rows >= first - start) & (rows < end - start)

    if window <= TILE:
        return [(0, window, mask)]
    whole = (window - 1) // TILE * TILE
    return [(0, ALIGN, mask), (ALIGN, whole, None), (whole, window, mask)]


def key_rows_masked(values, start, first, end, fill):
    window, lanes = values.shape
    return jnp.concatenate(
        [
            values[low:high]
            if mask is None
            else jnp.where(mask(low, high, lanes), values[low:high], fill)
            for low, high, mask in window_parts(window, start, first, end)
        ],
        axis=0,
    )


def store_window(ref, cols, values, start, first, end):
    window, lanes = values.shape
    for low, high, mask in window_parts(window, start, first, end):
        at = pl.ds(pl.multiple_of(start + low, ALIGN), high - low)
        part = values[low:high]
        if mask is not None:
            part = jnp.where(mask(low, high, lanes), part, ref[at, cols].astype(F32))
        ref[at, cols] = part.astype(BF16)


def pair_columns(pair, base=0):
    return pl.ds(pl.multiple_of(base + pair * PAIR, PAIR), PAIR)


DEPTH = 2
TOGETHER = 4


def run_staged(pairs, count, score, weigh, finish):
    def work(units):
        scored = {}
        for step in range(len(units) + DEPTH):
            if step < len(units):
                scored[step] = score(*units[step])
            if step >= DEPTH:
                pair, part = units[step - DEPTH]
                weigh(pair, part, scored.pop(step - DEPTH))
                if part == count - 1:
                    finish(pair)

    if count <= TOGETHER:
        work([(pair, part) for pair in range(pairs) for part in range(count)])
    else:

        @pl.loop(0, pairs)
        def _(pair):
            work([(pair, part) for part in range(count)])


def split_pair(rows):
    lane = lax.broadcasted_iota(jnp.int32, rows.shape, 1)
    zero = jnp.zeros_like(rows)
    return jnp.concatenate(
        [jnp.where(lane < HEAD, rows, zero), jnp.where(lane < HEAD, zero, rows)], axis=0
    )


def merge_pair(columns):
    rows = columns.shape[1] // 2
    row = lax.broadcasted_iota(jnp.int32, (PAIR, rows), 0)
    return jnp.where(row < HEAD, columns[:, :rows], columns[:, rows:]).T


def spread_mask():
    row = lax.broadcasted_iota(jnp.int32, (128 // RANK, 128), 0)
    return row == lax.broadcasted_iota(jnp.int32, (128 // RANK, 128), 1) // RANK


def prepare_kernel(tp_ref, factors_ref, wq_ref, wk_ref, wv_ref, wcat_ref, upq_ref, upv_ref):
    features, width = wq_ref.shape
    flat = features * RANK // 128
    steps = features // 128
    own = tp_ref[0] * (width // 128)
    group = 128 // RANK
    picked = spread_mask()
    lane = lax.broadcasted_iota(jnp.int32, (128, 128), 1)
    row = lax.broadcasted_iota(jnp.int32, (128, 128), 0)
    compact = jnp.zeros((features, 128), F32)
    for which, (w_ref, up_ref) in enumerate(((wq_ref, upq_ref), (wv_ref, upv_ref))):
        held = factors_ref[which * flat : (which + 1) * flat, :].reshape(flat, 1, 128)
        down = jnp.where(picked[None], jnp.broadcast_to(held, (flat, group, 128)), 0.0)
        down = down.reshape(features, 128).astype(BF16)
        base = (2 + which) * flat
        for step in range(width // 128):
            part = factors_ref[pl.ds(base + own + step, RANK, stride=steps), :]
            up_ref[:, step * 128 : (step + 1) * 128] = jnp.concatenate([part] * group).astype(
                BF16
            )
        scale = LOG2E / math.sqrt(HEAD) if which == 0 else 1.0
        combined = w_ref[...].astype(F32) + ADAPTER_SCALE * nn(down, up_ref[...])
        at = which * 2 * width
        wcat_ref[:, at : at + width] = (combined * scale).astype(BF16)
        choose = jnp.where(lane == which * RANK + row % RANK, 1.0, 0.0).astype(BF16)
        compact = compact + nn(down, choose)
    wcat_ref[:, width : 2 * width] = wk_ref[...]
    wcat_ref[:, 3 * width :] = compact.astype(BF16)


def prepare(tp, factors, wq, wk, wv):
    features, width = wq.shape
    return pl.pallas_call(
        prepare_kernel,
        out_shape=[
            pltpu.VMEM((features, 3 * width + 128), BF16),
            shape_of((128, width), BF16),
            shape_of((128, width), BF16),
        ],
        in_specs=[SMEM] + [VMEM] * 4,
        out_specs=[VMEM] * 3,
        compiler_params=params(56),
        cost_estimate=pl.CostEstimate(
            flops=4 * 128 * features * width, bytes_accessed=9 * features * width, transcendentals=0
        ),
        name="prepare",
    )(tp, factors, wq, wk, wv)


def forward_kernel(
    longest,
    tp_ref,
    lengths_ref,
    xown_ref,
    xoth_ref,
    wcat_ref,
    qkv_out,
    mid_out,
    keep_out,
    send_out,
    lse_ref,
    x_buf,
    qkv_buf,
    mid_buf,
    att_buf,
    vt_buf,
    p_buf,
    in_sem,
    out_sem,
):
    rows, width = xown_ref.shape
    half = rows // 2
    pairs = width // PAIR
    me = tp_ref[0]
    mine = pl.ds(pl.multiple_of(me * width, 128), width)
    theirs = pl.ds(pl.multiple_of((1 - me) * width, 128), width)
    copy = pltpu.make_async_copy
    block = min(512, rows)
    blocks = rows // block

    def loads(index):
        at = pl.ds(pl.multiple_of(index * block, block), block)
        return [
            copy(xown_ref.at[at], x_buf.at[at, mine], in_sem.at[0, index]),
            copy(xoth_ref.at[at], x_buf.at[at, theirs], in_sem.at[1, index]),
        ]

    def stores(index):
        at = pl.ds(pl.multiple_of(index * block, block), block)
        return [
            copy(qkv_buf.at[at], qkv_out.at[at], out_sem.at[0, index]),
            copy(mid_buf.at[at], mid_out.at[at], out_sem.at[1, index]),
        ]

    for index in range(blocks):
        start_all(loads(index))
    qkv_buf[rows:, :] = jnp.zeros((qkv_buf.shape[0] - rows, 3 * width), BF16)
    lse_ref[...] = jnp.full(lse_ref.shape, -MASKED, F32)

    @pl.loop(0, blocks)
    def _(index):
        at = pl.ds(pl.multiple_of(index * block, block), block)
        wait_all(loads(index))
        features = x_buf[at, :]
        for low in range(0, 3 * width, 256):
            high = min(low + 256, wcat_ref.shape[1])
            part = nn(features, wcat_ref[:, low:high]).astype(BF16)
            inner = min(high, 3 * width) - low
            qkv_buf[at, low : low + inner] = part[:, :inner]
            if inner < high - low:
                mid_buf[at, :] = part[:, inner:]
        start_all(stores(index))

    def visit(count, start, first, end, tile):
        window = window_of(count, longest)
        sizes = [tile_rows(count, part, window) for part in range(count)]
        covered = sum(sizes)
        keys_at = pl.ds(start, window)

        def score(pair, part):
            if part == 0:
                vt_buf[pair, :, :window] = qkv_buf[keys_at, pair_columns(pair, 2 * width)].T
            low = pl.multiple_of(start + part * TILE, ALIGN)
            queries = split_pair(qkv_buf[pl.ds(low, sizes[part]), pair_columns(pair)])
            return nt(qkv_buf[keys_at, pair_columns(pair, width)], queries)

        inverse = {}

        def weigh(pair, part, scores):
            low = start + part * TILE
            scores = key_rows_masked(scores, start, first, end, MASKED)
            top = jnp.max(scores, axis=0, keepdims=True)
            weights = jnp.exp2(scores - top)
            total = jnp.sum(weights, axis=0, keepdims=True)
            p_buf[pair, :window, tile_lanes(part, sizes[part])] = weights.astype(BF16)
            inverse[part if count > TOGETHER else (pair, part)] = 1.0 / total
            lane = lax.broadcasted_iota(jnp.int32, total.shape, 1)
            spot = low + jnp.where(lane < sizes[part], lane, lane - sizes[part])
            spread = jnp.where((spot >= first) & (spot < end), top + jnp.log2(total), -MASKED)
            if sizes[part] < TILE:
                rest = jnp.full((1, 2 * (TILE - sizes[part])), -MASKED, F32)
                spread = jnp.concatenate([spread, rest], axis=1)
            lse_ref[pair, pl.ds(tile + part, 1), :] = spread

        def finish(pair):
            columns = nn(vt_buf[pair, :, :window], p_buf[pair, :window, : 2 * covered])
            merged = [
                merge_pair(
                    columns[:, tile_lanes(part, sizes[part])]
                    * inverse[part if count > TOGETHER else (pair, part)]
                )
                for part in range(count)
            ]
            merged = jnp.concatenate(merged, axis=0)[:window]
            store_window(att_buf, pair_columns(pair), merged, start, first, end)

        run_staged(pairs, count, score, weigh, finish)

    for_each_sentence(lengths_ref, longest, rows, rows, lambda index: None, visit)
    mine_rows = pl.ds(pl.multiple_of(me * half, half), half)
    their_rows = pl.ds(pl.multiple_of((1 - me) * half, half), half)
    last = start_all(
        [
            copy(att_buf.at[their_rows], send_out, out_sem.at[0, blocks]),
            copy(att_buf.at[mine_rows], keep_out, out_sem.at[1, blocks]),
        ]
    )
    for index in range(blocks):
        wait_all(stores(index))
    wait_all(last)


def tiles_at_most(rows, sentences):
    return -(-(rows + sentences * (ALIGN - 1 + TILE - 1)) // TILE)


def widest_window(longest):
    return -(-(longest + ALIGN - 1) // TILE) * TILE


def window_of(count, longest):
    return min(count * TILE, -(-(longest + ALIGN - 1) // ALIGN) * ALIGN)


def tile_rows(count, part, window):
    return TILE // 2 if window - part * TILE <= TILE // 2 else TILE


def tile_lanes(part, rows):
    return slice(part * 2 * TILE, part * 2 * TILE + 2 * rows)


def forward(tp, lengths, x_own, x_oth, wcat, longest):
    rows, width = x_own.shape
    half = rows // 2
    pairs = width // PAIR
    tiles = -(-tiles_at_most(rows, lengths.shape[0]) // 8) * 8
    padded = rows + TILE
    widest = widest_window(longest)
    blocks = rows // min(512, rows)
    return pl.pallas_call(
        functools.partial(forward_kernel, longest),
        out_shape=[
            shape_of((rows, 3 * width), BF16),
            shape_of((rows, 128), BF16),
            shape_of((half, width), BF16),
            pltpu.VMEM((half, width), BF16),
            shape_of((pairs, tiles, 2 * TILE), F32),
        ],
        in_specs=[SMEM, SMEM, ANY, VMEM, VMEM],
        out_specs=[ANY] * 3 + [VMEM] * 2,
        scratch_shapes=[
            pltpu.VMEM((rows, 2 * width), BF16),
            pltpu.VMEM((padded, 3 * width), BF16),
            pltpu.VMEM((rows, 128), BF16),
            pltpu.VMEM((padded, width), BF16),
            pltpu.VMEM((pairs, PAIR, widest), BF16),
            pltpu.VMEM((pairs, widest, 2 * widest), BF16),
            pltpu.SemaphoreType.DMA((2, blocks)),
            pltpu.SemaphoreType.DMA((2, blocks + 1)),
        ],
        compiler_params=params(56),
        cost_estimate=pl.CostEstimate(
            flops=20 * rows * width * width, bytes_accessed=14 * rows * width, transcendentals=0
        ),
        name="forward",
    )(tp, lengths, x_own, x_oth, wcat)


def cdf_and_slope(upper):
    below = 0.5 + 0.5 * lax.erf(upper * math.sqrt(0.5))
    bell = jnp.exp2(upper * upper * (-0.5 * LOG2E))
    return below, below + upper * bell * (1.0 / math.sqrt(2.0 * math.pi))


def row_mean(values):
    return jnp.mean(values, axis=-1, keepdims=True)


def norm_pull(scale, normed, pulled):
    return scale * (pulled - row_mean(pulled) - normed * row_mean(pulled * normed))


BAND = 64


def rows_kernel(
    tp_ref,
    keep_ref,
    recv_ref,
    xown_ref,
    xoth_ref,
    cotown_ref,
    cototh_ref,
    wout_own,
    wout_oth,
    wup_own,
    wup_oth,
    wdown_own,
    wdown_oth,
    gain1_ref,
    shift1_ref,
    gain2_ref,
    shift2_ref,
    enc_out,
    enc_send,
    dres_out,
    datt_keep,
    datt_send,
    att_buf,
    x_buf,
    cot_buf,
    wout_buf,
    wup_buf,
    wdown_buf,
    normed_buf,
    scale_buf,
    low_buf,
    act_buf,
    slope_buf,
    fresh_buf,
    held_buf,
    outer_buf,
    dres_buf,
    enc_buf,
    datt_buf,
    in_sem,
    out_sem,
):
    half, width = keep_ref.shape
    units = wup_own.shape[1]
    me = tp_ref[0]
    mine = pl.ds(pl.multiple_of(me * width, 128), width)
    theirs = pl.ds(pl.multiple_of((1 - me) * width, 128), width)
    own_rows = pl.ds(pl.multiple_of(me * half, half), half)
    copy = pltpu.make_async_copy
    first = start_all(
        [
            copy(wout_own, wout_buf.at[pl.ds(0, width)], in_sem.at[2]),
            copy(wout_oth, wout_buf.at[pl.ds(width, width)], in_sem.at[3]),
            copy(keep_ref, att_buf.at[:, pl.ds(0, width)], in_sem.at[0]),
            copy(recv_ref, att_buf.at[:, pl.ds(width, width)], in_sem.at[1]),
            copy(xown_ref.at[own_rows], x_buf.at[:, mine], in_sem.at[4]),
            copy(xoth_ref.at[own_rows], x_buf.at[:, theirs], in_sem.at[5]),
        ]
    )
    up_loads = (
        [
            copy(wup_own, wup_buf.at[:, pl.ds(0, units)], in_sem.at[6]),
            copy(wup_oth, wup_buf.at[:, pl.ds(units, units)], in_sem.at[7]),
        ]
    )
    down_loads = (
        [
            copy(wdown_own, wdown_buf.at[pl.ds(0, units)], in_sem.at[8]),
            copy(wdown_oth, wdown_buf.at[pl.ds(units, units)], in_sem.at[9]),
        ]
    )
    cot_loads = (
        [
            copy(cotown_ref.at[own_rows], cot_buf.at[:, mine], in_sem.at[10]),
            copy(cototh_ref, cot_buf.at[:, theirs], in_sem.at[11]),
        ]
    )
    gain1, shift1, gain2, shift2 = (
        ref[...].reshape(1, 2 * width) for ref in (gain1_ref, shift1_ref, gain2_ref, shift2_ref)
    )
    block = min(256, half)
    blocks = half // block
    chunk = min(768, units)
    chunks = 2 * units // chunk
    features = 2 * width
    strips = [slice(low, low + 256) for low in range(0, features, 256)]
    sides = [slice(0, width), slice(width, features)]
    bands = [slice(low, low + BAND) for low in range(0, block, BAND)]

    def rows_of(index):
        return pl.ds(pl.multiple_of(index * block, block), block)

    def band_of(index, band):
        return pl.ds(pl.multiple_of(index * block + band.start, BAND), BAND)

    def cols_of(part):
        return pl.ds(pl.multiple_of(part * chunk, chunk), chunk)

    def mix(index, strip):
        at = rows_of(index)
        fresh_buf[:, strip] = x_buf[at, strip].astype(F32) + nn(att_buf[at, :], wout_buf[:, strip])

    def first_norm(index, band):
        at = band_of(index, band)
        resid = held_buf[band, :]
        centered = resid - row_mean(resid)
        scale = lax.rsqrt(row_mean(centered * centered) + EPS_NORM)
        normed = centered * scale
        scale_buf[at, :] = scale
        normed_buf[at, :] = normed
        low_buf[at, :] = (normed * gain1 + shift1).astype(BF16)

    def widen(part):
        cols = cols_of(part)
        upper = nn(low_buf[...], wup_buf[:, cols])
        below, slope = cdf_and_slope(upper)
        act_buf[:, cols] = (upper * below).astype(BF16)
        slope_buf[:, cols] = slope.astype(BF16)

    def narrow(index, strip):
        at = rows_of(index)
        hidden = normed_buf[at, strip] * gain1[:, strip] + shift1[:, strip]
        fresh_buf[:, strip] = hidden + nn(act_buf[at, :], wdown_buf[:, strip])

    def second_norm(index, band):
        at = band_of(index, band)
        outer = held_buf[band, :]
        centered = outer - row_mean(outer)
        scale = lax.rsqrt(row_mean(centered * centered) + EPS_NORM)
        normed = centered * scale
        enc_buf[at, :] = (normed * gain2 + shift2).astype(BF16)
        d_outer = norm_pull(scale, normed, cot_buf[at, :].astype(F32) * gain2)
        outer_buf[at, :] = d_outer
        low_buf[at, :] = d_outer.astype(BF16)

    def widen_back(part):
        cols = cols_of(part)
        d_act = nt(low_buf[...], wdown_buf[cols, :])
        act_buf[:, cols] = (d_act * slope_buf[:, cols].astype(F32)).astype(BF16)

    def narrow_back(index, strip):
        at = rows_of(index)
        fresh_buf[:, strip] = outer_buf[at, strip] + nt(act_buf[at, :], wup_buf[strip, :])

    def first_norm_back(index, band):
        at = band_of(index, band)
        d_res = norm_pull(scale_buf[at, :], normed_buf[at, :], held_buf[band, :] * gain1)
        dres_buf[at, :] = d_res.astype(BF16)

    def unmix(strip):
        datt_buf[:, strip] = nt(dres_buf[...], wout_buf[strip, :]).astype(BF16)

    def step(at, product, norm):
        held_buf[...] = fresh_buf[...]
        for turn in range(max(len(strips), len(bands))):
            if product is not None and turn < len(strips):
                product(at, strips[turn])
            if turn < len(bands):
                norm(jnp.maximum(at - 1, 0), bands[turn])

    def staggered(product, norm):
        @pl.loop(0, blocks)
        def _(at):
            step(at, product, norm)

        step(blocks, None, norm)

    wait_all(first)
    start_all(up_loads)
    start_all(down_loads)
    start_all(cot_loads)
    staggered(mix, first_norm)
    wait_all(up_loads)
    pl.loop(0, chunks)(widen)
    wait_all(down_loads)
    wait_all(cot_loads)
    staggered(narrow, second_norm)
    enc_stores = start_all(
        [
            copy(enc_buf.at[:, theirs], enc_send, out_sem.at[3]),
            copy(enc_buf.at[:, mine], enc_out.at[own_rows], out_sem.at[4]),
        ]
    )
    pl.loop(0, chunks)(widen_back)
    staggered(narrow_back, first_norm_back)
    last = start_all([copy(dres_buf, dres_out, out_sem.at[2])])
    unmix(sides[1])
    last += start_all([copy(datt_buf.at[:, pl.ds(width, width)], datt_send, out_sem.at[0])])
    unmix(sides[0])
    last += start_all([copy(datt_buf.at[:, pl.ds(0, width)], datt_keep, out_sem.at[1])])
    wait_all(last)
    wait_all(enc_stores)


def rows_step(tp, keep, recv, x_own, x_oth, cot_own, cot_oth, weights, norms):
    half, width = keep.shape
    units = weights[2].shape[1]
    block = min(256, half)
    return pl.pallas_call(
        rows_kernel,
        out_shape=[
            shape_of((2 * half, width), BF16),
            shape_of((half, width), BF16),
            shape_of((half, 2 * width), BF16),
            shape_of((half, width), BF16),
            pltpu.VMEM((half, width), BF16),
        ],
        in_specs=[SMEM, ANY, VMEM, ANY, VMEM, ANY, VMEM, ANY, VMEM] + [ANY] * 4 + [VMEM] * 4,
        out_specs=[ANY] * 4 + [VMEM],
        scratch_shapes=[
            pltpu.VMEM((half, 2 * width), BF16),
            pltpu.VMEM((half, 2 * width), BF16),
            pltpu.VMEM((half, 2 * width), BF16),
            pltpu.VMEM((2 * width, 2 * width), BF16),
            pltpu.VMEM((2 * width, 2 * units), BF16),
            pltpu.VMEM((2 * units, 2 * width), BF16),
            pltpu.VMEM((half, 2 * width), F32),
            pltpu.VMEM((half, 1), F32),
            pltpu.VMEM((half, 2 * width), BF16),
            pltpu.VMEM((half, 2 * units), BF16),
            pltpu.VMEM((half, 2 * units), BF16),
            pltpu.VMEM((block, 2 * width), F32),
            pltpu.VMEM((block, 2 * width), F32),
            pltpu.VMEM((half, 2 * width), F32),
            pltpu.VMEM((half, 2 * width), BF16),
            pltpu.VMEM((half, 2 * width), BF16),
            pltpu.VMEM((half, 2 * width), BF16),
            pltpu.SemaphoreType.DMA((12,)),
            pltpu.SemaphoreType.DMA((5,)),
        ],
        compiler_params=params(56),
        cost_estimate=pl.CostEstimate(
            flops=2 * half * (4 * width * (2 * width + 4 * units)),
            bytes_accessed=24 * half * width,
            transcendentals=0,
        ),
        name="rows_step",
    )(tp, keep, recv, x_own, x_oth, cot_own, cot_oth, *weights, *norms)


def backward_kernel(
    longest,
    tp_ref,
    lengths_ref,
    qkv_ref,
    dkeep_ref,
    drecv_ref,
    xown_ref,
    xoth_ref,
    mid_ref,
    lse_ref,
    upq_ref,
    upv_ref,
    wcat_ref,
    dres_ref,
    tok_keep_out,
    tok_send_out,
    keep_ref,
    send_ref,
    qkv_buf,
    do_buf,
    x_buf,
    mid_buf,
    d_buf,
    kt_buf,
    q_split,
    do_split,
    p_buf,
    ds_buf,
    grad_ref,
    wcat_buf,
    dres_buf,
    tok_keep_buf,
    tok_send_buf,
    in_sem,
    late_sem,
    out_sem,
):
    half, width = dkeep_ref.shape
    rows = 2 * half
    pairs = width // PAIR
    me = tp_ref[0]
    mine = pl.ds(pl.multiple_of(me * width, 128), width)
    theirs = pl.ds(pl.multiple_of((1 - me) * width, 128), width)
    copy = pltpu.make_async_copy
    block = min(512, half)
    blocks = rows // block

    def block_rows(index):
        return pl.ds(pl.multiple_of(index * block, block), block)

    def d_load(ref, part, index):
        return copy(ref.at[block_rows(part)], do_buf.at[block_rows(index)], in_sem.at[1, index])

    def qkv_load(index):
        at = block_rows(index)
        return copy(qkv_ref.at[at], qkv_buf.at[at], in_sem.at[0, index])

    for index in range(blocks):
        qkv_load(index).start()
        if index < blocks // 2:
            d_load(dkeep_ref, index, me * (blocks // 2) + index).start()
            d_load(drecv_ref, index, (1 - me) * (blocks // 2) + index).start()
    late = start_all(
        [
            copy(xown_ref, x_buf.at[:, mine], late_sem.at[0]),
            copy(xoth_ref, x_buf.at[:, theirs], late_sem.at[1]),
            copy(mid_ref, mid_buf, late_sem.at[2]),
            copy(wcat_ref, wcat_buf, late_sem.at[3]),
            copy(dres_ref, dres_buf, late_sem.at[4]),
        ]
    )
    for buf in (qkv_buf, do_buf):
        buf[rows:, :] = jnp.zeros((buf.shape[0] - rows, buf.shape[1]), BF16)

    def await_chunk(index):
        qkv_load(index).wait()
        d_load(dkeep_ref, 0, index).wait()

    def visit(count, start, first, end, tile):
        window = window_of(count, longest)
        sizes = [tile_rows(count, part, window) for part in range(count)]
        covered = sum(sizes)
        keys_at = pl.ds(start, window)

        def lanes(part):
            return tile_lanes(part, sizes[part])

        def score(pair, part):
            keys = qkv_buf[keys_at, pair_columns(pair, width)]
            if part == 0:
                kt_buf[pair, :, :window] = keys.T
            at = pl.ds(pl.multiple_of(start + part * TILE, ALIGN), sizes[part])
            queries = split_pair(qkv_buf[at, pair_columns(pair)])
            d_rows = split_pair(do_buf[at, pair_columns(pair)])
            q_split[pair, lanes(part), :] = queries
            do_split[pair, lanes(part), :] = d_rows
            return (
                nt(keys, queries),
                nt(qkv_buf[keys_at, pair_columns(pair, 2 * width)], d_rows),
            )

        def weigh(pair, part, scored):
            scores, d_probs = scored
            probs = jnp.exp2(scores - lse_ref[pair, pl.ds(tile + part, 1), :][:, : 2 * sizes[part]])
            probs = key_rows_masked(probs, start, first, end, 0.0)
            product = probs * d_probs
            delta = jnp.sum(product, axis=0, keepdims=True)
            p_buf[pair, :window, lanes(part)] = probs.astype(BF16)
            ds_buf[pair, :window, lanes(part)] = (product - probs * delta).astype(BF16)

        def finish(pair):
            every = slice(0, 2 * covered)
            d_scores = ds_buf[pair, :window, every]
            d_values = nn(p_buf[pair, :window, every], do_split[pair, every, :])
            d_keys = nn(d_scores, q_split[pair, every, :]) * LN2
            columns = nn(kt_buf[pair, :, :window], d_scores) * LN2
            d_queries = jnp.concatenate(
                [merge_pair(columns[:, lanes(part)]) for part in range(count)], axis=0
            )[:window]
            for base, values in enumerate((d_queries, d_keys, d_values)):
                store_window(d_buf, pair_columns(pair, base * width), values, start, first, end)

        run_staged(pairs, count, score, weigh, finish)

    for_each_sentence(lengths_ref, longest, rows, block, await_chunk, visit)
    wait_all(late)

    def token_stores(index):
        at = block_rows(index)
        return [
            copy(tok_send_buf.at[at], tok_send_out.at[at], out_sem.at[0, index]),
            copy(tok_keep_buf.at[at], tok_keep_out.at[at], out_sem.at[1, index]),
        ]

    @pl.loop(0, blocks)
    def _(index):
        at = block_rows(index)
        total = nt(d_buf[at, :], wcat_buf[:, : 3 * width])
        low, high = total[:, :width], total[:, width:]
        tok_keep_buf[at, :] = jnp.where(me == 0, low, high)
        tok_send_buf[at, :] = jnp.where(me == 0, high, low).astype(BF16)

        @pl.when(index // (blocks // 2) == me)
        def _():
            resid = dres_buf[block_rows(lax.rem(index, blocks // 2)), :].astype(F32)
            low, high = resid[:, :width], resid[:, width:]
            tok_keep_buf[at, :] += jnp.where(me == 0, low, high)
            sent = tok_send_buf[at, :].astype(F32) + jnp.where(me == 0, high, low)
            tok_send_buf[at, :] = sent.astype(BF16)

        start_all(token_stores(index))

    d_query = d_buf[:rows, :width]
    d_value = d_buf[:rows, 2 * width :]
    mid = mid_buf[...]
    picked = spread_mask()
    features = 2 * width
    flat = features * RANK // 128
    steps = features // 128
    natural = ADAPTER_SCALE / (math.sqrt(HEAD) * LN2)
    for which, (grads, up_ref, scale) in enumerate(
        ((d_query, upq_ref, natural), (d_value, upv_ref, ADAPTER_SCALE))
    ):
        d_mid = (nt(up_ref[...], grads) * scale).astype(BF16)
        down = nn(d_mid, x_buf[...]).T
        down = jnp.where(picked[None], down.reshape(flat, 128 // RANK, 128), 0.0)
        grad_ref[pl.ds(which * flat, flat), :] = jnp.sum(down, axis=1)
        up = tn(mid, grads)[which * RANK : (which + 1) * RANK] * scale
        base = (2 + which) * flat
        own = me * (width // 128)
        other = (1 - me) * (width // 128)
        for step in range(width // 128):
            part = up[:, step * 128 : (step + 1) * 128]
            grad_ref[pl.ds(base + own + step, RANK, stride=steps), :] = part
            grad_ref[pl.ds(base + other + step, RANK, stride=steps), :] = jnp.zeros_like(part)
    share = keep_ref.shape[0]
    keep_ref[...] = grad_ref[pl.ds(pl.multiple_of(me * share, 8), share), :]
    send_ref[...] = grad_ref[pl.ds(pl.multiple_of((1 - me) * share, 8), share), :]
    for index in range(blocks):
        wait_all(token_stores(index))


def backward(
    tp, lengths, qkv, d_keep, d_recv, x_own, x_oth, mid, lse, up_q, up_v, wcat, dres, longest
):
    half, width = d_keep.shape
    rows = 2 * half
    pairs = width // PAIR
    padded = rows + TILE
    widest = widest_window(longest)
    blocks = rows // min(512, half)
    return pl.pallas_call(
        functools.partial(backward_kernel, longest),
        out_shape=[
            shape_of((rows, width), F32),
            shape_of((rows, width), BF16),
            pltpu.VMEM((4 * width * RANK // 128, 128), F32),
            pltpu.VMEM((4 * width * RANK // 128, 128), F32),
        ],
        in_specs=[SMEM, SMEM, ANY, ANY, VMEM, ANY, VMEM, ANY] + [VMEM] * 3 + [ANY] * 2,
        out_specs=[ANY, ANY, VMEM, VMEM],
        scratch_shapes=[
            pltpu.VMEM((padded, 3 * width), BF16),
            pltpu.VMEM((padded, width), BF16),
            pltpu.VMEM((rows, 2 * width), BF16),
            pltpu.VMEM((rows, 128), BF16),
            pltpu.VMEM((padded, 3 * width), BF16),
            pltpu.VMEM((pairs, PAIR, widest), BF16),
            pltpu.VMEM((pairs, 2 * widest, PAIR), BF16),
            pltpu.VMEM((pairs, 2 * widest, PAIR), BF16),
            pltpu.VMEM((pairs, widest, 2 * widest), BF16),
            pltpu.VMEM((pairs, widest, 2 * widest), BF16),
            pltpu.VMEM((8 * width * RANK // 128, 128), F32),
            pltpu.VMEM(wcat.shape, BF16),
            pltpu.VMEM((half, 2 * width), BF16),
            pltpu.VMEM((rows, width), F32),
            pltpu.VMEM((rows, width), BF16),
            pltpu.SemaphoreType.DMA((2, blocks)),
            pltpu.SemaphoreType.DMA((5,)),
            pltpu.SemaphoreType.DMA((2, blocks)),
        ],
        compiler_params=params(56),
        cost_estimate=pl.CostEstimate(
            flops=30 * rows * width * width, bytes_accessed=20 * rows * width, transcendentals=0
        ),
        name="backward",
    )(tp, lengths, qkv, d_keep, d_recv, x_own, x_oth, mid, lse, up_q, up_v, wcat, dres)


def adam_update(gradient, moment_one, moment_two, weights, rates):
    first_new = BETA_ONE * moment_one + (1.0 - BETA_ONE) * gradient
    second_new = BETA_TWO * moment_two + (1.0 - BETA_TWO) * gradient * gradient
    update = first_new / BIAS_ONE / (jnp.sqrt(second_new / BIAS_TWO) + EPS_ADAM)
    return first_new, second_new, weights - rates * (update + DECAY_RATE * weights)


def exchange_groups(size):
    step = 1
    while step < size:
        if step * 2 < size:
            yield step, [step, 2 * step, 3 * step]
            step *= 4
        else:
            yield step, [step]
            step *= 2


def partners(values, size, offsets):
    return [
        lax.ppermute(values, "dp", [(i, i ^ offset) for i in range(size)]) for offset in offsets
    ]


def joined(total, moments, others, index):
    rows = total.shape[0]
    sums = [other[:rows] for other in others]
    parts = [moments] + [other[rows:] for other in others]
    if len(sums) == 3:
        total = (total + sums[0]) + (sums[1] + sums[2])
    else:
        total = total + sums[0]
    count = len(parts)
    ordered = [
        functools.reduce(
            lambda held, offset: jnp.where(index == offset, parts[spot ^ offset], held),
            range(1, count),
            parts[spot],
        )
        for spot in range(count)
    ]
    return total, jnp.concatenate(ordered, axis=0)


def in_order(mine, other, me):
    return jnp.where(
        me == 0, jnp.concatenate([mine, other], axis=0), jnp.concatenate([other, mine], axis=0)
    )


def in_vmem(values):
    return pltpu.with_memory_space_constraint(values, pltpu.VMEM)


def tied(*values):
    return lax.optimization_barrier(values)


def swap(values):
    return lax.ppermute(values, "tp", [(0, 1), (1, 0)])


def body(
    tokens,
    lengths,
    query_weight,
    w_key,
    value_weight,
    w_out,
    w_up,
    w_down,
    gain_attn,
    shift_attn,
    gain_ffn,
    shift_ffn,
    factors,
    first_moment,
    second_moment,
    cotangent,
):
    rows, width = tokens.shape
    features = 2 * width
    half = rows // 2
    longest = min(512, rows)
    me = lax.axis_index("tp")
    tp = me.astype(jnp.int32).reshape(1)
    dp_size = lax.axis_size("dp")
    other_rows = (1 - me) * half
    size_down = features * RANK
    own_lengths = lengths.reshape(-1)

    share = first_moment.shape[0]
    share_rows = -(-2 * share // 128)

    x_oth = swap(tokens)
    cot_oth = swap(lax.dynamic_slice_in_dim(cotangent, other_rows, half, 0))
    out_oth = swap(w_out)
    wcat, up_q, up_v = prepare(tp, factors.reshape(-1, 128), query_weight, w_key, value_weight)
    x_oth, cot_oth, out_oth, wcat, w_up_late, w_down_late = tied(
        x_oth, cot_oth, out_oth, wcat, w_up, w_down
    )
    up_oth, down_oth = swap(w_up_late), swap(w_down_late)
    cot_oth, out_oth, x_oth = in_vmem(cot_oth), in_vmem(out_oth), in_vmem(x_oth)

    qkv, mid, att_keep, att_send, lse = forward(
        tp, own_lengths, tokens, x_oth, wcat, longest
    )
    att_recv = in_vmem(swap(att_send))
    moments = jnp.concatenate([first_moment, second_moment])
    moments = jnp.pad(moments, (0, share_rows * 128 - 2 * share)).reshape(share_rows, 128)
    encoded, enc_send, dres, datt_keep, datt_send = rows_step(
        tp,
        att_keep,
        att_recv,
        tokens,
        x_oth,
        cotangent,
        cot_oth,
        (w_out, out_oth, w_up, up_oth, w_down, down_oth),
        (gain_attn, shift_attn, gain_ffn, shift_ffn),
    )
    datt_recv = in_vmem(swap(datt_send))
    enc_recv = swap(enc_send)
    tok_keep, tok_send, grad_keep, grad_send = backward(
        tp,
        own_lengths,
        qkv,
        datt_keep,
        datt_recv,
        tokens,
        x_oth,
        mid,
        lse,
        up_q,
        up_v,
        wcat,
        dres,
        longest,
    )
    grad_send, enc_recv = tied(grad_send, enc_recv)
    total = grad_keep + swap(grad_send)
    total, tok_send = tied(total, tok_send)
    tok_recv = swap(tok_send)
    encoded = lax.dynamic_update_slice(encoded, enc_recv, (other_rows, 0))
    d_tokens = tok_keep + tok_recv.astype(F32)
    place = lax.axis_index("dp")
    for turn, (step, offsets) in enumerate(exchange_groups(dp_size)):
        others = partners(jnp.concatenate([total, moments], axis=0), dp_size, offsets)
        if turn == 0:
            others, encoded = tied(others, encoded)
        elif turn == 1:
            others, d_tokens = tied(others, d_tokens)
        total, moments = joined(total, moments, others, (place // step) % (len(offsets) + 1))
    mine = jnp.concatenate([total, moments], axis=0)
    other = swap(mine)
    half_rows = total.shape[0]
    total = in_order(mine[:half_rows], other[:half_rows], me)
    moments = jnp.where(
        me == 0, jnp.stack([mine, other]), jnp.stack([other, mine])
    )[:, half_rows:].reshape(2, dp_size, -1)[:, :, : 2 * share]
    moments = jnp.swapaxes(moments, 0, 1).reshape(2 * dp_size, 2, share)

    gradient = total.reshape(-1) * (1.0 / math.sqrt(rows * dp_size))
    place = jnp.arange(gradient.shape[0], dtype=jnp.int32)
    rates = jnp.where(place < 2 * size_down, RATE_DOWN, RATE_DOWN * RATE_RATIO)
    _, _, factors_new = adam_update(
        gradient, moments[:, 0].reshape(-1), moments[:, 1].reshape(-1), factors, rates
    )
    share_start = lax.axis_index(("dp", "tp")) * share
    grad_share = lax.dynamic_slice_in_dim(gradient, share_start, share)
    first_new, second_new, _ = adam_update(grad_share, first_moment, second_moment, 0.0, 0.0)
    return encoded, d_tokens, grad_share, first_new, second_new, factors_new


def solution(mesh):
    placed = (
        P("dp", "tp"),
        P("dp", None),
        P(None, "tp"),
        P(None, "tp"),
        P(None, "tp"),
        P("tp", None),
        P(None, "tp"),
        P("tp", None),
        P(),
        P(),
        P(),
        P(),
        P(),
        P(("dp", "tp")),
        P(("dp", "tp")),
        P("dp", "tp"),
    )
    return jax.shard_map(
        body,
        mesh=mesh,
        in_specs=placed,
        out_specs=(
            P("dp", "tp"),
            P("dp", "tp"),
            P(("dp", "tp")),
            P(("dp", "tp")),
            P(("dp", "tp")),
            P(),
        ),
        check_vma=False,
    )
```

```python
import functools
import math

import jax
import jax.numpy as jnp
from jax import lax
from jax.experimental import pallas as pl
from jax.experimental.pallas import tpu as pltpu
from jax.sharding import PartitionSpec as P

HEAD = 64
RANK = 8
EPS_NORM = 1e-05
EPS_ADAM = 1e-08
BETA_ONE = 0.9
BETA_TWO = 0.999
BIAS_ONE = 1.0 - 0.9**10
BIAS_TWO = 1.0 - 0.999**10
RATE_DOWN = 0.002
RATE_RATIO = 16.0
DECAY_RATE = 0.01
ADAPTER_SCALE = 2.0
MASKED = -1e30
LOG2E = 1.4426950408889634
LN2 = 0.6931471805599453

TILE = 128
ALIGN = 16
PAIR = 2 * HEAD
BF16 = jnp.bfloat16
F32 = jnp.float32

ANY = pl.BlockSpec(memory_space=pl.ANY)
SMEM = pl.BlockSpec(memory_space=pltpu.SMEM)
VMEM = pl.BlockSpec(memory_space=pltpu.VMEM)


def shape_of(dims, kind):
    return jax.ShapeDtypeStruct(dims, kind)


def params(mib):
    return pltpu.CompilerParams(vmem_limit_bytes=mib * 1024 * 1024)


def nn(left, right):
    return lax.dot_general(left, right, (((1,), (0,)), ((), ())), preferred_element_type=F32)


def nt(left, right):
    return lax.dot_general(left, right, (((1,), (1,)), ((), ())), preferred_element_type=F32)


def tn(left, right):
    return lax.dot_general(left, right, (((0,), (0,)), ((), ())), preferred_element_type=F32)


def start_all(copies):
    for copy in copies:
        copy.start()
    return copies


def wait_all(copies):
    for copy in copies:
        copy.wait()


def for_each_sentence(lengths_ref, longest, rows, chunk, await_chunk, visit):
    def one(index, carry):
        first, tile, loaded = carry
        end = first + lengths_ref[index]
        start = pl.multiple_of((first // ALIGN) * ALIGN, ALIGN)
        steps = (end - start + (TILE - 1)) // TILE
        needed = jnp.minimum((start + steps * TILE + chunk - 1) // chunk, rows // chunk)
        loaded = await_chunks(loaded, needed)
        for count in range(1, (longest + ALIGN - 1 + TILE - 1) // TILE + 1):

            @pl.when(steps == count)
            def _():
                visit(count, start, first, end, tile)

        return end, tile + steps, loaded

    def await_chunks(loaded, needed):
        def one_chunk(index, _):
            await_chunk(index)
            return 0

        lax.fori_loop(loaded, needed, one_chunk, 0)
        return jnp.maximum(loaded, needed)

    zero = jnp.int32(0)
    carry = lax.fori_loop(0, lengths_ref.shape[0], one, (zero, zero, zero))
    await_chunks(carry[2], jnp.int32(rows // chunk))


def window_parts(window, start, first, end):
    def mask(low, high, lanes):
        rows = low + lax.broadcasted_iota(jnp.int32, (high - low, lanes), 0)
        return (rows >= first - start) & (rows < end - start)

    if window <= TILE:
        return [(0, window, mask)]
    whole = (window - 1) // TILE * TILE
    return [(0, ALIGN, mask), (ALIGN, whole, None), (whole, window, mask)]


def key_rows_masked(values, start, first, end, fill):
    window, lanes = values.shape
    return jnp.concatenate(
        [
            values[low:high]
            if mask is None
            else jnp.where(mask(low, high, lanes), values[low:high], fill)
            for low, high, mask in window_parts(window, start, first, end)
        ],
        axis=0,
    )


def store_window(ref, cols, values, start, first, end):
    window, lanes = values.shape
    for low, high, mask in window_parts(window, start, first, end):
        at = pl.ds(pl.multiple_of(start + low, ALIGN), high - low)
        part = values[low:high]
        if mask is not None:
            part = jnp.where(mask(low, high, lanes), part, ref[at, cols].astype(F32))
        ref[at, cols] = part.astype(BF16)


def pair_columns(pair, base=0):
    return pl.ds(pl.multiple_of(base + pair * PAIR, PAIR), PAIR)


DEPTH = 2
TOGETHER = 4


def run_staged(pairs, count, score, weigh, finish):
    def work(units):
        scored = {}
        for step in range(len(units) + DEPTH):
            if step < len(units):
                scored[step] = score(*units[step])
            if step >= DEPTH:
                pair, part = units[step - DEPTH]
                weigh(pair, part, scored.pop(step - DEPTH))
                if part == count - 1:
                    finish(pair)

    if count <= TOGETHER:
        work([(pair, part) for pair in range(pairs) for part in range(count)])
    else:

        @pl.loop(0, pairs)
        def _(pair):
            work([(pair, part) for part in range(count)])


def split_pair(rows):
    lane = lax.broadcasted_iota(jnp.int32, rows.shape, 1)
    zero = jnp.zeros_like(rows)
    return jnp.concatenate(
        [jnp.where(lane < HEAD, rows, zero), jnp.where(lane < HEAD, zero, rows)], axis=0
    )


def merge_pair(columns):
    rows = columns.shape[1] // 2
    row = lax.broadcasted_iota(jnp.int32, (PAIR, rows), 0)
    return jnp.where(row < HEAD, columns[:, :rows], columns[:, rows:]).T


def spread_mask():
    row = lax.broadcasted_iota(jnp.int32, (128 // RANK, 128), 0)
    return row == lax.broadcasted_iota(jnp.int32, (128 // RANK, 128), 1) // RANK


def prepare_kernel(tp_ref, factors_ref, wq_ref, wk_ref, wv_ref, wcat_ref, upq_ref, upv_ref):
    features, width = wq_ref.shape
    flat = features * RANK // 128
    steps = features // 128
    own = tp_ref[0] * (width // 128)
    group = 128 // RANK
    picked = spread_mask()
    lane = lax.broadcasted_iota(jnp.int32, (128, 128), 1)
    row = lax.broadcasted_iota(jnp.int32, (128, 128), 0)
    compact = jnp.zeros((features, 128), F32)
    for which, (w_ref, up_ref) in enumerate(((wq_ref, upq_ref), (wv_ref, upv_ref))):
        held = factors_ref[which * flat : (which + 1) * flat, :].reshape(flat, 1, 128)
        down = jnp.where(picked[None], jnp.broadcast_to(held, (flat, group, 128)), 0.0)
        down = down.reshape(features, 128).astype(BF16)
        base = (2 + which) * flat
        for step in range(width // 128):
            part = factors_ref[pl.ds(base + own + step, RANK, stride=steps), :]
            up_ref[:, step * 128 : (step + 1) * 128] = jnp.concatenate([part] * group).astype(
                BF16
            )
        scale = LOG2E / math.sqrt(HEAD) if which == 0 else 1.0
        combined = w_ref[...].astype(F32) + ADAPTER_SCALE * nn(down, up_ref[...])
        at = which * 2 * width
        wcat_ref[:, at : at + width] = (combined * scale).astype(BF16)
        choose = jnp.where(lane == which * RANK + row % RANK, 1.0, 0.0).astype(BF16)
        compact = compact + nn(down, choose)
    wcat_ref[:, width : 2 * width] = wk_ref[...]
    wcat_ref[:, 3 * width :] = compact.astype(BF16)


def prepare(tp, factors, wq, wk, wv):
    features, width = wq.shape
    return pl.pallas_call(
        prepare_kernel,
        out_shape=[
            shape_of((features, 3 * width + 128), BF16),
            shape_of((128, width), BF16),
            shape_of((128, width), BF16),
        ],
        in_specs=[SMEM] + [VMEM] * 4,
        out_specs=[VMEM] * 3,
        compiler_params=params(56),
        cost_estimate=pl.CostEstimate(
            flops=4 * 128 * features * width, bytes_accessed=9 * features * width, transcendentals=0
        ),
        name="prepare",
    )(tp, factors, wq, wk, wv)


def forward_kernel(
    longest,
    tp_ref,
    lengths_ref,
    xown_ref,
    xoth_ref,
    wcat_ref,
    qkv_out,
    mid_out,
    keep_out,
    send_out,
    lse_ref,
    x_buf,
    qkv_buf,
    mid_buf,
    att_buf,
    vt_buf,
    p_buf,
    in_sem,
    out_sem,
):
    rows, width = xown_ref.shape
    half = rows // 2
    pairs = width // PAIR
    me = tp_ref[0]
    mine = pl.ds(pl.multiple_of(me * width, 128), width)
    theirs = pl.ds(pl.multiple_of((1 - me) * width, 128), width)
    copy = pltpu.make_async_copy
    block = min(512, rows)
    blocks = rows // block

    def loads(index):
        at = pl.ds(pl.multiple_of(index * block, block), block)
        return [
            copy(xown_ref.at[at], x_buf.at[at, mine], in_sem.at[0, index]),
            copy(xoth_ref.at[at], x_buf.at[at, theirs], in_sem.at[1, index]),
        ]

    def stores(index):
        at = pl.ds(pl.multiple_of(index * block, block), block)
        return [
            copy(qkv_buf.at[at], qkv_out.at[at], out_sem.at[0, index]),
            copy(mid_buf.at[at], mid_out.at[at], out_sem.at[1, index]),
        ]

    for index in range(blocks):
        start_all(loads(index))
    qkv_buf[rows:, :] = jnp.zeros((qkv_buf.shape[0] - rows, 3 * width), BF16)
    lse_ref[...] = jnp.full(lse_ref.shape, -MASKED, F32)

    @pl.loop(0, blocks)
    def _(index):
        at = pl.ds(pl.multiple_of(index * block, block), block)
        wait_all(loads(index))
        features = x_buf[at, :]
        for low in range(0, 3 * width, 256):
            high = min(low + 256, wcat_ref.shape[1])
            part = nn(features, wcat_ref[:, low:high]).astype(BF16)
            inner = min(high, 3 * width) - low
            qkv_buf[at, low : low + inner] = part[:, :inner]
            if inner < high - low:
                mid_buf[at, :] = part[:, inner:]
        start_all(stores(index))

    def visit(count, start, first, end, tile):
        window = window_of(count, longest)
        sizes = [tile_rows(count, part, window) for part in range(count)]
        covered = sum(sizes)
        keys_at = pl.ds(start, window)

        def score(pair, part):
            if part == 0:
                vt_buf[pair, :, :window] = qkv_buf[keys_at, pair_columns(pair, 2 * width)].T
            low = pl.multiple_of(start + part * TILE, ALIGN)
            queries = split_pair(qkv_buf[pl.ds(low, sizes[part]), pair_columns(pair)])
            return nt(qkv_buf[keys_at, pair_columns(pair, width)], queries)

        inverse = {}

        def weigh(pair, part, scores):
            low = start + part * TILE
            scores = key_rows_masked(scores, start, first, end, MASKED)
            top = jnp.max(scores, axis=0, keepdims=True)
            weights = jnp.exp2(scores - top)
            total = jnp.sum(weights, axis=0, keepdims=True)
            p_buf[pair, :window, tile_lanes(part, sizes[part])] = weights.astype(BF16)
            inverse[part if count > TOGETHER else (pair, part)] = 1.0 / total
            lane = lax.broadcasted_iota(jnp.int32, total.shape, 1)
            spot = low + jnp.where(lane < sizes[part], lane, lane - sizes[part])
            spread = jnp.where((spot >= first) & (spot < end), top + jnp.log2(total), -MASKED)
            if sizes[part] < TILE:
                rest = jnp.full((1, 2 * (TILE - sizes[part])), -MASKED, F32)
                spread = jnp.concatenate([spread, rest], axis=1)
            lse_ref[pair, pl.ds(tile + part, 1), :] = spread

        def finish(pair):
            columns = nn(vt_buf[pair, :, :window], p_buf[pair, :window, : 2 * covered])
            merged = [
                merge_pair(
                    columns[:, tile_lanes(part, sizes[part])]
                    * inverse[part if count > TOGETHER else (pair, part)]
                )
                for part in range(count)
            ]
            merged = jnp.concatenate(merged, axis=0)[:window]
            store_window(att_buf, pair_columns(pair), merged, start, first, end)

        run_staged(pairs, count, score, weigh, finish)

    for_each_sentence(lengths_ref, longest, rows, rows, lambda index: None, visit)
    mine_rows = pl.ds(pl.multiple_of(me * half, half), half)
    their_rows = pl.ds(pl.multiple_of((1 - me) * half, half), half)
    last = start_all(
        [
            copy(att_buf.at[their_rows], send_out, out_sem.at[0, blocks]),
            copy(att_buf.at[mine_rows], keep_out, out_sem.at[1, blocks]),
        ]
    )
    for index in range(blocks):
        wait_all(stores(index))
    wait_all(last)


def tiles_at_most(rows, sentences):
    return -(-(rows + sentences * (ALIGN - 1 + TILE - 1)) // TILE)


def widest_window(longest):
    return -(-(longest + ALIGN - 1) // TILE) * TILE


def window_of(count, longest):
    return min(count * TILE, -(-(longest + ALIGN - 1) // ALIGN) * ALIGN)


def tile_rows(count, part, window):
    return TILE // 2 if window - part * TILE <= TILE // 2 else TILE


def tile_lanes(part, rows):
    return slice(part * 2 * TILE, part * 2 * TILE + 2 * rows)


def forward(tp, lengths, x_own, x_oth, wcat, longest):
    rows, width = x_own.shape
    half = rows // 2
    pairs = width // PAIR
    tiles = -(-tiles_at_most(rows, lengths.shape[0]) // 8) * 8
    padded = rows + TILE
    widest = widest_window(longest)
    blocks = rows // min(512, rows)
    return pl.pallas_call(
        functools.partial(forward_kernel, longest),
        out_shape=[
            shape_of((rows, 3 * width), BF16),
            shape_of((rows, 128), BF16),
            shape_of((half, width), BF16),
            pltpu.VMEM((half, width), BF16),
            shape_of((pairs, tiles, 2 * TILE), F32),
        ],
        in_specs=[SMEM, SMEM, ANY, VMEM, VMEM],
        out_specs=[ANY] * 3 + [VMEM] * 2,
        scratch_shapes=[
            pltpu.VMEM((rows, 2 * width), BF16),
            pltpu.VMEM((padded, 3 * width), BF16),
            pltpu.VMEM((rows, 128), BF16),
            pltpu.VMEM((padded, width), BF16),
            pltpu.VMEM((pairs, PAIR, widest), BF16),
            pltpu.VMEM((pairs, widest, 2 * widest), BF16),
            pltpu.SemaphoreType.DMA((2, blocks)),
            pltpu.SemaphoreType.DMA((2, blocks + 1)),
        ],
        compiler_params=params(56),
        cost_estimate=pl.CostEstimate(
            flops=20 * rows * width * width, bytes_accessed=14 * rows * width, transcendentals=0
        ),
        name="forward",
    )(tp, lengths, x_own, x_oth, wcat)


def cdf_and_slope(upper):
    below = 0.5 + 0.5 * lax.erf(upper * math.sqrt(0.5))
    bell = jnp.exp2(upper * upper * (-0.5 * LOG2E))
    return below, below + upper * bell * (1.0 / math.sqrt(2.0 * math.pi))


def row_mean(values):
    return jnp.mean(values, axis=-1, keepdims=True)


def norm_pull(scale, normed, pulled):
    return scale * (pulled - row_mean(pulled) - normed * row_mean(pulled * normed))


BAND = 64


def rows_kernel(
    tp_ref,
    keep_ref,
    recv_ref,
    xown_ref,
    xoth_ref,
    cotown_ref,
    cototh_ref,
    wout_own,
    wout_oth,
    wup_own,
    wup_oth,
    wdown_own,
    wdown_oth,
    gain1_ref,
    shift1_ref,
    gain2_ref,
    shift2_ref,
    enc_out,
    enc_send,
    dres_out,
    datt_keep,
    datt_send,
    att_buf,
    x_buf,
    cot_buf,
    wout_buf,
    wup_buf,
    wdown_buf,
    normed_buf,
    scale_buf,
    low_buf,
    act_buf,
    slope_buf,
    fresh_buf,
    held_buf,
    outer_buf,
    dres_buf,
    enc_buf,
    datt_buf,
    in_sem,
    out_sem,
):
    half, width = keep_ref.shape
    units = wup_own.shape[1]
    me = tp_ref[0]
    mine = pl.ds(pl.multiple_of(me * width, 128), width)
    theirs = pl.ds(pl.multiple_of((1 - me) * width, 128), width)
    own_rows = pl.ds(pl.multiple_of(me * half, half), half)
    copy = pltpu.make_async_copy
    first = start_all(
        [
            copy(wout_own, wout_buf.at[pl.ds(0, width)], in_sem.at[2]),
            copy(wout_oth, wout_buf.at[pl.ds(width, width)], in_sem.at[3]),
            copy(keep_ref, att_buf.at[:, pl.ds(0, width)], in_sem.at[0]),
            copy(recv_ref, att_buf.at[:, pl.ds(width, width)], in_sem.at[1]),
            copy(xown_ref.at[own_rows], x_buf.at[:, mine], in_sem.at[4]),
            copy(xoth_ref.at[own_rows], x_buf.at[:, theirs], in_sem.at[5]),
        ]
    )
    up_loads = (
        [
            copy(wup_own, wup_buf.at[:, pl.ds(0, units)], in_sem.at[6]),
            copy(wup_oth, wup_buf.at[:, pl.ds(units, units)], in_sem.at[7]),
        ]
    )
    down_loads = (
        [
            copy(wdown_own, wdown_buf.at[pl.ds(0, units)], in_sem.at[8]),
            copy(wdown_oth, wdown_buf.at[pl.ds(units, units)], in_sem.at[9]),
        ]
    )
    cot_loads = (
        [
            copy(cotown_ref.at[own_rows], cot_buf.at[:, mine], in_sem.at[10]),
            copy(cototh_ref, cot_buf.at[:, theirs], in_sem.at[11]),
        ]
    )
    gain1, shift1, gain2, shift2 = (
        ref[...].reshape(1, 2 * width) for ref in (gain1_ref, shift1_ref, gain2_ref, shift2_ref)
    )
    block = min(256, half)
    blocks = half // block
    chunk = min(768, units)
    chunks = 2 * units // chunk
    features = 2 * width
    strips = [slice(low, low + 256) for low in range(0, features, 256)]
    sides = [slice(0, width), slice(width, features)]
    bands = [slice(low, low + BAND) for low in range(0, block, BAND)]

    def rows_of(index):
        return pl.ds(pl.multiple_of(index * block, block), block)

    def band_of(index, band):
        return pl.ds(pl.multiple_of(index * block + band.start, BAND), BAND)

    def cols_of(part):
        return pl.ds(pl.multiple_of(part * chunk, chunk), chunk)

    def mix(index, strip):
        at = rows_of(index)
        fresh_buf[:, strip] = x_buf[at, strip].astype(F32) + nn(att_buf[at, :], wout_buf[:, strip])

    def first_norm(index, band):
        at = band_of(index, band)
        resid = held_buf[band, :]
        centered = resid - row_mean(resid)
        scale = lax.rsqrt(row_mean(centered * centered) + EPS_NORM)
        normed = centered * scale
        scale_buf[at, :] = scale
        normed_buf[at, :] = normed
        low_buf[at, :] = (normed * gain1 + shift1).astype(BF16)

    def widen(part):
        cols = cols_of(part)
        upper = nn(low_buf[...], wup_buf[:, cols])
        below, slope = cdf_and_slope(upper)
        act_buf[:, cols] = (upper * below).astype(BF16)
        slope_buf[:, cols] = slope.astype(BF16)

    def narrow(index, strip):
        at = rows_of(index)
        hidden = normed_buf[at, strip] * gain1[:, strip] + shift1[:, strip]
        fresh_buf[:, strip] = hidden + nn(act_buf[at, :], wdown_buf[:, strip])

    def second_norm(index, band):
        at = band_of(index, band)
        outer = held_buf[band, :]
        centered = outer - row_mean(outer)
        scale = lax.rsqrt(row_mean(centered * centered) + EPS_NORM)
        normed = centered * scale
        enc_buf[at, :] = (normed * gain2 + shift2).astype(BF16)
        d_outer = norm_pull(scale, normed, cot_buf[at, :].astype(F32) * gain2)
        outer_buf[at, :] = d_outer
        low_buf[at, :] = d_outer.astype(BF16)

    def widen_back(part):
        cols = cols_of(part)
        d_act = nt(low_buf[...], wdown_buf[cols, :])
        act_buf[:, cols] = (d_act * slope_buf[:, cols].astype(F32)).astype(BF16)

    def narrow_back(index, strip):
        at = rows_of(index)
        fresh_buf[:, strip] = outer_buf[at, strip] + nt(act_buf[at, :], wup_buf[strip, :])

    def first_norm_back(index, band):
        at = band_of(index, band)
        d_res = norm_pull(scale_buf[at, :], normed_buf[at, :], held_buf[band, :] * gain1)
        dres_buf[at, :] = d_res.astype(BF16)

    def unmix(strip):
        datt_buf[:, strip] = nt(dres_buf[...], wout_buf[strip, :]).astype(BF16)

    def step(at, product, norm):
        held_buf[...] = fresh_buf[...]
        for turn in range(max(len(strips), len(bands))):
            if product is not None and turn < len(strips):
                product(at, strips[turn])
            if turn < len(bands):
                norm(jnp.maximum(at - 1, 0), bands[turn])

    def staggered(product, norm):
        @pl.loop(0, blocks)
        def _(at):
            step(at, product, norm)

        step(blocks, None, norm)

    wait_all(first)
    start_all(up_loads)
    start_all(down_loads)
    start_all(cot_loads)
    staggered(mix, first_norm)
    wait_all(up_loads)
    pl.loop(0, chunks)(widen)
    wait_all(down_loads)
    wait_all(cot_loads)
    staggered(narrow, second_norm)
    enc_stores = start_all(
        [
            copy(enc_buf.at[:, theirs], enc_send, out_sem.at[3]),
            copy(enc_buf.at[:, mine], enc_out.at[own_rows], out_sem.at[4]),
        ]
    )
    pl.loop(0, chunks)(widen_back)
    staggered(narrow_back, first_norm_back)
    last = start_all([copy(dres_buf, dres_out, out_sem.at[2])])
    unmix(sides[1])
    last += start_all([copy(datt_buf.at[:, pl.ds(width, width)], datt_send, out_sem.at[0])])
    unmix(sides[0])
    last += start_all([copy(datt_buf.at[:, pl.ds(0, width)], datt_keep, out_sem.at[1])])
    wait_all(last)
    wait_all(enc_stores)


def rows_step(tp, keep, recv, x_own, x_oth, cot_own, cot_oth, weights, norms):
    half, width = keep.shape
    units = weights[2].shape[1]
    block = min(256, half)
    return pl.pallas_call(
        rows_kernel,
        out_shape=[
            shape_of((2 * half, width), BF16),
            shape_of((half, width), BF16),
            shape_of((half, 2 * width), BF16),
            shape_of((half, width), BF16),
            pltpu.VMEM((half, width), BF16),
        ],
        in_specs=[SMEM, ANY, VMEM, ANY, VMEM, ANY, VMEM, ANY, VMEM] + [ANY] * 4 + [VMEM] * 4,
        out_specs=[ANY] * 4 + [VMEM],
        scratch_shapes=[
            pltpu.VMEM((half, 2 * width), BF16),
            pltpu.VMEM((half, 2 * width), BF16),
            pltpu.VMEM((half, 2 * width), BF16),
            pltpu.VMEM((2 * width, 2 * width), BF16),
            pltpu.VMEM((2 * width, 2 * units), BF16),
            pltpu.VMEM((2 * units, 2 * width), BF16),
            pltpu.VMEM((half, 2 * width), F32),
            pltpu.VMEM((half, 1), F32),
            pltpu.VMEM((half, 2 * width), BF16),
            pltpu.VMEM((half, 2 * units), BF16),
            pltpu.VMEM((half, 2 * units), BF16),
            pltpu.VMEM((block, 2 * width), F32),
            pltpu.VMEM((block, 2 * width), F32),
            pltpu.VMEM((half, 2 * width), F32),
            pltpu.VMEM((half, 2 * width), BF16),
            pltpu.VMEM((half, 2 * width), BF16),
            pltpu.VMEM((half, 2 * width), BF16),
            pltpu.SemaphoreType.DMA((12,)),
            pltpu.SemaphoreType.DMA((5,)),
        ],
        compiler_params=params(56),
        cost_estimate=pl.CostEstimate(
            flops=2 * half * (4 * width * (2 * width + 4 * units)),
            bytes_accessed=24 * half * width,
            transcendentals=0,
        ),
        name="rows_step",
    )(tp, keep, recv, x_own, x_oth, cot_own, cot_oth, *weights, *norms)


def backward_kernel(
    longest,
    tp_ref,
    lengths_ref,
    qkv_ref,
    dkeep_ref,
    drecv_ref,
    xown_ref,
    xoth_ref,
    mid_ref,
    lse_ref,
    upq_ref,
    upv_ref,
    wcat_ref,
    dres_ref,
    tok_keep_out,
    tok_send_out,
    keep_ref,
    send_ref,
    qkv_buf,
    do_buf,
    x_buf,
    mid_buf,
    d_buf,
    kt_buf,
    q_split,
    do_split,
    p_buf,
    ds_buf,
    grad_ref,
    wcat_buf,
    dres_buf,
    tok_keep_buf,
    tok_send_buf,
    in_sem,
    late_sem,
    out_sem,
):
    half, width = dkeep_ref.shape
    rows = 2 * half
    pairs = width // PAIR
    me = tp_ref[0]
    mine = pl.ds(pl.multiple_of(me * width, 128), width)
    theirs = pl.ds(pl.multiple_of((1 - me) * width, 128), width)
    copy = pltpu.make_async_copy
    block = min(512, half)
    blocks = rows // block

    def block_rows(index):
        return pl.ds(pl.multiple_of(index * block, block), block)

    def d_load(ref, part, index):
        return copy(ref.at[block_rows(part)], do_buf.at[block_rows(index)], in_sem.at[1, index])

    def qkv_load(index):
        at = block_rows(index)
        return copy(qkv_ref.at[at], qkv_buf.at[at], in_sem.at[0, index])

    for index in range(blocks):
        qkv_load(index).start()
        if index < blocks // 2:
            d_load(dkeep_ref, index, me * (blocks // 2) + index).start()
            d_load(drecv_ref, index, (1 - me) * (blocks // 2) + index).start()
    late = start_all(
        [
            copy(xown_ref, x_buf.at[:, mine], late_sem.at[0]),
            copy(xoth_ref, x_buf.at[:, theirs], late_sem.at[1]),
            copy(mid_ref, mid_buf, late_sem.at[2]),
            copy(wcat_ref, wcat_buf, late_sem.at[3]),
            copy(dres_ref, dres_buf, late_sem.at[4]),
        ]
    )
    for buf in (qkv_buf, do_buf):
        buf[rows:, :] = jnp.zeros((buf.shape[0] - rows, buf.shape[1]), BF16)

    def await_chunk(index):
        qkv_load(index).wait()
        d_load(dkeep_ref, 0, index).wait()

    def visit(count, start, first, end, tile):
        window = window_of(count, longest)
        sizes = [tile_rows(count, part, window) for part in range(count)]
        covered = sum(sizes)
        keys_at = pl.ds(start, window)

        def lanes(part):
            return tile_lanes(part, sizes[part])

        def score(pair, part):
            keys = qkv_buf[keys_at, pair_columns(pair, width)]
            if part == 0:
                kt_buf[pair, :, :window] = keys.T
            at = pl.ds(pl.multiple_of(start + part * TILE, ALIGN), sizes[part])
            queries = split_pair(qkv_buf[at, pair_columns(pair)])
            d_rows = split_pair(do_buf[at, pair_columns(pair)])
            q_split[pair, lanes(part), :] = queries
            do_split[pair, lanes(part), :] = d_rows
            return (
                nt(keys, queries),
                nt(qkv_buf[keys_at, pair_columns(pair, 2 * width)], d_rows),
            )

        def weigh(pair, part, scored):
            scores, d_probs = scored
            probs = jnp.exp2(scores - lse_ref[pair, pl.ds(tile + part, 1), :][:, : 2 * sizes[part]])
            probs = key_rows_masked(probs, start, first, end, 0.0)
            product = probs * d_probs
            delta = jnp.sum(product, axis=0, keepdims=True)
            p_buf[pair, :window, lanes(part)] = probs.astype(BF16)
            ds_buf[pair, :window, lanes(part)] = (product - probs * delta).astype(BF16)

        def finish(pair):
            every = slice(0, 2 * covered)
            d_scores = ds_buf[pair, :window, every]
            d_values = nn(p_buf[pair, :window, every], do_split[pair, every, :])
            d_keys = nn(d_scores, q_split[pair, every, :]) * LN2
            columns = nn(kt_buf[pair, :, :window], d_scores) * LN2
            d_queries = jnp.concatenate(
                [merge_pair(columns[:, lanes(part)]) for part in range(count)], axis=0
            )[:window]
            for base, values in enumerate((d_queries, d_keys, d_values)):
                store_window(d_buf, pair_columns(pair, base * width), values, start, first, end)

        run_staged(pairs, count, score, weigh, finish)

    for_each_sentence(lengths_ref, longest, rows, block, await_chunk, visit)
    wait_all(late)

    def token_stores(index):
        at = block_rows(index)
        return [
            copy(tok_send_buf.at[at], tok_send_out.at[at], out_sem.at[0, index]),
            copy(tok_keep_buf.at[at], tok_keep_out.at[at], out_sem.at[1, index]),
        ]

    @pl.loop(0, blocks)
    def _(index):
        at = block_rows(index)
        total = nt(d_buf[at, :], wcat_buf[:, : 3 * width])
        low, high = total[:, :width], total[:, width:]
        tok_keep_buf[at, :] = jnp.where(me == 0, low, high)
        tok_send_buf[at, :] = jnp.where(me == 0, high, low).astype(BF16)

        @pl.when(index // (blocks // 2) == me)
        def _():
            resid = dres_buf[block_rows(lax.rem(index, blocks // 2)), :].astype(F32)
            low, high = resid[:, :width], resid[:, width:]
            tok_keep_buf[at, :] += jnp.where(me == 0, low, high)
            sent = tok_send_buf[at, :].astype(F32) + jnp.where(me == 0, high, low)
            tok_send_buf[at, :] = sent.astype(BF16)

        start_all(token_stores(index))

    d_query = d_buf[:rows, :width]
    d_value = d_buf[:rows, 2 * width :]
    mid = mid_buf[...]
    picked = spread_mask()
    features = 2 * width
    flat = features * RANK // 128
    steps = features // 128
    natural = ADAPTER_SCALE / (math.sqrt(HEAD) * LN2)
    for which, (grads, up_ref, scale) in enumerate(
        ((d_query, upq_ref, natural), (d_value, upv_ref, ADAPTER_SCALE))
    ):
        d_mid = (nt(up_ref[...], grads) * scale).astype(BF16)
        down = nn(d_mid, x_buf[...]).T
        down = jnp.where(picked[None], down.reshape(flat, 128 // RANK, 128), 0.0)
        grad_ref[pl.ds(which * flat, flat), :] = jnp.sum(down, axis=1)
        up = tn(mid, grads)[which * RANK : (which + 1) * RANK] * scale
        base = (2 + which) * flat
        own = me * (width // 128)
        other = (1 - me) * (width // 128)
        for step in range(width // 128):
            part = up[:, step * 128 : (step + 1) * 128]
            grad_ref[pl.ds(base + own + step, RANK, stride=steps), :] = part
            grad_ref[pl.ds(base + other + step, RANK, stride=steps), :] = jnp.zeros_like(part)
    share = keep_ref.shape[0]
    keep_ref[...] = grad_ref[pl.ds(pl.multiple_of(me * share, 8), share), :]
    send_ref[...] = grad_ref[pl.ds(pl.multiple_of((1 - me) * share, 8), share), :]
    for index in range(blocks):
        wait_all(token_stores(index))


def backward(
    tp, lengths, qkv, d_keep, d_recv, x_own, x_oth, mid, lse, up_q, up_v, wcat, dres, longest
):
    half, width = d_keep.shape
    rows = 2 * half
    pairs = width // PAIR
    padded = rows + TILE
    widest = widest_window(longest)
    blocks = rows // min(512, half)
    return pl.pallas_call(
        functools.partial(backward_kernel, longest),
        out_shape=[
            shape_of((rows, width), F32),
            shape_of((rows, width), BF16),
            pltpu.VMEM((4 * width * RANK // 128, 128), F32),
            pltpu.VMEM((4 * width * RANK // 128, 128), F32),
        ],
        in_specs=[SMEM, SMEM, ANY, ANY, VMEM, ANY, VMEM, ANY] + [VMEM] * 3 + [ANY] * 2,
        out_specs=[ANY, ANY, VMEM, VMEM],
        scratch_shapes=[
            pltpu.VMEM((padded, 3 * width), BF16),
            pltpu.VMEM((padded, width), BF16),
            pltpu.VMEM((rows, 2 * width), BF16),
            pltpu.VMEM((rows, 128), BF16),
            pltpu.VMEM((padded, 3 * width), BF16),
            pltpu.VMEM((pairs, PAIR, widest), BF16),
            pltpu.VMEM((pairs, 2 * widest, PAIR), BF16),
            pltpu.VMEM((pairs, 2 * widest, PAIR), BF16),
            pltpu.VMEM((pairs, widest, 2 * widest), BF16),
            pltpu.VMEM((pairs, widest, 2 * widest), BF16),
            pltpu.VMEM((8 * width * RANK // 128, 128), F32),
            pltpu.VMEM(wcat.shape, BF16),
            pltpu.VMEM((half, 2 * width), BF16),
            pltpu.VMEM((rows, width), F32),
            pltpu.VMEM((rows, width), BF16),
            pltpu.SemaphoreType.DMA((2, blocks)),
            pltpu.SemaphoreType.DMA((5,)),
            pltpu.SemaphoreType.DMA((2, blocks)),
        ],
        compiler_params=params(56),
        cost_estimate=pl.CostEstimate(
            flops=30 * rows * width * width, bytes_accessed=20 * rows * width, transcendentals=0
        ),
        name="backward",
    )(tp, lengths, qkv, d_keep, d_recv, x_own, x_oth, mid, lse, up_q, up_v, wcat, dres)


def adam_update(gradient, moment_one, moment_two, weights, rates):
    first_new = BETA_ONE * moment_one + (1.0 - BETA_ONE) * gradient
    second_new = BETA_TWO * moment_two + (1.0 - BETA_TWO) * gradient * gradient
    update = first_new / BIAS_ONE / (jnp.sqrt(second_new / BIAS_TWO) + EPS_ADAM)
    return first_new, second_new, weights - rates * (update + DECAY_RATE * weights)


def exchange_groups(size):
    step = 1
    while step < size:
        if step * 2 < size:
            yield step, [step, 2 * step, 3 * step]
            step *= 4
        else:
            yield step, [step]
            step *= 2


def partners(values, size, offsets):
    return [
        lax.ppermute(values, "dp", [(i, i ^ offset) for i in range(size)]) for offset in offsets
    ]


def joined(total, moments, others, index):
    rows = total.shape[0]
    sums = [other[:rows] for other in others]
    parts = [moments] + [other[rows:] for other in others]
    if len(sums) == 3:
        total = (total + sums[0]) + (sums[1] + sums[2])
    else:
        total = total + sums[0]
    count = len(parts)
    ordered = [
        functools.reduce(
            lambda held, offset: jnp.where(index == offset, parts[spot ^ offset], held),
            range(1, count),
            parts[spot],
        )
        for spot in range(count)
    ]
    return total, jnp.concatenate(ordered, axis=0)


def in_order(mine, other, me):
    return jnp.where(
        me == 0, jnp.concatenate([mine, other], axis=0), jnp.concatenate([other, mine], axis=0)
    )


def in_vmem(values):
    return pltpu.with_memory_space_constraint(values, pltpu.VMEM)


def tied(*values):
    return lax.optimization_barrier(values)


def swap(values):
    return lax.ppermute(values, "tp", [(0, 1), (1, 0)])


def body(
    tokens,
    lengths,
    query_weight,
    w_key,
    value_weight,
    w_out,
    w_up,
    w_down,
    gain_attn,
    shift_attn,
    gain_ffn,
    shift_ffn,
    factors,
    first_moment,
    second_moment,
    cotangent,
):
    rows, width = tokens.shape
    features = 2 * width
    half = rows // 2
    longest = min(512, rows)
    me = lax.axis_index("tp")
    tp = me.astype(jnp.int32).reshape(1)
    dp_size = lax.axis_size("dp")
    other_rows = (1 - me) * half
    size_down = features * RANK
    own_lengths = lengths.reshape(-1)

    share = first_moment.shape[0]
    share_rows = -(-2 * share // 128)

    x_oth = swap(tokens)
    cot_oth = swap(lax.dynamic_slice_in_dim(cotangent, other_rows, half, 0))
    out_oth = swap(w_out)
    wcat, up_q, up_v = prepare(tp, factors.reshape(-1, 128), query_weight, w_key, value_weight)
    x_oth, cot_oth, out_oth, wcat, w_up_late, w_down_late = tied(
        x_oth, cot_oth, out_oth, wcat, w_up, w_down
    )
    up_oth, down_oth = swap(w_up_late), swap(w_down_late)
    cot_oth, out_oth, x_oth = in_vmem(cot_oth), in_vmem(out_oth), in_vmem(x_oth)

    qkv, mid, att_keep, att_send, lse = forward(
        tp, own_lengths, tokens, x_oth, wcat, longest
    )
    att_recv = in_vmem(swap(att_send))
    moments = jnp.concatenate([first_moment, second_moment])
    moments = jnp.pad(moments, (0, share_rows * 128 - 2 * share)).reshape(share_rows, 128)
    encoded, enc_send, dres, datt_keep, datt_send = rows_step(
        tp,
        att_keep,
        att_recv,
        tokens,
        x_oth,
        cotangent,
        cot_oth,
        (w_out, out_oth, w_up, up_oth, w_down, down_oth),
        (gain_attn, shift_attn, gain_ffn, shift_ffn),
    )
    datt_recv = in_vmem(swap(datt_send))
    enc_recv = swap(enc_send)
    tok_keep, tok_send, grad_keep, grad_send = backward(
        tp,
        own_lengths,
        qkv,
        datt_keep,
        datt_recv,
        tokens,
        x_oth,
        mid,
        lse,
        up_q,
        up_v,
        wcat,
        dres,
        longest,
    )
    grad_send, enc_recv = tied(grad_send, enc_recv)
    total = grad_keep + swap(grad_send)
    total, tok_send = tied(total, tok_send)
    tok_recv = swap(tok_send)
    encoded = lax.dynamic_update_slice(encoded, enc_recv, (other_rows, 0))
    d_tokens = tok_keep + tok_recv.astype(F32)
    place = lax.axis_index("dp")
    for turn, (step, offsets) in enumerate(exchange_groups(dp_size)):
        others = partners(jnp.concatenate([total, moments], axis=0), dp_size, offsets)
        if turn == 0:
            others, encoded = tied(others, encoded)
        elif turn == 1:
            others, d_tokens = tied(others, d_tokens)
        total, moments = joined(total, moments, others, (place // step) % (len(offsets) + 1))
    mine = jnp.concatenate([total, moments], axis=0)
    other = swap(mine)
    half_rows = total.shape[0]
    total = in_order(mine[:half_rows], other[:half_rows], me)
    moments = jnp.where(
        me == 0, jnp.stack([mine, other]), jnp.stack([other, mine])
    )[:, half_rows:].reshape(2, dp_size, -1)[:, :, : 2 * share]
    moments = jnp.swapaxes(moments, 0, 1).reshape(2 * dp_size, 2, share)

    gradient = total.reshape(-1) * (1.0 / math.sqrt(rows * dp_size))
    place = jnp.arange(gradient.shape[0], dtype=jnp.int32)
    rates = jnp.where(place < 2 * size_down, RATE_DOWN, RATE_DOWN * RATE_RATIO)
    _, _, factors_new = adam_update(
        gradient, moments[:, 0].reshape(-1), moments[:, 1].reshape(-1), factors, rates
    )
    share_start = lax.axis_index(("dp", "tp")) * share
    grad_share = lax.dynamic_slice_in_dim(gradient, share_start, share)
    first_new, second_new, _ = adam_update(grad_share, first_moment, second_moment, 0.0, 0.0)
    return encoded, d_tokens, grad_share, first_new, second_new, factors_new


def solution(mesh):
    placed = (
        P("dp", "tp"),
        P("dp", None),
        P(None, "tp"),
        P(None, "tp"),
        P(None, "tp"),
        P("tp", None),
        P(None, "tp"),
        P("tp", None),
        P(),
        P(),
        P(),
        P(),
        P(),
        P(("dp", "tp")),
        P(("dp", "tp")),
        P("dp", "tp"),
    )
    return jax.shard_map(
        body,
        mesh=mesh,
        in_specs=placed,
        out_specs=(
            P("dp", "tp"),
            P("dp", "tp"),
            P(("dp", "tp")),
            P(("dp", "tp")),
            P(("dp", "tp")),
            P(),
        ),
        check_vma=False,
    )
```

```python
import functools
import math

import jax
import jax.numpy as jnp
from jax import lax
from jax.experimental import pallas as pl
from jax.experimental.pallas import tpu as pltpu
from jax.sharding import PartitionSpec as P

HEAD = 64
RANK = 8
EPS_NORM = 1e-05
EPS_ADAM = 1e-08
BETA_ONE = 0.9
BETA_TWO = 0.999
BIAS_ONE = 1.0 - 0.9**10
BIAS_TWO = 1.0 - 0.999**10
RATE_DOWN = 0.002
RATE_RATIO = 16.0
DECAY_RATE = 0.01
ADAPTER_SCALE = 2.0
MASKED = -1e30
LOG2E = 1.4426950408889634
LN2 = 0.6931471805599453

TILE = 128
ALIGN = 16
PAIR = 2 * HEAD
BF16 = jnp.bfloat16
F32 = jnp.float32

ANY = pl.BlockSpec(memory_space=pl.ANY)
SMEM = pl.BlockSpec(memory_space=pltpu.SMEM)
VMEM = pl.BlockSpec(memory_space=pltpu.VMEM)


def shape_of(dims, kind):
    return jax.ShapeDtypeStruct(dims, kind)


def params(mib):
    return pltpu.CompilerParams(vmem_limit_bytes=mib * 1024 * 1024)


def nn(left, right):
    return lax.dot_general(left, right, (((1,), (0,)), ((), ())), preferred_element_type=F32)


def nt(left, right):
    return lax.dot_general(left, right, (((1,), (1,)), ((), ())), preferred_element_type=F32)


def tn(left, right):
    return lax.dot_general(left, right, (((0,), (0,)), ((), ())), preferred_element_type=F32)


def start_all(copies):
    for copy in copies:
        copy.start()
    return copies


def wait_all(copies):
    for copy in copies:
        copy.wait()


def for_each_sentence(lengths_ref, longest, rows, chunk, await_chunk, visit):
    def one(index, carry):
        first, tile, loaded = carry
        end = first + lengths_ref[index]
        start = pl.multiple_of((first // ALIGN) * ALIGN, ALIGN)
        steps = (end - start + (TILE - 1)) // TILE
        needed = jnp.minimum((start + steps * TILE + chunk - 1) // chunk, rows // chunk)
        loaded = await_chunks(loaded, needed)
        for count in range(1, (longest + ALIGN - 1 + TILE - 1) // TILE + 1):

            @pl.when(steps == count)
            def _():
                visit(count, start, first, end, tile)

        return end, tile + steps, loaded

    def await_chunks(loaded, needed):
        def one_chunk(index, _):
            await_chunk(index)
            return 0

        lax.fori_loop(loaded, needed, one_chunk, 0)
        return jnp.maximum(loaded, needed)

    zero = jnp.int32(0)
    carry = lax.fori_loop(0, lengths_ref.shape[0], one, (zero, zero, zero))
    await_chunks(carry[2], jnp.int32(rows // chunk))


def window_parts(window, start, first, end):
    def mask(low, high, lanes):
        rows = low + lax.broadcasted_iota(jnp.int32, (high - low, lanes), 0)
        return (rows >= first - start) & (rows < end - start)

    if window <= TILE:
        return [(0, window, mask)]
    whole = (window - 1) // TILE * TILE
    return [(0, ALIGN, mask), (ALIGN, whole, None), (whole, window, mask)]


def key_rows_masked(values, start, first, end, fill):
    window, lanes = values.shape
    return jnp.concatenate(
        [
            values[low:high]
            if mask is None
            else jnp.where(mask(low, high, lanes), values[low:high], fill)
            for low, high, mask in window_parts(window, start, first, end)
        ],
        axis=0,
    )


def store_window(ref, cols, values, start, first, end):
    window, lanes = values.shape
    for low, high, mask in window_parts(window, start, first, end):
        at = pl.ds(pl.multiple_of(start + low, ALIGN), high - low)
        part = values[low:high]
        if mask is not None:
            part = jnp.where(mask(low, high, lanes), part, ref[at, cols].astype(F32))
        ref[at, cols] = part.astype(BF16)


def pair_columns(pair, base=0):
    return pl.ds(pl.multiple_of(base + pair * PAIR, PAIR), PAIR)


DEPTH = 2
TOGETHER = 4


def run_staged(pairs, count, score, weigh, finish):
    def work(units):
        scored = {}
        for step in range(len(units) + DEPTH):
            if step < len(units):
                scored[step] = score(*units[step])
            if step >= DEPTH:
                pair, part = units[step - DEPTH]
                weigh(pair, part, scored.pop(step - DEPTH))
                if part == count - 1:
                    finish(pair)

    if count <= TOGETHER:
        work([(pair, part) for pair in range(pairs) for part in range(count)])
    else:

        @pl.loop(0, pairs)
        def _(pair):
            work([(pair, part) for part in range(count)])


def split_pair(rows):
    lane = lax.broadcasted_iota(jnp.int32, rows.shape, 1)
    zero = jnp.zeros_like(rows)
    return jnp.concatenate(
        [jnp.where(lane < HEAD, rows, zero), jnp.where(lane < HEAD, zero, rows)], axis=0
    )


def merge_pair(columns):
    rows = columns.shape[1] // 2
    row = lax.broadcasted_iota(jnp.int32, (PAIR, rows), 0)
    return jnp.where(row < HEAD, columns[:, :rows], columns[:, rows:]).T


def spread_mask():
    row = lax.broadcasted_iota(jnp.int32, (128 // RANK, 128), 0)
    return row == lax.broadcasted_iota(jnp.int32, (128 // RANK, 128), 1) // RANK


def prepare_kernel(tp_ref, factors_ref, wq_ref, wk_ref, wv_ref, wcat_ref, upq_ref, upv_ref):
    features, width = wq_ref.shape
    flat = features * RANK // 128
    steps = features // 128
    own = tp_ref[0] * (width // 128)
    group = 128 // RANK
    picked = spread_mask()
    lane = lax.broadcasted_iota(jnp.int32, (128, 128), 1)
    row = lax.broadcasted_iota(jnp.int32, (128, 128), 0)
    compact = jnp.zeros((features, 128), F32)
    for which, (w_ref, up_ref) in enumerate(((wq_ref, upq_ref), (wv_ref, upv_ref))):
        held = factors_ref[which * flat : (which + 1) * flat, :].reshape(flat, 1, 128)
        down = jnp.where(picked[None], jnp.broadcast_to(held, (flat, group, 128)), 0.0)
        down = down.reshape(features, 128).astype(BF16)
        base = (2 + which) * flat
        for step in range(width // 128):
            part = factors_ref[pl.ds(base + own + step, RANK, stride=steps), :]
            up_ref[:, step * 128 : (step + 1) * 128] = jnp.concatenate([part] * group).astype(
                BF16
            )
        scale = LOG2E / math.sqrt(HEAD) if which == 0 else 1.0
        combined = w_ref[...].astype(F32) + ADAPTER_SCALE * nn(down, up_ref[...])
        at = which * 2 * width
        wcat_ref[:, at : at + width] = (combined * scale).astype(BF16)
        choose = jnp.where(lane == which * RANK + row % RANK, 1.0, 0.0).astype(BF16)
        compact = compact + nn(down, choose)
    wcat_ref[:, width : 2 * width] = wk_ref[...]
    wcat_ref[:, 3 * width :] = compact.astype(BF16)


def prepare(tp, factors, wq, wk, wv):
    features, width = wq.shape
    return pl.pallas_call(
        prepare_kernel,
        out_shape=[
            shape_of((features, 3 * width + 128), BF16),
            shape_of((128, width), BF16),
            shape_of((128, width), BF16),
        ],
        in_specs=[SMEM] + [VMEM] * 4,
        out_specs=[VMEM] * 3,
        compiler_params=params(56),
        cost_estimate=pl.CostEstimate(
            flops=4 * 128 * features * width, bytes_accessed=9 * features * width, transcendentals=0
        ),
        name="prepare",
    )(tp, factors, wq, wk, wv)


def forward_kernel(
    longest,
    tp_ref,
    lengths_ref,
    xown_ref,
    xoth_ref,
    wcat_ref,
    qkv_out,
    mid_out,
    keep_out,
    send_out,
    lse_ref,
    x_buf,
    qkv_buf,
    mid_buf,
    att_buf,
    vt_buf,
    p_buf,
    in_sem,
    out_sem,
):
    rows, width = xown_ref.shape
    half = rows // 2
    pairs = width // PAIR
    me = tp_ref[0]
    mine = pl.ds(pl.multiple_of(me * width, 128), width)
    theirs = pl.ds(pl.multiple_of((1 - me) * width, 128), width)
    copy = pltpu.make_async_copy
    block = min(512, rows)
    blocks = rows // block

    def loads(index):
        at = pl.ds(pl.multiple_of(index * block, block), block)
        return [
            copy(xown_ref.at[at], x_buf.at[at, mine], in_sem.at[0, index]),
            copy(xoth_ref.at[at], x_buf.at[at, theirs], in_sem.at[1, index]),
        ]

    def stores(index):
        at = pl.ds(pl.multiple_of(index * block, block), block)
        return [
            copy(qkv_buf.at[at], qkv_out.at[at], out_sem.at[0, index]),
            copy(mid_buf.at[at], mid_out.at[at], out_sem.at[1, index]),
        ]

    for index in range(blocks):
        start_all(loads(index))
    qkv_buf[rows:, :] = jnp.zeros((qkv_buf.shape[0] - rows, 3 * width), BF16)
    lse_ref[...] = jnp.full(lse_ref.shape, -MASKED, F32)

    @pl.loop(0, blocks)
    def _(index):
        at = pl.ds(pl.multiple_of(index * block, block), block)
        wait_all(loads(index))
        features = x_buf[at, :]
        for low in range(0, 3 * width, 256):
            high = min(low + 256, wcat_ref.shape[1])
            part = nn(features, wcat_ref[:, low:high]).astype(BF16)
            inner = min(high, 3 * width) - low
            qkv_buf[at, low : low + inner] = part[:, :inner]
            if inner < high - low:
                mid_buf[at, :] = part[:, inner:]
        start_all(stores(index))

    def visit(count, start, first, end, tile):
        window = window_of(count, longest)
        sizes = [tile_rows(count, part, window) for part in range(count)]
        covered = sum(sizes)
        keys_at = pl.ds(start, window)

        def score(pair, part):
            if part == 0:
                vt_buf[pair, :, :window] = qkv_buf[keys_at, pair_columns(pair, 2 * width)].T
            low = pl.multiple_of(start + part * TILE, ALIGN)
            queries = split_pair(qkv_buf[pl.ds(low, sizes[part]), pair_columns(pair)])
            return nt(qkv_buf[keys_at, pair_columns(pair, width)], queries)

        inverse = {}

        def weigh(pair, part, scores):
            low = start + part * TILE
            scores = key_rows_masked(scores, start, first, end, MASKED)
            top = jnp.max(scores, axis=0, keepdims=True)
            weights = jnp.exp2(scores - top)
            total = jnp.sum(weights, axis=0, keepdims=True)
            p_buf[pair, :window, tile_lanes(part, sizes[part])] = weights.astype(BF16)
            inverse[part if count > TOGETHER else (pair, part)] = 1.0 / total
            lane = lax.broadcasted_iota(jnp.int32, total.shape, 1)
            spot = low + jnp.where(lane < sizes[part], lane, lane - sizes[part])
            spread = jnp.where((spot >= first) & (spot < end), top + jnp.log2(total), -MASKED)
            if sizes[part] < TILE:
                rest = jnp.full((1, 2 * (TILE - sizes[part])), -MASKED, F32)
                spread = jnp.concatenate([spread, rest], axis=1)
            lse_ref[pair, pl.ds(tile + part, 1), :] = spread

        def finish(pair):
            columns = nn(vt_buf[pair, :, :window], p_buf[pair, :window, : 2 * covered])
            merged = [
                merge_pair(
                    columns[:, tile_lanes(part, sizes[part])]
                    * inverse[part if count > TOGETHER else (pair, part)]
                )
                for part in range(count)
            ]
            merged = jnp.concatenate(merged, axis=0)[:window]
            store_window(att_buf, pair_columns(pair), merged, start, first, end)

        run_staged(pairs, count, score, weigh, finish)

    for_each_sentence(lengths_ref, longest, rows, rows, lambda index: None, visit)
    mine_rows = pl.ds(pl.multiple_of(me * half, half), half)
    their_rows = pl.ds(pl.multiple_of((1 - me) * half, half), half)
    last = start_all(
        [
            copy(att_buf.at[their_rows], send_out, out_sem.at[0, blocks]),
            copy(att_buf.at[mine_rows], keep_out, out_sem.at[1, blocks]),
        ]
    )
    for index in range(blocks):
        wait_all(stores(index))
    wait_all(last)


def tiles_at_most(rows, sentences):
    return -(-(rows + sentences * (ALIGN - 1 + TILE - 1)) // TILE)


def widest_window(longest):
    return -(-(longest + ALIGN - 1) // TILE) * TILE


def window_of(count, longest):
    return min(count * TILE, -(-(longest + ALIGN - 1) // ALIGN) * ALIGN)


def tile_rows(count, part, window):
    return TILE // 2 if window - part * TILE <= TILE // 2 else TILE


def tile_lanes(part, rows):
    return slice(part * 2 * TILE, part * 2 * TILE + 2 * rows)


def forward(tp, lengths, x_own, x_oth, wcat, longest):
    rows, width = x_own.shape
    half = rows // 2
    pairs = width // PAIR
    tiles = -(-tiles_at_most(rows, lengths.shape[0]) // 8) * 8
    padded = rows + TILE
    widest = widest_window(longest)
    blocks = rows // min(512, rows)
    return pl.pallas_call(
        functools.partial(forward_kernel, longest),
        out_shape=[
            shape_of((rows, 3 * width), BF16),
            shape_of((rows, 128), BF16),
            pltpu.VMEM((half, width), BF16),
            pltpu.VMEM((half, width), BF16),
            shape_of((pairs, tiles, 2 * TILE), F32),
        ],
        in_specs=[SMEM, SMEM, ANY, VMEM, VMEM],
        out_specs=[ANY] * 2 + [VMEM] * 3,
        scratch_shapes=[
            pltpu.VMEM((rows, 2 * width), BF16),
            pltpu.VMEM((padded, 3 * width), BF16),
            pltpu.VMEM((rows, 128), BF16),
            pltpu.VMEM((padded, width), BF16),
            pltpu.VMEM((pairs, PAIR, widest), BF16),
            pltpu.VMEM((pairs, widest, 2 * widest), BF16),
            pltpu.SemaphoreType.DMA((2, blocks)),
            pltpu.SemaphoreType.DMA((2, blocks + 1)),
        ],
        compiler_params=params(56),
        cost_estimate=pl.CostEstimate(
            flops=20 * rows * width * width, bytes_accessed=14 * rows * width, transcendentals=0
        ),
        name="forward",
    )(tp, lengths, x_own, x_oth, wcat)


def cdf_and_slope(upper):
    below = 0.5 + 0.5 * lax.erf(upper * math.sqrt(0.5))
    bell = jnp.exp2(upper * upper * (-0.5 * LOG2E))
    return below, below + upper * bell * (1.0 / math.sqrt(2.0 * math.pi))


def row_mean(values):
    return jnp.mean(values, axis=-1, keepdims=True)


def norm_pull(scale, normed, pulled):
    return scale * (pulled - row_mean(pulled) - normed * row_mean(pulled * normed))


BAND = 64


def rows_kernel(
    tp_ref,
    keep_ref,
    recv_ref,
    xown_ref,
    xoth_ref,
    cotown_ref,
    cototh_ref,
    wout_own,
    wout_oth,
    wup_own,
    wup_oth,
    wdown_own,
    wdown_oth,
    gain1_ref,
    shift1_ref,
    gain2_ref,
    shift2_ref,
    enc_out,
    enc_send,
    dres_out,
    datt_keep,
    datt_send,
    att_buf,
    x_buf,
    cot_buf,
    wout_buf,
    wup_buf,
    wdown_buf,
    normed_buf,
    scale_buf,
    low_buf,
    act_buf,
    slope_buf,
    fresh_buf,
    held_buf,
    outer_buf,
    dres_buf,
    enc_buf,
    datt_buf,
    in_sem,
    out_sem,
):
    half, width = keep_ref.shape
    units = wup_own.shape[1]
    me = tp_ref[0]
    mine = pl.ds(pl.multiple_of(me * width, 128), width)
    theirs = pl.ds(pl.multiple_of((1 - me) * width, 128), width)
    own_rows = pl.ds(pl.multiple_of(me * half, half), half)
    copy = pltpu.make_async_copy
    first = start_all(
        [
            copy(wout_own, wout_buf.at[pl.ds(0, width)], in_sem.at[2]),
            copy(wout_oth, wout_buf.at[pl.ds(width, width)], in_sem.at[3]),
            copy(keep_ref, att_buf.at[:, pl.ds(0, width)], in_sem.at[0]),
            copy(recv_ref, att_buf.at[:, pl.ds(width, width)], in_sem.at[1]),
            copy(xown_ref.at[own_rows], x_buf.at[:, mine], in_sem.at[4]),
            copy(xoth_ref.at[own_rows], x_buf.at[:, theirs], in_sem.at[5]),
        ]
    )
    up_loads = (
        [
            copy(wup_own, wup_buf.at[:, pl.ds(0, units)], in_sem.at[6]),
            copy(wup_oth, wup_buf.at[:, pl.ds(units, units)], in_sem.at[7]),
        ]
    )
    down_loads = (
        [
            copy(wdown_own, wdown_buf.at[pl.ds(0, units)], in_sem.at[8]),
            copy(wdown_oth, wdown_buf.at[pl.ds(units, units)], in_sem.at[9]),
        ]
    )
    cot_loads = (
        [
            copy(cotown_ref.at[own_rows], cot_buf.at[:, mine], in_sem.at[10]),
            copy(cototh_ref, cot_buf.at[:, theirs], in_sem.at[11]),
        ]
    )
    gain1, shift1, gain2, shift2 = (
        ref[...].reshape(1, 2 * width) for ref in (gain1_ref, shift1_ref, gain2_ref, shift2_ref)
    )
    block = min(256, half)
    blocks = half // block
    chunk = min(768, units)
    chunks = 2 * units // chunk
    features = 2 * width
    strips = [slice(low, low + 256) for low in range(0, features, 256)]
    sides = [slice(0, width), slice(width, features)]
    bands = [slice(low, low + BAND) for low in range(0, block, BAND)]

    def rows_of(index):
        return pl.ds(pl.multiple_of(index * block, block), block)

    def band_of(index, band):
        return pl.ds(pl.multiple_of(index * block + band.start, BAND), BAND)

    def cols_of(part):
        return pl.ds(pl.multiple_of(part * chunk, chunk), chunk)

    def mix(index, strip):
        at = rows_of(index)
        fresh_buf[:, strip] = x_buf[at, strip].astype(F32) + nn(att_buf[at, :], wout_buf[:, strip])

    def first_norm(index, band):
        at = band_of(index, band)
        resid = held_buf[band, :]
        centered = resid - row_mean(resid)
        scale = lax.rsqrt(row_mean(centered * centered) + EPS_NORM)
        normed = centered * scale
        scale_buf[at, :] = scale
        normed_buf[at, :] = normed
        low_buf[at, :] = (normed * gain1 + shift1).astype(BF16)

    def widen(part):
        cols = cols_of(part)
        upper = nn(low_buf[...], wup_buf[:, cols])
        below, slope = cdf_and_slope(upper)
        act_buf[:, cols] = (upper * below).astype(BF16)
        slope_buf[:, cols] = slope.astype(BF16)

    def narrow(index, strip):
        at = rows_of(index)
        hidden = normed_buf[at, strip] * gain1[:, strip] + shift1[:, strip]
        fresh_buf[:, strip] = hidden + nn(act_buf[at, :], wdown_buf[:, strip])

    def second_norm(index, band):
        at = band_of(index, band)
        outer = held_buf[band, :]
        centered = outer - row_mean(outer)
        scale = lax.rsqrt(row_mean(centered * centered) + EPS_NORM)
        normed = centered * scale
        enc_buf[at, :] = (normed * gain2 + shift2).astype(BF16)
        d_outer = norm_pull(scale, normed, cot_buf[at, :].astype(F32) * gain2)
        outer_buf[at, :] = d_outer
        low_buf[at, :] = d_outer.astype(BF16)

    def widen_back(part):
        cols = cols_of(part)
        d_act = nt(low_buf[...], wdown_buf[cols, :])
        act_buf[:, cols] = (d_act * slope_buf[:, cols].astype(F32)).astype(BF16)

    def narrow_back(index, strip):
        at = rows_of(index)
        fresh_buf[:, strip] = outer_buf[at, strip] + nt(act_buf[at, :], wup_buf[strip, :])

    def first_norm_back(index, band):
        at = band_of(index, band)
        d_res = norm_pull(scale_buf[at, :], normed_buf[at, :], held_buf[band, :] * gain1)
        dres_buf[at, :] = d_res.astype(BF16)

    def unmix(strip):
        datt_buf[:, strip] = nt(dres_buf[...], wout_buf[strip, :]).astype(BF16)

    def step(at, product, norm):
        held_buf[...] = fresh_buf[...]
        for turn in range(max(len(strips), len(bands))):
            if product is not None and turn < len(strips):
                product(at, strips[turn])
            if turn < len(bands):
                norm(jnp.maximum(at - 1, 0), bands[turn])

    def staggered(product, norm):
        @pl.loop(0, blocks)
        def _(at):
            step(at, product, norm)

        step(blocks, None, norm)

    wait_all(first)
    start_all(up_loads)
    start_all(down_loads)
    start_all(cot_loads)
    staggered(mix, first_norm)
    wait_all(up_loads)
    pl.loop(0, chunks)(widen)
    wait_all(down_loads)
    wait_all(cot_loads)
    staggered(narrow, second_norm)
    enc_stores = start_all(
        [
            copy(enc_buf.at[:, theirs], enc_send, out_sem.at[3]),
            copy(enc_buf.at[:, mine], enc_out.at[own_rows], out_sem.at[4]),
        ]
    )
    pl.loop(0, chunks)(widen_back)
    staggered(narrow_back, first_norm_back)
    last = start_all([copy(dres_buf, dres_out, out_sem.at[2])])
    unmix(sides[1])
    last += start_all([copy(datt_buf.at[:, pl.ds(width, width)], datt_send, out_sem.at[0])])
    unmix(sides[0])
    last += start_all([copy(datt_buf.at[:, pl.ds(0, width)], datt_keep, out_sem.at[1])])
    wait_all(last)
    wait_all(enc_stores)


def rows_step(tp, keep, recv, x_own, x_oth, cot_own, cot_oth, weights, norms):
    half, width = keep.shape
    units = weights[2].shape[1]
    block = min(256, half)
    return pl.pallas_call(
        rows_kernel,
        out_shape=[
            shape_of((2 * half, width), BF16),
            shape_of((half, width), BF16),
            shape_of((half, 2 * width), BF16),
            pltpu.VMEM((half, width), BF16),
            pltpu.VMEM((half, width), BF16),
        ],
        in_specs=[SMEM, VMEM, VMEM, ANY, VMEM, ANY, VMEM, ANY, VMEM] + [ANY] * 4 + [VMEM] * 4,
        out_specs=[ANY] * 3 + [VMEM] * 2,
        scratch_shapes=[
            pltpu.VMEM((half, 2 * width), BF16),
            pltpu.VMEM((half, 2 * width), BF16),
            pltpu.VMEM((half, 2 * width), BF16),
            pltpu.VMEM((2 * width, 2 * width), BF16),
            pltpu.VMEM((2 * width, 2 * units), BF16),
            pltpu.VMEM((2 * units, 2 * width), BF16),
            pltpu.VMEM((half, 2 * width), F32),
            pltpu.VMEM((half, 1), F32),
            pltpu.VMEM((half, 2 * width), BF16),
            pltpu.VMEM((half, 2 * units), BF16),
            pltpu.VMEM((half, 2 * units), BF16),
            pltpu.VMEM((block, 2 * width), F32),
            pltpu.VMEM((block, 2 * width), F32),
            pltpu.VMEM((half, 2 * width), F32),
            pltpu.VMEM((half, 2 * width), BF16),
            pltpu.VMEM((half, 2 * width), BF16),
            pltpu.VMEM((half, 2 * width), BF16),
            pltpu.SemaphoreType.DMA((12,)),
            pltpu.SemaphoreType.DMA((5,)),
        ],
        compiler_params=params(56),
        cost_estimate=pl.CostEstimate(
            flops=2 * half * (4 * width * (2 * width + 4 * units)),
            bytes_accessed=24 * half * width,
            transcendentals=0,
        ),
        name="rows_step",
    )(tp, keep, recv, x_own, x_oth, cot_own, cot_oth, *weights, *norms)


def backward_kernel(
    longest,
    tp_ref,
    lengths_ref,
    qkv_ref,
    dkeep_ref,
    drecv_ref,
    xown_ref,
    xoth_ref,
    mid_ref,
    lse_ref,
    upq_ref,
    upv_ref,
    wcat_ref,
    dres_ref,
    tok_keep_out,
    tok_send_out,
    keep_ref,
    send_ref,
    qkv_buf,
    do_buf,
    x_buf,
    mid_buf,
    d_buf,
    kt_buf,
    q_split,
    do_split,
    p_buf,
    ds_buf,
    grad_ref,
    wcat_buf,
    dres_buf,
    tok_keep_buf,
    tok_send_buf,
    in_sem,
    late_sem,
    out_sem,
):
    half, width = dkeep_ref.shape
    rows = 2 * half
    pairs = width // PAIR
    me = tp_ref[0]
    mine = pl.ds(pl.multiple_of(me * width, 128), width)
    theirs = pl.ds(pl.multiple_of((1 - me) * width, 128), width)
    copy = pltpu.make_async_copy
    block = min(512, half)
    blocks = rows // block

    def block_rows(index):
        return pl.ds(pl.multiple_of(index * block, block), block)

    def d_load(ref, part, index):
        return copy(ref.at[block_rows(part)], do_buf.at[block_rows(index)], in_sem.at[1, index])

    def qkv_load(index):
        at = block_rows(index)
        return copy(qkv_ref.at[at], qkv_buf.at[at], in_sem.at[0, index])

    for index in range(blocks):
        qkv_load(index).start()
        if index < blocks // 2:
            d_load(dkeep_ref, index, me * (blocks // 2) + index).start()
            d_load(drecv_ref, index, (1 - me) * (blocks // 2) + index).start()
    late = start_all(
        [
            copy(xown_ref, x_buf.at[:, mine], late_sem.at[0]),
            copy(xoth_ref, x_buf.at[:, theirs], late_sem.at[1]),
            copy(mid_ref, mid_buf, late_sem.at[2]),
            copy(wcat_ref, wcat_buf, late_sem.at[3]),
            copy(dres_ref, dres_buf, late_sem.at[4]),
        ]
    )
    for buf in (qkv_buf, do_buf):
        buf[rows:, :] = jnp.zeros((buf.shape[0] - rows, buf.shape[1]), BF16)

    def await_chunk(index):
        qkv_load(index).wait()
        d_load(dkeep_ref, 0, index).wait()

    def visit(count, start, first, end, tile):
        window = window_of(count, longest)
        sizes = [tile_rows(count, part, window) for part in range(count)]
        covered = sum(sizes)
        keys_at = pl.ds(start, window)

        def lanes(part):
            return tile_lanes(part, sizes[part])

        def score(pair, part):
            keys = qkv_buf[keys_at, pair_columns(pair, width)]
            if part == 0:
                kt_buf[pair, :, :window] = keys.T
            at = pl.ds(pl.multiple_of(start + part * TILE, ALIGN), sizes[part])
            queries = split_pair(qkv_buf[at, pair_columns(pair)])
            d_rows = split_pair(do_buf[at, pair_columns(pair)])
            q_split[pair, lanes(part), :] = queries
            do_split[pair, lanes(part), :] = d_rows
            return (
                nt(keys, queries),
                nt(qkv_buf[keys_at, pair_columns(pair, 2 * width)], d_rows),
            )

        def weigh(pair, part, scored):
            scores, d_probs = scored
            probs = jnp.exp2(scores - lse_ref[pair, pl.ds(tile + part, 1), :][:, : 2 * sizes[part]])
            probs = key_rows_masked(probs, start, first, end, 0.0)
            product = probs * d_probs
            delta = jnp.sum(product, axis=0, keepdims=True)
            p_buf[pair, :window, lanes(part)] = probs.astype(BF16)
            ds_buf[pair, :window, lanes(part)] = (product - probs * delta).astype(BF16)

        def finish(pair):
            every = slice(0, 2 * covered)
            d_scores = ds_buf[pair, :window, every]
            d_values = nn(p_buf[pair, :window, every], do_split[pair, every, :])
            d_keys = nn(d_scores, q_split[pair, every, :]) * LN2
            columns = nn(kt_buf[pair, :, :window], d_scores) * LN2
            d_queries = jnp.concatenate(
                [merge_pair(columns[:, lanes(part)]) for part in range(count)], axis=0
            )[:window]
            for base, values in enumerate((d_queries, d_keys, d_values)):
                store_window(d_buf, pair_columns(pair, base * width), values, start, first, end)

        run_staged(pairs, count, score, weigh, finish)

    for_each_sentence(lengths_ref, longest, rows, block, await_chunk, visit)
    wait_all(late)

    def token_stores(index):
        at = block_rows(index)
        return [
            copy(tok_send_buf.at[at], tok_send_out.at[at], out_sem.at[0, index]),
            copy(tok_keep_buf.at[at], tok_keep_out.at[at], out_sem.at[1, index]),
        ]

    @pl.loop(0, blocks)
    def _(index):
        at = block_rows(index)
        total = nt(d_buf[at, :], wcat_buf[:, : 3 * width])
        low, high = total[:, :width], total[:, width:]
        tok_keep_buf[at, :] = jnp.where(me == 0, low, high)
        tok_send_buf[at, :] = jnp.where(me == 0, high, low).astype(BF16)

        @pl.when(index // (blocks // 2) == me)
        def _():
            resid = dres_buf[block_rows(lax.rem(index, blocks // 2)), :].astype(F32)
            low, high = resid[:, :width], resid[:, width:]
            tok_keep_buf[at, :] += jnp.where(me == 0, low, high)
            sent = tok_send_buf[at, :].astype(F32) + jnp.where(me == 0, high, low)
            tok_send_buf[at, :] = sent.astype(BF16)

        start_all(token_stores(index))

    d_query = d_buf[:rows, :width]
    d_value = d_buf[:rows, 2 * width :]
    mid = mid_buf[...]
    picked = spread_mask()
    features = 2 * width
    flat = features * RANK // 128
    steps = features // 128
    natural = ADAPTER_SCALE / (math.sqrt(HEAD) * LN2)
    for which, (grads, up_ref, scale) in enumerate(
        ((d_query, upq_ref, natural), (d_value, upv_ref, ADAPTER_SCALE))
    ):
        d_mid = (nt(up_ref[...], grads) * scale).astype(BF16)
        down = nn(d_mid, x_buf[...]).T
        down = jnp.where(picked[None], down.reshape(flat, 128 // RANK, 128), 0.0)
        grad_ref[pl.ds(which * flat, flat), :] = jnp.sum(down, axis=1)
        up = tn(mid, grads)[which * RANK : (which + 1) * RANK] * scale
        base = (2 + which) * flat
        own = me * (width // 128)
        other = (1 - me) * (width // 128)
        for step in range(width // 128):
            part = up[:, step * 128 : (step + 1) * 128]
            grad_ref[pl.ds(base + own + step, RANK, stride=steps), :] = part
            grad_ref[pl.ds(base + other + step, RANK, stride=steps), :] = jnp.zeros_like(part)
    share = keep_ref.shape[0]
    keep_ref[...] = grad_ref[pl.ds(pl.multiple_of(me * share, 8), share), :]
    send_ref[...] = grad_ref[pl.ds(pl.multiple_of((1 - me) * share, 8), share), :]
    for index in range(blocks):
        wait_all(token_stores(index))


def backward(
    tp, lengths, qkv, d_keep, d_recv, x_own, x_oth, mid, lse, up_q, up_v, wcat, dres, longest
):
    half, width = d_keep.shape
    rows = 2 * half
    pairs = width // PAIR
    padded = rows + TILE
    widest = widest_window(longest)
    blocks = rows // min(512, half)
    return pl.pallas_call(
        functools.partial(backward_kernel, longest),
        out_shape=[
            shape_of((rows, width), F32),
            shape_of((rows, width), BF16),
            pltpu.VMEM((4 * width * RANK // 128, 128), F32),
            pltpu.VMEM((4 * width * RANK // 128, 128), F32),
        ],
        in_specs=[SMEM, SMEM, ANY, VMEM, VMEM, ANY, VMEM, ANY] + [VMEM] * 3 + [ANY] * 2,
        out_specs=[ANY, ANY, VMEM, VMEM],
        scratch_shapes=[
            pltpu.VMEM((padded, 3 * width), BF16),
            pltpu.VMEM((padded, width), BF16),
            pltpu.VMEM((rows, 2 * width), BF16),
            pltpu.VMEM((rows, 128), BF16),
            pltpu.VMEM((padded, 3 * width), BF16),
            pltpu.VMEM((pairs, PAIR, widest), BF16),
            pltpu.VMEM((pairs, 2 * widest, PAIR), BF16),
            pltpu.VMEM((pairs, 2 * widest, PAIR), BF16),
            pltpu.VMEM((pairs, widest, 2 * widest), BF16),
            pltpu.VMEM((pairs, widest, 2 * widest), BF16),
            pltpu.VMEM((8 * width * RANK // 128, 128), F32),
            pltpu.VMEM(wcat.shape, BF16),
            pltpu.VMEM((half, 2 * width), BF16),
            pltpu.VMEM((rows, width), F32),
            pltpu.VMEM((rows, width), BF16),
            pltpu.SemaphoreType.DMA((2, blocks)),
            pltpu.SemaphoreType.DMA((5,)),
            pltpu.SemaphoreType.DMA((2, blocks)),
        ],
        compiler_params=params(56),
        cost_estimate=pl.CostEstimate(
            flops=30 * rows * width * width, bytes_accessed=20 * rows * width, transcendentals=0
        ),
        name="backward",
    )(tp, lengths, qkv, d_keep, d_recv, x_own, x_oth, mid, lse, up_q, up_v, wcat, dres)


def adam_update(gradient, moment_one, moment_two, weights, rates):
    first_new = BETA_ONE * moment_one + (1.0 - BETA_ONE) * gradient
    second_new = BETA_TWO * moment_two + (1.0 - BETA_TWO) * gradient * gradient
    update = first_new / BIAS_ONE / (jnp.sqrt(second_new / BIAS_TWO) + EPS_ADAM)
    return first_new, second_new, weights - rates * (update + DECAY_RATE * weights)


def exchange_groups(size):
    step = 1
    while step < size:
        if step * 2 < size:
            yield step, [step, 2 * step, 3 * step]
            step *= 4
        else:
            yield step, [step]
            step *= 2


def partners(values, size, offsets):
    return [
        lax.ppermute(values, "dp", [(i, i ^ offset) for i in range(size)]) for offset in offsets
    ]


def joined(total, moments, others, index):
    rows = total.shape[0]
    sums = [other[:rows] for other in others]
    parts = [moments] + [other[rows:] for other in others]
    if len(sums) == 3:
        total = (total + sums[0]) + (sums[1] + sums[2])
    else:
        total = total + sums[0]
    count = len(parts)
    ordered = [
        functools.reduce(
            lambda held, offset: jnp.where(index == offset, parts[spot ^ offset], held),
            range(1, count),
            parts[spot],
        )
        for spot in range(count)
    ]
    return total, jnp.concatenate(ordered, axis=0)


def in_order(mine, other, me):
    return jnp.where(
        me == 0, jnp.concatenate([mine, other], axis=0), jnp.concatenate([other, mine], axis=0)
    )


def in_vmem(values):
    return pltpu.with_memory_space_constraint(values, pltpu.VMEM)


def tied(*values):
    return lax.optimization_barrier(values)


def swap(values):
    return lax.ppermute(values, "tp", [(0, 1), (1, 0)])


def body(
    tokens,
    lengths,
    query_weight,
    w_key,
    value_weight,
    w_out,
    w_up,
    w_down,
    gain_attn,
    shift_attn,
    gain_ffn,
    shift_ffn,
    factors,
    first_moment,
    second_moment,
    cotangent,
):
    rows, width = tokens.shape
    features = 2 * width
    half = rows // 2
    longest = min(512, rows)
    me = lax.axis_index("tp")
    tp = me.astype(jnp.int32).reshape(1)
    dp_size = lax.axis_size("dp")
    other_rows = (1 - me) * half
    size_down = features * RANK
    own_lengths = lengths.reshape(-1)

    share = first_moment.shape[0]
    share_rows = -(-2 * share // 128)

    x_oth = swap(tokens)
    cot_oth = swap(lax.dynamic_slice_in_dim(cotangent, other_rows, half, 0))
    out_oth = swap(w_out)
    wcat, up_q, up_v = prepare(tp, factors.reshape(-1, 128), query_weight, w_key, value_weight)
    x_oth, cot_oth, out_oth, wcat, w_up_late, w_down_late = tied(
        x_oth, cot_oth, out_oth, wcat, w_up, w_down
    )
    up_oth, down_oth = swap(w_up_late), swap(w_down_late)
    cot_oth, out_oth, x_oth = in_vmem(cot_oth), in_vmem(out_oth), in_vmem(x_oth)

    qkv, mid, att_keep, att_send, lse = forward(
        tp, own_lengths, tokens, x_oth, wcat, longest
    )
    att_recv = in_vmem(swap(att_send))
    att_keep = in_vmem(att_keep)
    moments = jnp.concatenate([first_moment, second_moment])
    moments = jnp.pad(moments, (0, share_rows * 128 - 2 * share)).reshape(share_rows, 128)
    encoded, enc_send, dres, datt_keep, datt_send = rows_step(
        tp,
        att_keep,
        att_recv,
        tokens,
        x_oth,
        cotangent,
        cot_oth,
        (w_out, out_oth, w_up, up_oth, w_down, down_oth),
        (gain_attn, shift_attn, gain_ffn, shift_ffn),
    )
    datt_recv = in_vmem(swap(datt_send))
    datt_keep = in_vmem(datt_keep)
    enc_recv = swap(enc_send)
    tok_keep, tok_send, grad_keep, grad_send = backward(
        tp,
        own_lengths,
        qkv,
        datt_keep,
        datt_recv,
        tokens,
        x_oth,
        mid,
        lse,
        up_q,
        up_v,
        wcat,
        dres,
        longest,
    )
    grad_send, enc_recv = tied(grad_send, enc_recv)
    total = grad_keep + swap(grad_send)
    total, tok_send = tied(total, tok_send)
    tok_recv = swap(tok_send)
    encoded = lax.dynamic_update_slice(encoded, enc_recv, (other_rows, 0))
    d_tokens = tok_keep + tok_recv.astype(F32)
    place = lax.axis_index("dp")
    for turn, (step, offsets) in enumerate(exchange_groups(dp_size)):
        others = partners(jnp.concatenate([total, moments], axis=0), dp_size, offsets)
        if turn == 0:
            others, encoded = tied(others, encoded)
        elif turn == 1:
            others, d_tokens = tied(others, d_tokens)
        total, moments = joined(total, moments, others, (place // step) % (len(offsets) + 1))
    mine = jnp.concatenate([total, moments], axis=0)
    other = swap(mine)
    half_rows = total.shape[0]
    total = in_order(mine[:half_rows], other[:half_rows], me)
    moments = jnp.where(
        me == 0, jnp.stack([mine, other]), jnp.stack([other, mine])
    )[:, half_rows:].reshape(2, dp_size, -1)[:, :, : 2 * share]
    moments = jnp.swapaxes(moments, 0, 1).reshape(2 * dp_size, 2, share)

    gradient = total.reshape(-1) * (1.0 / math.sqrt(rows * dp_size))
    place = jnp.arange(gradient.shape[0], dtype=jnp.int32)
    rates = jnp.where(place < 2 * size_down, RATE_DOWN, RATE_DOWN * RATE_RATIO)
    _, _, factors_new = adam_update(
        gradient, moments[:, 0].reshape(-1), moments[:, 1].reshape(-1), factors, rates
    )
    share_start = lax.axis_index(("dp", "tp")) * share
    grad_share = lax.dynamic_slice_in_dim(gradient, share_start, share)
    first_new, second_new, _ = adam_update(grad_share, first_moment, second_moment, 0.0, 0.0)
    return encoded, d_tokens, grad_share, first_new, second_new, factors_new


def solution(mesh):
    placed = (
        P("dp", "tp"),
        P("dp", None),
        P(None, "tp"),
        P(None, "tp"),
        P(None, "tp"),
        P("tp", None),
        P(None, "tp"),
        P("tp", None),
        P(),
        P(),
        P(),
        P(),
        P(),
        P(("dp", "tp")),
        P(("dp", "tp")),
        P("dp", "tp"),
    )
    return jax.shard_map(
        body,
        mesh=mesh,
        in_specs=placed,
        out_specs=(
            P("dp", "tp"),
            P("dp", "tp"),
            P(("dp", "tp")),
            P(("dp", "tp")),
            P(("dp", "tp")),
            P(),
        ),
        check_vma=False,
    )
```
